256 devices in a mesh: row: 8 (over y, core), col: 32 (over z, x).
Axes of the slice: x: 4, y: 4, z: 8, core: 2. Of those that a mesh axis runs over, the one named last changes fastest.
Arguments:
- sigma_top: float32 [8192, 8192], P('row', 'col')
- panel: float32 [4, 8192, 512], P(None, ('row', 'col')), may hold values from -0.0007324219 to 0.0007324219
- parent_panel: float32 [3, 512, 512], replicated, may hold values from -0.1875 to 0.1875
- diag_inverse: float32 [4, 512, 512], replicated, as said below
- block_depth: int32 [64], replicated, may hold values from 0 to 4, as said below
Outputs:
- sigma_cols: float32 [4, 8192, 512], P(None, ('row', 'col'))
- sigma_link: float32 [3, 512, 512], P(None, 'row')
- sigma_diag: float32 [4, 512, 512], P(None, 'row')
The draws below stay inside these ranges and needn't reach their ends.
Inputs may be any that keep to these rules, and one draw needn't show every extreme that they name: Ancestor rows are nested: supernode k holds block b among its ancestor rows exactly when block_depth[b] > k. Each diag_inverse[k] is lower triangular. sigma_top is symmetric: sigma_top[i, j] = sigma_top[j, i] exactly.
All inputs are finite; a program needn't handle non-finite values.
Results may differ from the reference program's by a relative error of at most 0.0001.
Values sent between devices are 32-bit elements; how exact they have to be, the bound alone decides.
No kernel may reach another device: no remote copies, remote signals or barrier semaphores. Data moves between devices by JAX's collectives and lax.ppermute only.
A program may use at most 128 MiB of HBM per device.

```python
import math
import jax
import jax.numpy as jnp
from jax import lax

ANC = 8192
W = 512
STEPS = 4
BLOCK = 128
NBLK = 64


def draw_sigma_top(key, part):
    key = jax.random.fold_in(key, 11)
    noise_key, level_key = jax.random.split(key)
    noise = jax.random.normal(noise_key, (ANC, ANC), jnp.float32)
    level = jnp.exp(jax.random.uniform(level_key, (ANC,), jnp.float32, math.log(0.5), math.log(2.0)))
    spread_vals = (noise + noise.T) * (0.22 * math.sqrt(ANC) / math.sqrt(2.0))
    return spread_vals + jnp.diag(level * ANC)


def draw_diag_inverse(key, part):
    key = jax.random.fold_in(key, 23)
    noise_key, lead_key = jax.random.split(key)
    below_mask = (jnp.arange(W)[:, None] > jnp.arange(W)[None, :]).astype(jnp.float32)
    noise = jax.random.normal(noise_key, (STEPS, W, W), jnp.float32)
    leading = jnp.exp(jax.random.uniform(lead_key, (STEPS, W), jnp.float32, math.log(0.7), math.log(1.4)))
    return noise * below_mask * (0.4 / math.sqrt(W)) + jnp.eye(W, dtype=jnp.float32) * leading[:, None, :]


def draw_block_depth(key, part):
    key = jax.random.fold_in(key, 37)
    order = jax.random.permutation(key, NBLK)
    return (order % (STEPS + 1)).astype(jnp.int32)


def levels(rng, shape, shards, least, high):
    def one(dim, blocks):
        heights = jax.random.uniform(jax.random.fold_in(jax.random.fold_in(rng, 6), dim), (blocks,), jnp.float32, least / len(shards), high / len(shards))
        return jnp.repeat(jnp.exp(heights), shape[dim] // blocks).reshape((-1,) + (1,) * (len(shape) - dim - 1))

    factor_of = one(*shards[0])
    for cut in shards[1:]:
        factor_of = factor_of * one(*cut)
    return factor_of


def centred(stream_key, dims, scale, bound, cuts=(), kind=jnp.bfloat16):
    result = scale * jax.random.normal(stream_key, dims, jnp.float32)
    if cuts:
        result = result * levels(stream_key, dims, cuts, -0.22, 0.18)
    return jnp.clip(result, -bound, bound).astype(kind)


def setup_inputs(seed: int = 0) -> dict:
    key_of = jax.random.split(jax.random.key(seed), 6)
    sigma_top = draw_sigma_top(jax.random.fold_in(key_of[5], 71), 0)
    panel = centred(key_of[1], (STEPS, ANC, W), (ANC * ANC) ** -0.5, 0.0007324219, ((1, 256),), jnp.float32)
    parent_panel = centred(key_of[2], (STEPS - 1, W, W), (2 * W) ** -0.5, 0.1875, (), jnp.float32)
    diag_inverse = draw_diag_inverse(jax.random.fold_in(key_of[5], 71), 0)
    block_depth = draw_block_depth(jax.random.fold_in(key_of[5], 71), 0)
    return dict(sigma_top=sigma_top, panel=panel, parent_panel=parent_panel, diag_inverse=diag_inverse, block_depth=block_depth)


def reference(sigma_top, panel, parent_panel, diag_inverse, block_depth):
    highest = lax.Precision.HIGHEST
    row_blocks = jnp.arange(ANC, dtype=jnp.int32) // BLOCK
    depth_rows = block_depth[row_blocks]
    column_list = []
    link_list = []
    diagonals = []
    for section in range(STEPS):
        row_mask = jnp.where(depth_rows > section, 1.0, 0.0).astype(jnp.float32)[:, None]
        masked_panel = row_mask * panel[section]
        product = jnp.dot(sigma_top, masked_panel, precision=highest)
        inverse = diag_inverse[section]
        diag_block = jnp.dot(inverse.T, inverse, precision=highest)
        if section > 0:
            parent = parent_panel[section - 1]
            earlier = column_list[-1]
            product = product + jnp.dot(earlier, parent, precision=highest)
            crossed = jnp.dot(earlier.T, masked_panel, precision=highest)
            link_block = -(crossed + jnp.dot(diagonals[-1], parent, precision=highest))
            link_list.append(link_block)
        new_cols = -row_mask * product
        diag_block = diag_block - jnp.dot(masked_panel.T, new_cols, precision=highest)
        if section > 0:
            diag_block = diag_block - jnp.dot(parent.T, link_list[-1], precision=highest)
        column_list.append(new_cols)
        diagonals.append(diag_block)
    return jnp.stack(column_list), jnp.stack(link_list), jnp.stack(diagonals)
```

```python
import jax
import jax.numpy as jnp
from jax import lax
from jax.sharding import Mesh, PartitionSpec as P

BLOCK = 128
ROW = ("y", "core")
COL = ("z", "x")
ALL = ROW + COL


def matmul(a, b, dims=((1,), (0,)), precision=lax.Precision.HIGHEST):
    return lax.dot_general(a, b, (dims, ((), ())), precision=precision, preferred_element_type=jnp.float32)


def row_depth(block_depth, first_row, row_total):
    blocks = (first_row + jnp.arange(row_total, dtype=jnp.int32)) // BLOCK
    block_ids = jnp.arange(block_depth.shape[0], dtype=jnp.int32)
    matched = (blocks[:, None] == block_ids[None, :]).astype(jnp.int32)
    return jnp.sum(matched * block_depth[None, :], axis=1)


def shards(sigma_top, panel, parent_panel, diag_inverse, block_depth):
    rows_n, cols_n = lax.axis_size(ROW), lax.axis_size(COL)
    r, c = lax.axis_index(ROW), lax.axis_index(COL)
    steps, share, width = panel.shape
    group = sigma_top.shape[1]
    part = width // rows_n
    depth = row_depth(block_depth, (r * cols_n + c) * share, share)
    masks = [jnp.where(depth > k, 1.0, 0.0).astype(jnp.float32)[:, None] for k in range(steps)]

    n = []
    for k in range(steps):
        value = masks[k] * panel[k]
        if k:
            value = value - matmul(n[-1], parent_panel[k - 1])
        n.append(value)
    natural = jnp.concatenate(n, axis=1)
    sliced = jnp.stack(n, 1).reshape(share, steps, rows_n, part).transpose(0, 2, 1, 3).reshape(share, steps * width)

    to_group = [(i * cols_n + j, (j % rows_n) * cols_n + i * (cols_n // rows_n) + j // rows_n)
                for i in range(rows_n) for j in range(cols_n)]
    moved = lax.ppermute(natural, ALL, to_group)
    group_n = lax.all_gather(moved, ROW, axis=0, tiled=True)

    gathered = lax.all_gather(sliced, COL, axis=0, tiled=True)
    partial = matmul(gathered, sigma_top, ((0,), (0,)))
    y = lax.psum_scatter(partial, ROW, scatter_dimension=0, tiled=True).reshape(steps, part, group)

    grams = []
    for k in range(steps):
        grams.append(matmul(y[k], group_n[:, k * width:(k + 1) * width]))
    for k in range(1, steps):
        grams.append(matmul(y[k - 1], group_n[:, k * width:(k + 1) * width]))
    count = len(grams)
    z_n, x_n = lax.axis_size("z"), lax.axis_size("x")
    tiles = jnp.stack(grams).reshape(count, z_n, part // z_n, x_n, width // x_n).transpose(1, 3, 0, 2, 4)
    tiles = tiles.reshape((cols_n,) + tiles.shape[2:])
    mine = jnp.sum(lax.all_to_all(tiles, COL, 0, 0, tiled=True), axis=0)
    every = lax.all_to_all(jnp.broadcast_to(mine[None], (cols_n,) + mine.shape), COL, 0, 0, tiled=True)
    every = every.reshape((z_n, x_n) + mine.shape).transpose(2, 0, 3, 1, 4).reshape(count, part, width)

    start = r * part
    diags, links = [], []
    inner = None
    for k in range(steps):
        inverse = diag_inverse[k]
        if k < steps - 1:
            full = matmul(inverse, inverse, ((0,), (0,)))
            if k:
                full = full + matmul(parent_panel[k - 1], inner, ((0,), (0,)))
            own = lax.dynamic_slice_in_dim(full, start, part, 0)
            inner = matmul(full, parent_panel[k])
            links.append(every[steps + k] - lax.dynamic_slice_in_dim(inner, start, part, 0))
        else:
            own = matmul(lax.dynamic_slice_in_dim(inverse, start, part, 1), inverse, ((0,), (0,)))
            if k:
                own = own + matmul(lax.dynamic_slice_in_dim(parent_panel[k - 1], start, part, 1), inner, ((0,), (0,)))
        diags.append(own + every[k])

    blocks = y.reshape(steps, part, rows_n, share).transpose(2, 0, 3, 1)
    blocks = blocks.reshape(rows_n, steps * share * part // width, width)
    blocks = lax.all_to_all(blocks, ROW, 0, 0, tiled=True)
    mine_y = blocks.reshape(rows_n, steps, share, part).transpose(1, 2, 0, 3).reshape(steps, share, width)
    own_y = lax.ppermute(mine_y, ALL, [(b, a) for a, b in to_group])
    cols = jnp.stack([-masks[k] * own_y[k] for k in range(steps)])
    return cols, jnp.stack(links), jnp.stack(diags)


def solution(mesh):
    axes = Mesh(mesh.devices.reshape(4, 2, 8, 4), ("y", "core", "z", "x"))
    return jax.shard_map(
        shards,
        mesh=axes,
        in_specs=(P(ROW, COL), P(None, ALL, None), P(), P(), P()),
        out_specs=(P(None, ALL, None), P(None, ROW, None), P(None, ROW, None)),
        check_vma=False,
    )
```

```python
import jax
import jax.numpy as jnp
from jax import lax
from jax.sharding import Mesh, PartitionSpec as P

BLOCK = 128
ROW = ("y", "core")
COL = ("z", "x")
ALL = ROW + COL


def matmul(a, b, dims=((1,), (0,)), precision=lax.Precision.HIGH):
    return lax.dot_general(a, b, (dims, ((), ())), precision=precision, preferred_element_type=jnp.float32)


def shift(value, axis, distance):
    n = lax.axis_size(axis)
    return lax.ppermute(value, axis, [(i, (i + distance) % n) for i in range(n)])


def ring(value, axis):
    half = value.shape[0] // 2
    out, up, down = [value], value, value
    for _ in range(lax.axis_size(axis) // 2 - 1):
        up, down = shift(up, axis, 1), shift(down, axis, -1)
        out += [up, down]
    out.append(jnp.concatenate([shift(up[:half], axis, 1), shift(down[half:], axis, -1)], axis=0))
    return out


def by_distance(value, axis, dim):
    n = lax.axis_size(axis)
    offsets = [0]
    for s in range(1, n // 2):
        offsets += [n - s, s]
    offsets.append(n // 2)
    me = lax.axis_index(axis)
    return jnp.concatenate([lax.dynamic_slice_in_dim(value, (me + o) % n, 1, dim) for o in offsets], axis=dim)


def core_half(value):
    me = lax.axis_index("core")
    return lax.dynamic_index_in_dim(value, me, 2, False) + shift(lax.dynamic_index_in_dim(value, 1 - me, 2, False), "core", 1)


def y_share(value):
    me = lax.axis_index("y")
    n = lax.axis_size("y")
    half = value.shape[2] // 2
    far, up, down, own = [lax.dynamic_index_in_dim(value, (me + o) % n, 1, False) for o in (2, 1, 3, 0)]
    from_low, from_high = shift(far[:, :half], "y", 1), shift(far[:, half:], "y", -1)
    up = jnp.concatenate([up[:, :half] + from_low, up[:, half:]], axis=1)
    down = jnp.concatenate([down[:, :half], down[:, half:] + from_high], axis=1)
    return own + shift(up, "y", 1) + shift(down, "y", -1)


def row_depth(block_depth, first_row, row_total):
    blocks = (first_row + jnp.arange(row_total, dtype=jnp.int32)) // BLOCK
    block_ids = jnp.arange(block_depth.shape[0], dtype=jnp.int32)
    matched = (blocks[:, None] == block_ids[None, :]).astype(jnp.int32)
    return jnp.sum(matched * block_depth[None, :], axis=1)


def shards(sigma_top, panel, parent_panel, diag_inverse, block_depth):
    rows_n, cols_n = lax.axis_size(ROW), lax.axis_size(COL)
    r, c = lax.axis_index(ROW), lax.axis_index(COL)
    steps, share, width = panel.shape
    group = sigma_top.shape[1]
    part = width // rows_n
    depth = row_depth(block_depth, (r * cols_n + c) * share, share)
    masks = [jnp.where(depth > k, 1.0, 0.0).astype(jnp.float32)[:, None] for k in range(steps)]

    n = []
    for k in range(steps):
        value = masks[k] * panel[k]
        if k:
            value = value - matmul(n[-1], parent_panel[k - 1])
        n.append(value)
    axis_n = {axis: lax.axis_size(axis) for axis in ALL}
    to_group = [(i * cols_n + j, (j % rows_n) * cols_n + i * (cols_n // rows_n) + j // rows_n)
                for i in range(rows_n) for j in range(cols_n)]
    natural = jnp.concatenate(n, axis=1)
    group_n = lax.all_gather(lax.ppermute(natural, ALL, to_group), ROW, axis=0, tiled=True)

    turned = by_distance(by_distance(sigma_top.reshape(axis_n["z"], axis_n["x"], share, group), "x", 1), "z", 0)
    z_major = turned.reshape(axis_n["z"], -1, group)
    x_major = turned.transpose(1, 0, 2, 3).reshape(axis_n["x"], -1, group)
    half = steps // 2
    sums = []
    for order, first in (("zx", 0), ("xz", half)):
        mine = jnp.concatenate(n[first:first + half], axis=1)
        bundle = jnp.concatenate(ring(mine, order[0]), axis=0)
        arrived = ring(bundle, order[1])
        tops = x_major if order == "zx" else z_major
        total = None
        at = 0
        sizes = [1, 1, 1, 1] if order == "zx" else [1, 2, 2, 2, 1]
        for size in sizes:
            block = arrived[at] if size == 1 else jnp.concatenate(arrived[at:at + size], axis=0)
            term = matmul(block, tops[at:at + size].reshape(-1, group), ((0,), (0,)))
            total = term if total is None else total + term
            at += size
        sums.append(core_half(total.reshape(half, axis_n["y"], 2, part, group)))
    y = y_share(jnp.concatenate(sums, axis=0))

    grams = []
    for k in range(steps):
        grams.append(matmul(y[k], group_n[:, k * width:(k + 1) * width]))
    for k in range(1, steps):
        grams.append(matmul(y[k - 1], group_n[:, k * width:(k + 1) * width]))
    count = len(grams)
    z_n, x_n = lax.axis_size("z"), lax.axis_size("x")
    tiles = jnp.stack(grams).reshape(count, z_n, part // z_n, x_n, width // x_n).transpose(1, 3, 0, 2, 4)
    tiles = tiles.reshape((cols_n,) + tiles.shape[2:])
    mine = jnp.sum(lax.all_to_all(tiles, COL, 0, 0, tiled=True), axis=0)
    every = lax.all_to_all(jnp.broadcast_to(mine[None], (cols_n,) + mine.shape), COL, 0, 0, tiled=True)
    every = every.reshape((z_n, x_n) + mine.shape).transpose(2, 0, 3, 1, 4).reshape(count, part, width)

    start = r * part
    diags, links = [], []
    inner = None
    for k in range(steps):
        inverse = diag_inverse[k]
        if k < steps - 1:
            full = matmul(inverse, inverse, ((0,), (0,)))
            if k:
                full = full + matmul(parent_panel[k - 1], inner, ((0,), (0,)))
            own = lax.dynamic_slice_in_dim(full, start, part, 0)
            inner = matmul(full, parent_panel[k])
            links.append(every[steps + k] - lax.dynamic_slice_in_dim(inner, start, part, 0))
        else:
            own = matmul(lax.dynamic_slice_in_dim(inverse, start, part, 1), inverse, ((0,), (0,)))
            if k:
                own = own + matmul(lax.dynamic_slice_in_dim(parent_panel[k - 1], start, part, 1), inner, ((0,), (0,)))
        diags.append(own + every[k])

    blocks = y.reshape(steps, part, rows_n, share).transpose(2, 0, 3, 1)
    blocks = blocks.reshape(rows_n, steps * share * part // width, width)
    blocks = lax.all_to_all(blocks, ROW, 0, 0, tiled=True)
    mine_y = blocks.reshape(rows_n, steps, share, part).transpose(1, 2, 0, 3).reshape(steps, share, width)
    own_y = lax.ppermute(mine_y, ALL, [(b, a) for a, b in to_group])
    cols = jnp.stack([-masks[k] * own_y[k] for k in range(steps)])
    return cols, jnp.stack(links), jnp.stack(diags)


def solution(mesh):
    axes = Mesh(mesh.devices.reshape(4, 2, 8, 4), ("y", "core", "z", "x"))
    return jax.shard_map(
        shards,
        mesh=axes,
        in_specs=(P(ROW, COL), P(None, ALL, None), P(), P(), P()),
        out_specs=(P(None, ALL, None), P(None, ROW, None), P(None, ROW, None)),
        check_vma=False,
    )
```

```python
import jax
import jax.numpy as jnp
from jax import lax
from jax.experimental import pallas as pl
from jax.experimental.pallas import tpu as pltpu
from jax.sharding import Mesh, PartitionSpec as P

BLOCK = 128
ROW = ("y", "core")
COL = ("z", "x")
ALL = ROW + COL
F32 = jnp.float32
HIGHEST = lax.Precision.HIGHEST
VMEM = pl.BlockSpec(memory_space=pltpu.VMEM)
SMEM = pl.BlockSpec(memory_space=pltpu.SMEM)
ANY = pl.BlockSpec(memory_space=pl.ANY)
VMEM_BYTES = 40 * 2**20


def matmul(a, b, dims=((1,), (0,)), precision=HIGHEST):
    return lax.dot_general(a, b, (dims, ((), ())), precision=precision, preferred_element_type=F32)


def local(kernel, out_shapes, specs, *args, after=()):
    many = isinstance(out_shapes, list)
    shapes = [jax.ShapeDtypeStruct(s, F32) for s in (out_shapes if many else [out_shapes])]
    out = pl.pallas_call(
        lambda *refs: kernel(*refs[:len(args)], *refs[len(args) + len(after):]),
        out_shape=shapes,
        in_specs=list(specs) + [ANY] * len(after),
        out_specs=[VMEM] * len(shapes),
        compiler_params=pltpu.CompilerParams(vmem_limit_bytes=VMEM_BYTES),
    )(*args, *after)
    return out if many else out[0]


def copy_kernel(src, dst):
    dst[...] = src[...]


def shift(value, axis, distance):
    n = lax.axis_size(axis)
    return lax.ppermute(value, axis, [(i, (i + distance) % n) for i in range(n)])


def ring(value, axis):
    half = value.shape[0] // 2
    out, up, down = [value], value, value
    for _ in range(lax.axis_size(axis) // 2 - 1):
        up, down = shift(up, axis, 1), shift(down, axis, -1)
        out += [up, down]
    return out + [shift(up[:half], axis, 1), shift(down[half:], axis, -1)]


def ring_sources(axis):
    n, me = lax.axis_size(axis), lax.axis_index(axis)
    offsets = [0]
    for s in range(1, n // 2):
        offsets += [n - s, s]
    return [(me + o) % n for o in offsets + [n // 2]]


def pick(value, index, dim):
    return lax.dynamic_index_in_dim(value, index, dim, False)


def shards(sigma_top, panel, parent_panel, diag_inverse, block_depth):
    rows_n, cols_n = lax.axis_size(ROW), lax.axis_size(COL)
    y_n, z_n, x_n = (lax.axis_size(axis) for axis in ("y", "z", "x"))
    r, c = lax.axis_index(ROW), lax.axis_index(COL)
    y_i, core = lax.axis_index("y"), lax.axis_index("core")
    steps, share, width = panel.shape
    group = sigma_top.shape[1]
    part = width // rows_n
    half = steps // 2
    links_n = steps - 1
    depth = lax.dynamic_slice_in_dim(block_depth, (r * cols_n + c) * share // BLOCK, 1)

    def masked(depth_ref, panel_ref, k):
        return jnp.where(depth_ref[0] > k, 1.0, 0.0).astype(F32) * panel_ref[k]

    def head_first(depth_ref, panel_ref, parent_ref, out):
        value = masked(depth_ref, panel_ref, 0)
        out[:, :width] = value
        for k in range(1, half):
            value = masked(depth_ref, panel_ref, k) - matmul(value, parent_ref[k - 1])
            out[:, k * width:(k + 1) * width] = value

    def head_second(depth_ref, panel_ref, parent_ref, first_ref, out):
        value = first_ref[:, (half - 1) * width:]
        for k in range(half, steps):
            value = masked(depth_ref, panel_ref, k) - matmul(value, parent_ref[k - 1])
            out[:, (k - half) * width:(k - half + 1) * width] = value

    n_z = local(head_first, (share, half * width), [SMEM, VMEM, VMEM], depth, panel, parent_panel)
    n_x = local(head_second, (share, half * width), [SMEM, VMEM, VMEM, VMEM], depth, panel, parent_panel, n_z)

    by_z = ring(n_z, "z")
    by_x = ring(n_x, "x")

    to_group = [(i * cols_n + j, (j % rows_n) * cols_n + i * (cols_n // rows_n) + j // rows_n)
                for i in range(rows_n) for j in range(cols_n)]

    def join(a, b, out):
        out[:, :half * width] = a[...]
        out[:, half * width:] = b[...]

    natural = local(join, (share, steps * width), [VMEM, VMEM], n_z, n_x, after=(by_z[1],))
    group_n = lax.all_gather(lax.ppermute(natural, ALL, to_group), ROW, axis=0, tiled=True)

    starts = jnp.stack([(zz * x_n + xx) * share for zz in ring_sources("z") for xx in ring_sources("x")])

    def turn(starts_ref, top, z_major, x_major):
        for i in range(z_n):
            for j in range(x_n):
                rows = top[pl.ds(pl.multiple_of(starts_ref[i * x_n + j], share), share), :]
                z_major[i, j * share:(j + 1) * share, :] = rows
                x_major[j, i * share:(i + 1) * share, :] = rows

    z_major, x_major = local(turn, [(z_n, x_n * share, group), (x_n, z_n * share, group)], [SMEM, VMEM],
                             starts.astype(jnp.int32), sigma_top, after=(by_z[1],))

    def product(total, blocks, tops):
        block = blocks[0] if len(blocks) == 1 else jnp.concatenate(blocks, axis=0)
        term = matmul(block, tops.reshape(-1, group), ((0,), (0,)), lax.Precision.HIGH)
        return term if total is None else total + term

    by_x[-1] = local(copy_kernel, by_x[-1].shape, [VMEM], by_x[-1], after=(by_z[-1],))
    z_sum = x_sum = None
    arrived = ring(jnp.concatenate(by_z, axis=0), "x")
    for j in range(x_n):
        z_sum = product(z_sum, arrived[j:] if j == x_n - 1 else arrived[j:j + 1], x_major[j:j + 1])
    arrived = ring(jnp.concatenate(by_x, axis=0), "z")
    x_sum = product(x_sum, arrived[:1], z_major[:1])
    for j in range(1, z_n - 1, 2):
        x_sum = product(x_sum, arrived[j:j + 2], z_major[j:j + 2])
    x_sum = product(x_sum, arrived[z_n - 1:], z_major[z_n - 1:])

    pieces = []
    for total in (z_sum, x_sum):
        total = total.reshape(half, y_n, 2, part, group)
        pieces.append(pick(total, core, 2) + shift(pick(total, 1 - core, 2), "core", 1))
    pieces = jnp.concatenate(pieces, axis=0)
    summands = [pick(pieces, y_i, 1)]
    for d in range(1, y_n):
        summands.append(shift(pick(pieces, (y_i + d) % y_n, 1), "y", d))

    count = steps + links_n
    t_rows, t_cols = part // z_n, width // x_n

    def gram(*refs):
        parts, n_ref, tiles, y_ref = refs[:y_n], refs[y_n], refs[y_n + 1], refs[y_n + 2]
        y_ref[...] = sum((p[...] for p in parts[1:]), parts[0][...]).reshape(steps * part, group)

        def put(which, value):
            for i in range(z_n):
                for j in range(x_n):
                    tiles[i * x_n + j, which] = value[i * t_rows:(i + 1) * t_rows, j * t_cols:(j + 1) * t_cols]

        for k in range(steps):
            first = max(k - 1, 0)
            value = matmul(y_ref[first * part:(k + 1) * part, :], n_ref[:, k * width:(k + 1) * width])
            put(k, value[(k - first) * part:])
            if k:
                put(steps + k - 1, value[:part])

    tiles, y_rows = local(gram, [(cols_n, count, t_rows, t_cols), (steps * part, group)], [VMEM] * (y_n + 1),
                          *summands, group_n)
    summed = lax.all_to_all(tiles, COL, 0, 0, tiled=True)

    def total_kernel(src, dst):
        total = src[0]
        for i in range(1, cols_n):
            total = total + src[i]
        for i in range(cols_n):
            dst[i] = total

    every = lax.all_to_all(local(total_kernel, tiles.shape, [VMEM], summed), COL, 0, 0, tiled=True)

    def turn_back(src, dst):
        dst[...] = src[...].T.reshape(rows_n, share, steps * part)

    home = local(turn_back, (rows_n, share, steps * part), [VMEM], y_rows)
    home = home.reshape(y_n, 2, share, steps * part)
    home = jnp.stack([pick(home, core, 1), shift(pick(home, 1 - core, 1), "core", 1)], axis=1)
    home = jnp.stack([pick(home, y_i, 0)] + [shift(pick(home, (y_i + d) % y_n, 0), "y", d) for d in range(1, y_n)])
    home = lax.ppermute(home, ALL, [(b, a) for a, b in to_group])
    sender = c % rows_n
    places = jnp.stack([((sender // 2 - i // 2) % y_n) * 2 + (sender % 2 + i % 2) % 2 for i in range(rows_n)])

    def finish_cols(places_ref, depth_ref, src, dst):
        for i in range(rows_n):
            value = src[places_ref[i]]
            for k in range(steps):
                sign = jnp.where(depth_ref[0] > k, -1.0, 0.0).astype(F32)
                dst[k, :, i * part:(i + 1) * part] = sign * value[:, k * part:(k + 1) * part]

    cols = local(finish_cols, (steps, share, width), [SMEM, SMEM, VMEM], places.astype(jnp.int32), depth,
                 home.reshape(rows_n, share, steps * part))

    def own_rows(first_ref, inverse_ref, parent_ref, diag_ref, link_ref):
        at = lax.broadcasted_iota(jnp.int32, (part, width), 0) + first_ref[0]
        unit = (lax.broadcasted_iota(jnp.int32, (part, width), 1) == at).astype(F32)
        rows, left = unit, [None] * steps
        for k in reversed(range(steps)):
            left[k] = matmul(rows, inverse_ref[k], ((1,), (1,)))
            if k:
                rows = jnp.concatenate([matmul(rows, parent_ref[k - 1], ((1,), (1,))), unit], axis=0)
        carried = None
        for k in range(steps):
            value = matmul(left[k], inverse_ref[k])
            if k:
                value = value + carried[:-part]
            diag_ref[k] = value[-part:]
            if k < links_n:
                carried = matmul(value, parent_ref[k])
                link_ref[k] = carried[-part:]

    diag_own, link_own = local(own_rows, [(steps, part, width), (links_n, part, width)], [SMEM, VMEM, VMEM],
                               (r * part).reshape(1).astype(jnp.int32), diag_inverse, parent_panel, after=(tiles,))

    def finish(src, diag_ref, link_ref, links, diags):
        for i in range(z_n):
            for j in range(x_n):
                place = (slice(i * t_rows, (i + 1) * t_rows), slice(j * t_cols, (j + 1) * t_cols))
                for k in range(steps):
                    diags[(k,) + place] = diag_ref[(k,) + place] + src[i * x_n + j, k]
                for k in range(links_n):
                    links[(k,) + place] = src[i * x_n + j, steps + k] - link_ref[(k,) + place]

    links, diags = local(finish, [(links_n, part, width), (steps, part, width)], [VMEM] * 3,
                         every, diag_own, link_own)
    return cols, links, diags


def solution(mesh):
    axes = Mesh(mesh.devices.reshape(4, 2, 8, 4), ("y", "core", "z", "x"))
    return jax.shard_map(
        shards,
        mesh=axes,
        in_specs=(P(ROW, COL), P(None, ALL, None), P(), P(), P()),
        out_specs=(P(None, ALL, None), P(None, ROW, None), P(None, ROW, None)),
        check_vma=False,
    )
```

```python
import jax
import jax.numpy as jnp
from jax import lax
from jax.experimental import pallas as pl
from jax.experimental.pallas import tpu as pltpu
from jax.sharding import Mesh, PartitionSpec as P

BLOCK = 128
ROW = ("y", "core")
COL = ("z", "x")
ALL = ROW + COL
F32 = jnp.float32
HIGHEST = lax.Precision.HIGHEST
VMEM = pl.BlockSpec(memory_space=pltpu.VMEM)
SMEM = pl.BlockSpec(memory_space=pltpu.SMEM)
ANY = pl.BlockSpec(memory_space=pl.ANY)
VMEM_BYTES = 40 * 2**20


def matmul(a, b, dims=((1,), (0,)), precision=HIGHEST):
    return lax.dot_general(a, b, (dims, ((), ())), precision=precision, preferred_element_type=F32)


def local(kernel, out_shapes, specs, *args, after=()):
    many = isinstance(out_shapes, list)
    shapes = [jax.ShapeDtypeStruct(s, F32) for s in (out_shapes if many else [out_shapes])]
    out = pl.pallas_call(
        lambda *refs: kernel(*refs[:len(args)], *refs[len(args) + len(after):]),
        out_shape=shapes,
        in_specs=list(specs) + [ANY] * len(after),
        out_specs=[VMEM] * len(shapes),
        compiler_params=pltpu.CompilerParams(vmem_limit_bytes=VMEM_BYTES),
    )(*args, *after)
    return out if many else out[0]


def pack(pieces, after=()):
    def kernel(*refs):
        at = 0
        for ref in refs[:-1]:
            refs[-1][at:at + ref.shape[0]] = ref[...]
            at += ref.shape[0]

    rows = sum(piece.shape[0] for piece in pieces)
    return local(kernel, (rows,) + pieces[0].shape[1:], [VMEM] * len(pieces), *pieces, after=after)


def shift(value, axis, distance):
    n = lax.axis_size(axis)
    return lax.ppermute(value, axis, [(i, (i + distance) % n) for i in range(n)])


def ring(value, axis):
    half = value.shape[0] // 2
    out, up, down = [value], value, value
    for _ in range(lax.axis_size(axis) // 2 - 1):
        up, down = shift(up, axis, 1), shift(down, axis, -1)
        out += [up, down]
    return out + [shift(up[:half], axis, 1), shift(down[half:], axis, -1)]


def ring_sources(axis):
    n, me = lax.axis_size(axis), lax.axis_index(axis)
    offsets = [0]
    for s in range(1, n // 2):
        offsets += [n - s, s]
    return [(me + o) % n for o in offsets + [n // 2]]


def pick(value, index, dim):
    return lax.dynamic_index_in_dim(value, index, dim, False)


def shards(sigma_top, panel, parent_panel, diag_inverse, block_depth):
    rows_n, cols_n = lax.axis_size(ROW), lax.axis_size(COL)
    y_n, z_n, x_n = (lax.axis_size(axis) for axis in ("y", "z", "x"))
    r, c = lax.axis_index(ROW), lax.axis_index(COL)
    y_i, core = lax.axis_index("y"), lax.axis_index("core")
    steps, share, width = panel.shape
    group = sigma_top.shape[1]
    part = width // rows_n
    half = steps // 2
    links_n = steps - 1
    depth = lax.dynamic_slice_in_dim(block_depth, (r * cols_n + c) * share // BLOCK, 1)

    def masked(depth_ref, panel_ref, k):
        return jnp.where(depth_ref[0] > k, 1.0, 0.0).astype(F32) * panel_ref[k]

    def head_first(depth_ref, panel_ref, parent_ref, out):
        value = masked(depth_ref, panel_ref, 0)
        out[:, :width] = value
        for k in range(1, half):
            value = masked(depth_ref, panel_ref, k) - matmul(value, parent_ref[k - 1])
            out[:, k * width:(k + 1) * width] = value

    def head_second(depth_ref, panel_ref, parent_ref, first_ref, out):
        value = first_ref[:, (half - 1) * width:]
        for k in range(half, steps):
            value = masked(depth_ref, panel_ref, k) - matmul(value, parent_ref[k - 1])
            out[:, (k - half) * width:(k - half + 1) * width] = value

    n_z = local(head_first, (share, half * width), [SMEM, VMEM, VMEM], depth, panel, parent_panel)
    n_x = local(head_second, (share, half * width), [SMEM, VMEM, VMEM, VMEM], depth, panel, parent_panel, n_z)

    by_z = ring(n_z, "z")
    by_x = ring(n_x, "x")

    to_group = [(i * cols_n + j, (j % rows_n) * cols_n + i * (cols_n // rows_n) + j // rows_n)
                for i in range(rows_n) for j in range(cols_n)]

    def join(a, b, out):
        out[:, :half * width] = a[...]
        out[:, half * width:] = b[...]

    natural = local(join, (share, steps * width), [VMEM, VMEM], n_z, n_x)
    group_n = lax.all_gather(lax.ppermute(natural, ALL, to_group), ROW, axis=0, tiled=True)

    starts = jnp.stack([(zz * x_n + xx) * share for zz in ring_sources("z") for xx in ring_sources("x")])

    def turn(starts_ref, top, z_major, x_major):
        for i in range(z_n):
            for j in range(x_n):
                rows = top[pl.ds(pl.multiple_of(starts_ref[i * x_n + j], share), share), :]
                z_major[i, j * share:(j + 1) * share, :] = rows
                x_major[j, i * share:(i + 1) * share, :] = rows

    z_major, x_major = local(turn, [(z_n, x_n * share, group), (x_n, z_n * share, group)], [SMEM, VMEM],
                             starts.astype(jnp.int32), sigma_top, after=(by_z[1],))

    def product(total, blocks, tops):
        block = blocks[0] if len(blocks) == 1 else jnp.concatenate(blocks, axis=0)
        term = matmul(block, tops.reshape(-1, group), ((0,), (0,)), lax.Precision.HIGH)
        return term if total is None else total + term

    z_sum = x_sum = None
    arrived = ring(pack(by_z), "x")
    for j in range(x_n):
        z_sum = product(z_sum, arrived[j:] if j == x_n - 1 else arrived[j:j + 1], x_major[j:j + 1])
    arrived = ring(pack(by_x, after=(by_z[-1],)), "z")
    x_sum = product(x_sum, arrived[:1], z_major[:1])
    for j in range(1, z_n - 1, 2):
        x_sum = product(x_sum, arrived[j:j + 2], z_major[j:j + 2])
    x_sum = product(x_sum, arrived[z_n - 1:], z_major[z_n - 1:])

    pieces = []
    for total in (z_sum, x_sum):
        total = total.reshape(half, y_n, 2, part, group)
        pieces.append(pick(total, core, 2) + shift(pick(total, 1 - core, 2), "core", 1))
    pieces = jnp.concatenate(pieces, axis=0)
    summands = [pick(pieces, y_i, 1)]
    for d in range(1, y_n):
        summands.append(shift(pick(pieces, (y_i + d) % y_n, 1), "y", d))

    count = steps + links_n
    t_rows, t_cols = part // z_n, width // x_n

    def gram(*refs):
        parts, n_ref, tiles, y_ref = refs[:y_n], refs[y_n], refs[y_n + 1], refs[y_n + 2]
        y_ref[...] = sum((p[...] for p in parts[1:]), parts[0][...]).reshape(steps * part, group)

        def put(which, value):
            for i in range(z_n):
                for j in range(x_n):
                    tiles[i * x_n + j, which] = value[i * t_rows:(i + 1) * t_rows, j * t_cols:(j + 1) * t_cols]

        for k in range(steps):
            first = max(k - 1, 0)
            value = matmul(y_ref[first * part:(k + 1) * part, :], n_ref[:, k * width:(k + 1) * width])
            put(k, value[(k - first) * part:])
            if k:
                put(steps + k - 1, value[:part])

    tiles, y_rows = local(gram, [(cols_n, count, t_rows, t_cols), (steps * part, group)], [VMEM] * (y_n + 1),
                          *summands, group_n)
    summed = lax.all_to_all(tiles, COL, 0, 0, tiled=True)

    def turn_back(src, dst):
        dst[...] = src[...].T.reshape(rows_n, share, steps * part)

    home = local(turn_back, (rows_n, share, steps * part), [VMEM], y_rows)
    home = home.reshape(y_n, 2, share, steps * part)
    home = jnp.stack([pick(home, core, 1), shift(pick(home, 1 - core, 1), "core", 1)], axis=1)
    home = jnp.stack([pick(home, y_i, 0)] + [shift(pick(home, (y_i + d) % y_n, 0), "y", d) for d in range(1, y_n)])
    def own_rows(first_ref, inverse_ref, parent_ref, diag_ref, link_ref):
        at = lax.broadcasted_iota(jnp.int32, (part, width), 0) + first_ref[0]
        unit = (lax.broadcasted_iota(jnp.int32, (part, width), 1) == at).astype(F32)
        rows, left = unit, [None] * steps
        for k in reversed(range(steps)):
            left[k] = matmul(rows, inverse_ref[k], ((1,), (1,)))
            if k:
                rows = jnp.concatenate([matmul(rows, parent_ref[k - 1], ((1,), (1,))), unit], axis=0)
        carried = None
        for k in range(steps):
            value = matmul(left[k], inverse_ref[k])
            if k:
                value = value + carried[:-part]
            diag_ref[k] = value[-part:]
            if k < links_n:
                carried = matmul(value, parent_ref[k])
                link_ref[k] = carried[-part:]

    diag_own, link_own = local(own_rows, [(steps, part, width), (links_n, part, width)], [SMEM, VMEM, VMEM],
                               (r * part).reshape(1).astype(jnp.int32), diag_inverse, parent_panel, after=(tiles,))

    def total_kernel(src, dst):
        total = src[0]
        for i in range(1, cols_n):
            total = total + src[i]
        for i in range(cols_n):
            dst[i] = total

    every = lax.all_to_all(local(total_kernel, tiles.shape, [VMEM], summed, after=(home, diag_own)), COL, 0, 0, tiled=True)

    home = lax.ppermute(home, ALL, [(b, a) for a, b in to_group])
    sender = c % rows_n
    places = jnp.stack([((sender // 2 - i // 2) % y_n) * 2 + (sender % 2 + i % 2) % 2 for i in range(rows_n)])

    def finish_cols(places_ref, depth_ref, src, dst):
        for i in range(rows_n):
            value = src[places_ref[i]]
            for k in range(steps):
                sign = jnp.where(depth_ref[0] > k, -1.0, 0.0).astype(F32)
                dst[k, :, i * part:(i + 1) * part] = sign * value[:, k * part:(k + 1) * part]

    cols = local(finish_cols, (steps, share, width), [SMEM, SMEM, VMEM], places.astype(jnp.int32), depth,
                 home.reshape(rows_n, share, steps * part))

    def finish(src, diag_ref, link_ref, links, diags):
        for i in range(z_n):
            for j in range(x_n):
                place = (slice(i * t_rows, (i + 1) * t_rows), slice(j * t_cols, (j + 1) * t_cols))
                for k in range(steps):
                    diags[(k,) + place] = diag_ref[(k,) + place] + src[i * x_n + j, k]
                for k in range(links_n):
                    links[(k,) + place] = src[i * x_n + j, steps + k] - link_ref[(k,) + place]

    links, diags = local(finish, [(links_n, part, width), (steps, part, width)], [VMEM] * 3,
                         every, diag_own, link_own)
    return cols, links, diags


def solution(mesh):
    axes = Mesh(mesh.devices.reshape(4, 2, 8, 4), ("y", "core", "z", "x"))
    return jax.shard_map(
        shards,
        mesh=axes,
        in_specs=(P(ROW, COL), P(None, ALL, None), P(), P(), P()),
        out_specs=(P(None, ALL, None), P(None, ROW, None), P(None, ROW, None)),
        check_vma=False,
    )
```

```python
import jax
import jax.numpy as jnp
from jax import lax
from jax.experimental import pallas as pl
from jax.experimental.pallas import tpu as pltpu
from jax.sharding import Mesh, PartitionSpec as P

BLOCK = 128
ROW = ("y", "core")
COL = ("z", "x")
ALL = ROW + COL
F32 = jnp.float32
HIGHEST = lax.Precision.HIGHEST
VMEM = pl.BlockSpec(memory_space=pltpu.VMEM)
SMEM = pl.BlockSpec(memory_space=pltpu.SMEM)
ANY = pl.BlockSpec(memory_space=pl.ANY)
VMEM_BYTES = 16 * 2**20


def matmul(a, b, dims=((1,), (0,)), precision=HIGHEST):
    return lax.dot_general(a, b, (dims, ((), ())), precision=precision, preferred_element_type=F32)


def local(kernel, out_shapes, specs, *args, after=(), scratch=()):
    many = isinstance(out_shapes, list)
    shapes = [jax.ShapeDtypeStruct(s, F32) for s in (out_shapes if many else [out_shapes])]
    out = pl.pallas_call(
        lambda *refs: kernel(*refs[:len(args)], *refs[len(args) + len(after):]),
        out_shape=shapes,
        in_specs=list(specs) + [ANY] * len(after),
        out_specs=[VMEM] * len(shapes),
        scratch_shapes=[pltpu.VMEM(shape, F32) for shape in scratch],
        compiler_params=pltpu.CompilerParams(vmem_limit_bytes=VMEM_BYTES),
    )(*args, *after)
    return out if many else out[0]


def pack(pieces, after=()):
    def kernel(*refs):
        at = 0
        for ref in refs[:-1]:
            refs[-1][at:at + ref.shape[0]] = ref[...]
            at += ref.shape[0]

    rows = sum(piece.shape[0] for piece in pieces)
    return local(kernel, (rows,) + pieces[0].shape[1:], [VMEM] * len(pieces), *pieces, after=after)


def shift(value, axis, distance):
    n = lax.axis_size(axis)
    return lax.ppermute(value, axis, [(i, (i + distance) % n) for i in range(n)])


def ring(value, axis):
    half = value.shape[0] // 2
    out, up, down = [value], value, value
    for _ in range(lax.axis_size(axis) // 2 - 1):
        up, down = shift(up, axis, 1), shift(down, axis, -1)
        out += [up, down]
    return out + [shift(up[:half], axis, 1), shift(down[half:], axis, -1)]


def ring_sources(axis):
    n, me = lax.axis_size(axis), lax.axis_index(axis)
    offsets = [0]
    for s in range(1, n // 2):
        offsets += [n - s, s]
    return [(me + o) % n for o in offsets + [n // 2]]


def pick(value, index, dim):
    return lax.dynamic_index_in_dim(value, index, dim, False)


def shards(sigma_top, panel, parent_panel, diag_inverse, block_depth):
    rows_n, cols_n = lax.axis_size(ROW), lax.axis_size(COL)
    y_n, z_n, x_n = (lax.axis_size(axis) for axis in ("y", "z", "x"))
    r, c = lax.axis_index(ROW), lax.axis_index(COL)
    y_i, core = lax.axis_index("y"), lax.axis_index("core")
    steps, share, width = panel.shape
    group = sigma_top.shape[1]
    part = width // rows_n
    half = steps // 2
    links_n = steps - 1
    depth = lax.dynamic_slice_in_dim(block_depth, (r * cols_n + c) * share // BLOCK, 1)

    to_group = [(i * cols_n + j, (j % rows_n) * cols_n + i * (cols_n // rows_n) + j // rows_n)
                for i in range(rows_n) for j in range(cols_n)]
    moved = lax.ppermute(panel, ALL, to_group)
    group_panel = lax.all_gather(moved, ROW, axis=0)
    group_depth = lax.dynamic_slice_in_dim(block_depth, c * group // BLOCK, group // BLOCK)

    def masked(depth_ref, panel_ref, k):
        return jnp.where(depth_ref[0] > k, 1.0, 0.0).astype(F32) * panel_ref[k]

    def head_first(depth_ref, panel_ref, parent_ref, out):
        value = masked(depth_ref, panel_ref, 0)
        out[:, :width] = value
        for k in range(1, half):
            value = masked(depth_ref, panel_ref, k) - matmul(value, parent_ref[k - 1])
            out[:, k * width:(k + 1) * width] = value

    def head_second(depth_ref, panel_ref, parent_ref, first_ref, out):
        value = first_ref[:, (half - 1) * width:]
        for k in range(half, steps):
            value = masked(depth_ref, panel_ref, k) - matmul(value, parent_ref[k - 1])
            out[:, (k - half) * width:(k - half + 1) * width] = value

    n_z = local(head_first, (share, half * width), [SMEM, VMEM, VMEM], depth, panel, parent_panel)
    n_x = local(head_second, (share, half * width), [SMEM, VMEM, VMEM, VMEM], depth, panel, parent_panel, n_z, after=(moved,))

    by_z = ring(n_z, "z")
    by_x = ring(n_x, "x")

    starts = jnp.stack([(zz * x_n + xx) * share for zz in ring_sources("z") for xx in ring_sources("x")])

    def turn(starts_ref, top, z_major, x_major):
        for i in range(z_n):
            for j in range(x_n):
                rows = top[pl.ds(pl.multiple_of(starts_ref[i * x_n + j], share), share), :]
                z_major[i, j * share:(j + 1) * share, :] = rows
                x_major[j, i * share:(i + 1) * share, :] = rows

    z_major, x_major = local(turn, [(z_n, x_n * share, group), (x_n, z_n * share, group)], [SMEM, VMEM],
                             starts.astype(jnp.int32), sigma_top, after=(by_z[1],))

    def product(total, blocks, tops):
        block = blocks[0] if len(blocks) == 1 else jnp.concatenate(blocks, axis=0)
        term = matmul(block, tops.reshape(-1, group), ((0,), (0,)), lax.Precision.HIGH)
        return term if total is None else total + term

    z_sum = x_sum = None
    arrived = ring(pack(by_z), "x")
    for j in range(x_n):
        z_sum = product(z_sum, arrived[j:] if j == x_n - 1 else arrived[j:j + 1], x_major[j:j + 1])
    arrived = ring(pack(by_x, after=(by_z[-1],)), "z")
    x_sum = product(x_sum, arrived[:1], z_major[:1])
    for j in range(1, z_n - 1, 2):
        x_sum = product(x_sum, arrived[j:j + 2], z_major[j:j + 2])
    x_sum = product(x_sum, arrived[z_n - 1:], z_major[z_n - 1:])

    def group_head(depth_ref, panel_ref, parent_ref, out):
        for k in range(steps):
            at = slice(k * width, (k + 1) * width)
            for i in range(rows_n):
                mask = jnp.where(depth_ref[i * share // BLOCK] > k, 1.0, 0.0).astype(F32)
                out[i * share:(i + 1) * share, at] = mask * panel_ref[i, k]
            if k:
                out[:, at] -= matmul(out[:, (k - 1) * width:k * width], parent_ref[k - 1])

    group_n = local(group_head, (group, steps * width), [SMEM, VMEM, VMEM], group_depth, group_panel, parent_panel)

    pieces = []
    for total in (z_sum, x_sum):
        total = total.reshape(half, y_n, 2, part, group)
        pieces.append(pick(total, core, 2) + shift(pick(total, 1 - core, 2), "core", 1))
    pieces = jnp.concatenate(pieces, axis=0)
    summands = [pick(pieces, y_i, 1)]
    for d in range(1, y_n):
        summands.append(shift(pick(pieces, (y_i + d) % y_n, 1), "y", d))

    def own_rows(first_ref, inverse_ref, parent_ref, diag_ref, link_ref):
        at = lax.broadcasted_iota(jnp.int32, (part, width), 0) + first_ref[0]
        unit = (lax.broadcasted_iota(jnp.int32, (part, width), 1) == at).astype(F32)
        rows, left = unit, [None] * steps
        for k in reversed(range(steps)):
            left[k] = matmul(rows, inverse_ref[k], ((1,), (1,)))
            if k:
                rows = jnp.concatenate([matmul(rows, parent_ref[k - 1], ((1,), (1,))), unit], axis=0)
        carried = None
        for k in range(steps):
            value = matmul(left[k], inverse_ref[k])
            if k:
                value = value + carried[:-part]
            diag_ref[k] = value[-part:]
            if k < links_n:
                carried = matmul(value, parent_ref[k])
                link_ref[k] = carried[-part:]

    diag_own, link_own = local(own_rows, [(steps, part, width), (links_n, part, width)], [SMEM, VMEM, VMEM],
                               (r * part).reshape(1).astype(jnp.int32), diag_inverse, parent_panel, after=(pieces,))

    count = steps + links_n
    t_rows, t_cols = part // z_n, width // x_n

    def gram(*refs):
        parts, n_ref, tiles, y_ref = refs[:y_n], refs[y_n], refs[y_n + 1], refs[y_n + 2]
        y_ref[...] = sum((p[...] for p in parts[1:]), parts[0][...]).reshape(steps * part, group)

        def put(which, value):
            for i in range(z_n):
                for j in range(x_n):
                    tiles[i * x_n + j, which] = value[i * t_rows:(i + 1) * t_rows, j * t_cols:(j + 1) * t_cols]

        for k in range(steps):
            first = max(k - 1, 0)
            value = matmul(y_ref[first * part:(k + 1) * part, :], n_ref[:, k * width:(k + 1) * width])
            put(k, value[(k - first) * part:])
            if k:
                put(steps + k - 1, value[:part])

    tiles, y_rows = local(gram, [(cols_n, count, t_rows, t_cols), (steps * part, group)], [VMEM] * (y_n + 1),
                          *summands, group_n, after=(diag_own,))
    summed = lax.all_to_all(tiles, COL, 0, 0, tiled=True)

    def turn_back(order_ref, src, *refs):
        refs[-1][...] = src[...].T
        for d in range(rows_n):
            refs[d][...] = refs[-1][pl.ds(pl.multiple_of(order_ref[d] * share, share), share), :]

    per = cols_n // rows_n
    order = (r + jnp.arange(rows_n, dtype=jnp.int32)) % rows_n
    home = list(local(turn_back, [(share, steps * part)] * rows_n, [SMEM, VMEM], order, y_rows,
                      scratch=[(group, steps * part)]))
    for d in range(rows_n):
        home[d] = lax.ppermute(home[d], ALL, [
            (i * cols_n + j, (j // per) * cols_n + (j % per) * rows_n + (i + d) % rows_n)
            for i in range(rows_n) for j in range(cols_n)])
    sender = (c % rows_n + rows_n - jnp.arange(rows_n, dtype=jnp.int32)) % rows_n

    def finish_cols(sender_ref, depth_ref, *refs):
        dst, held = refs[rows_n:]
        for d in range(rows_n):
            held[sender_ref[d]] = refs[d][...]
        for i in range(rows_n):
            for k in range(steps):
                sign = jnp.where(depth_ref[0] > k, -1.0, 0.0).astype(F32)
                dst[k, :, i * part:(i + 1) * part] = sign * held[i, :, k * part:(k + 1) * part]

    cols = local(finish_cols, (steps, share, width), [SMEM, SMEM] + [VMEM] * rows_n, sender, depth, *home,
                 scratch=[(rows_n, share, steps * part)])

    def total_kernel(src, dst):
        total = src[0]
        for i in range(1, cols_n):
            total = total + src[i]
        for i in range(cols_n):
            dst[i] = total

    every = lax.all_to_all(local(total_kernel, tiles.shape, [VMEM], summed), COL, 0, 0, tiled=True)

    def finish(src, diag_ref, link_ref, links, diags):
        for i in range(z_n):
            for j in range(x_n):
                place = (slice(i * t_rows, (i + 1) * t_rows), slice(j * t_cols, (j + 1) * t_cols))
                for k in range(steps):
                    diags[(k,) + place] = diag_ref[(k,) + place] + src[i * x_n + j, k]
                for k in range(links_n):
                    links[(k,) + place] = src[i * x_n + j, steps + k] - link_ref[(k,) + place]

    links, diags = local(finish, [(links_n, part, width), (steps, part, width)], [VMEM] * 3,
                         every, diag_own, link_own)
    return cols, links, diags


def solution(mesh):
    axes = Mesh(mesh.devices.reshape(4, 2, 8, 4), ("y", "core", "z", "x"))
    return jax.shard_map(
        shards,
        mesh=axes,
        in_specs=(P(ROW, COL), P(None, ALL, None), P(), P(), P()),
        out_specs=(P(None, ALL, None), P(None, ROW, None), P(None, ROW, None)),
        check_vma=False,
    )
```

```python
import jax
import jax.numpy as jnp
from jax import lax
from jax.experimental import pallas as pl
from jax.experimental.pallas import tpu as pltpu
from jax.sharding import Mesh, PartitionSpec as P

BLOCK = 128
ROW = ("y", "core")
COL = ("z", "x")
ALL = ROW + COL
F32 = jnp.float32
HIGHEST = lax.Precision.HIGHEST
VMEM = pl.BlockSpec(memory_space=pltpu.VMEM)
SMEM = pl.BlockSpec(memory_space=pltpu.SMEM)
ANY = pl.BlockSpec(memory_space=pl.ANY)
VMEM_BYTES = 16 * 2**20


def matmul(a, b, dims=((1,), (0,)), precision=HIGHEST):
    return lax.dot_general(a, b, (dims, ((), ())), precision=precision, preferred_element_type=F32)


def local(kernel, out_shapes, specs, *args, after=(), scratch=()):
    many = isinstance(out_shapes, list)
    shapes = [jax.ShapeDtypeStruct(s, F32) for s in (out_shapes if many else [out_shapes])]
    out = pl.pallas_call(
        lambda *refs: kernel(*refs[:len(args)], *refs[len(args) + len(after):]),
        out_shape=shapes,
        in_specs=list(specs) + [ANY] * len(after),
        out_specs=[VMEM] * len(shapes),
        scratch_shapes=[pltpu.VMEM(shape, F32) for shape in scratch],
        compiler_params=pltpu.CompilerParams(vmem_limit_bytes=VMEM_BYTES),
    )(*args, *after)
    return out if many else out[0]


def pack(pieces, after=()):
    def kernel(*refs):
        at = 0
        for ref in refs[:-1]:
            refs[-1][at:at + ref.shape[0]] = ref[...]
            at += ref.shape[0]

    rows = sum(piece.shape[0] for piece in pieces)
    return local(kernel, (rows,) + pieces[0].shape[1:], [VMEM] * len(pieces), *pieces, after=after)


def shift(value, axis, distance):
    n = lax.axis_size(axis)
    return lax.ppermute(value, axis, [(i, (i + distance) % n) for i in range(n)])


def ring(value, axis):
    half = value.shape[0] // 2
    out, up, down = [value], value, value
    for _ in range(lax.axis_size(axis) // 2 - 1):
        up, down = shift(up, axis, 1), shift(down, axis, -1)
        out += [up, down]
    return out + [shift(up[:half], axis, 1), shift(down[half:], axis, -1)]


def ring_sources(axis):
    n, me = lax.axis_size(axis), lax.axis_index(axis)
    offsets = [0]
    for s in range(1, n // 2):
        offsets += [n - s, s]
    return [(me + o) % n for o in offsets + [n // 2]]


def pick(value, index, dim):
    return lax.dynamic_index_in_dim(value, index, dim, False)


def shards(sigma_top, panel, parent_panel, diag_inverse, block_depth):
    rows_n, cols_n = lax.axis_size(ROW), lax.axis_size(COL)
    y_n, z_n, x_n = (lax.axis_size(axis) for axis in ("y", "z", "x"))
    r, c = lax.axis_index(ROW), lax.axis_index(COL)
    y_i, core, x_i = lax.axis_index("y"), lax.axis_index("core"), lax.axis_index("x")
    steps, share, width = panel.shape
    group = sigma_top.shape[1]
    part = width // rows_n
    half = steps // 2
    links_n = steps - 1
    depth = lax.dynamic_slice_in_dim(block_depth, (r * cols_n + c) * share // BLOCK, 1)

    group_panel = lax.all_gather(panel, ROW, axis=0)
    group_depth = pick(block_depth.reshape(rows_n, -1), c * share // BLOCK, 1)

    def masked(depth_ref, panel_ref, k):
        return jnp.where(depth_ref[0] > k, 1.0, 0.0).astype(F32) * panel_ref[k]

    def head_first(depth_ref, panel_ref, parent_ref, out):
        value = masked(depth_ref, panel_ref, 0)
        out[:, :width] = value
        for k in range(1, half):
            value = masked(depth_ref, panel_ref, k) - matmul(value, parent_ref[k - 1])
            out[:, k * width:(k + 1) * width] = value

    def head_second(depth_ref, panel_ref, parent_ref, first_ref, out):
        value = first_ref[:, (half - 1) * width:]
        for k in range(half, steps):
            value = masked(depth_ref, panel_ref, k) - matmul(value, parent_ref[k - 1])
            out[:, (k - half) * width:(k - half + 1) * width] = value

    n_z = local(head_first, (share, half * width), [SMEM, VMEM, VMEM], depth, panel, parent_panel)
    n_x = local(head_second, (share, half * width), [SMEM, VMEM, VMEM, VMEM], depth, panel, parent_panel, n_z)

    by_z = ring(n_z, "z")
    by_x = ring(n_x, "x")

    starts = jnp.stack([(zz * x_n + xx) * share for zz in ring_sources("z") for xx in ring_sources("x")])

    def turn(starts_ref, top, z_major, x_major):
        for i in range(z_n):
            for j in range(x_n):
                rows = top[pl.ds(pl.multiple_of(starts_ref[i * x_n + j], share), share), :]
                z_major[i, j * share:(j + 1) * share, :] = rows
                x_major[j, i * share:(i + 1) * share, :] = rows

    z_major, x_major = local(turn, [(z_n, x_n * share, group), (x_n, z_n * share, group)], [SMEM, VMEM],
                             starts.astype(jnp.int32), sigma_top, after=(by_z[1],))

    def product(total, blocks, tops):
        block = blocks[0] if len(blocks) == 1 else jnp.concatenate(blocks, axis=0)
        term = matmul(block, tops.reshape(-1, group), ((0,), (0,)), lax.Precision.HIGH)
        return term if total is None else total + term

    z_sum = x_sum = None
    arrived = ring(pack(by_z), "x")
    for j in range(x_n):
        z_sum = product(z_sum, arrived[j:] if j == x_n - 1 else arrived[j:j + 1], x_major[j:j + 1])
    arrived = ring(pack(by_x, after=(by_z[-1],)), "z")
    x_sum = product(x_sum, arrived[:1], z_major[:1])
    for j in range(1, z_n - 1, 2):
        x_sum = product(x_sum, arrived[j:j + 2], z_major[j:j + 2])
    x_sum = product(x_sum, arrived[z_n - 1:], z_major[z_n - 1:])

    def group_head(depth_ref, panel_ref, parent_ref, out):
        for k in range(steps):
            at = slice(k * width, (k + 1) * width)
            for i in range(rows_n):
                mask = jnp.where(depth_ref[i] > k, 1.0, 0.0).astype(F32)
                out[i * share:(i + 1) * share, at] = mask * panel_ref[i, k]
            if k:
                out[:, at] -= matmul(out[:, (k - 1) * width:k * width], parent_ref[k - 1])

    group_n = local(group_head, (rows_n * share, steps * width), [SMEM, VMEM, VMEM], group_depth, group_panel, parent_panel)

    def unit_rows(first_ref):
        at = lax.broadcasted_iota(jnp.int32, (part, width), 0) + first_ref[0]
        return (lax.broadcasted_iota(jnp.int32, (part, width), 1) == at).astype(F32)

    def down_first(first_ref, inverse_ref, parent_ref, left, rows):
        unit = unit_rows(first_ref)
        left[...] = matmul(unit, inverse_ref[...], ((1,), (1,)))
        rows[:part] = matmul(unit, parent_ref[...], ((1,), (1,)))
        rows[part:] = unit

    def down(first_ref, inverse_ref, parent_ref, above, left, rows):
        left[...] = matmul(above[...], inverse_ref[...], ((1,), (1,)))
        rows[:-part] = matmul(above[...], parent_ref[...], ((1,), (1,)))
        rows[-part:] = unit_rows(first_ref)

    def bottom(inverse_ref, parent_ref, above, own, carried):
        value = matmul(matmul(above[...], inverse_ref[...], ((1,), (1,))), inverse_ref[...])
        own[...] = value[-part:]
        carried[...] = matmul(value, parent_ref[...])

    def up(inverse_ref, parent_ref, left, below, own, carried):
        value = matmul(left[...], inverse_ref[...]) + below[:-part]
        own[...] = value[-part:]
        carried[...] = matmul(value, parent_ref[...])

    def up_last(inverse_ref, left, below, own):
        own[...] = matmul(left[...], inverse_ref[...]) + below[:-part]

    first = (r * part).reshape(1).astype(jnp.int32)
    lefts, rows = [None] * steps, None
    for k in range(steps - 1, 0, -1):
        args = [diag_inverse[k], parent_panel[k - 1]] + ([] if rows is None else [rows])
        tall = (steps - k) * part
        lefts[k], rows = local(down_first if rows is None else down, [(tall, width), (tall + part, width)],
                               [SMEM] + [VMEM] * len(args), first, *args)
    diag_own, link_own = [None] * steps, [None] * links_n
    diag_own[0], carried = local(bottom, [(part, width), (steps * part, width)], [VMEM] * 3,
                                 diag_inverse[0], parent_panel[0], rows)
    for k in range(1, steps):
        link_own[k - 1] = carried
        if k < steps - 1:
            diag_own[k], carried = local(up, [(part, width), ((steps - k) * part, width)], [VMEM] * 4,
                                         diag_inverse[k], parent_panel[k], lefts[k], carried)
        else:
            diag_own[k] = local(up_last, (part, width), [VMEM] * 3, diag_inverse[k], lefts[k], carried)

    def split(core_ref, total, keep, give):
        for k in range(half):
            for i in range(y_n):
                keep[k, i] = total[k, i, core_ref[0]]
                give[k, i] = total[k, i, 1 - core_ref[0]]

    core_at = core.reshape(1).astype(jnp.int32)
    pairs = []
    for total, after in ((z_sum, ()), (x_sum, (diag_own[-1],))):
        keep, give = local(split, [(half, y_n, part, group)] * 2, [SMEM, VMEM], core_at,
                           total.reshape(half, y_n, 2, part, group), after=after)
        pairs += [keep, shift(give, "core", 1)]

    def by_y(y_ref, keep_z, got_z, keep_x, got_x, *outs):
        for d in range(y_n):
            i = lax.rem(y_ref[0] + d, y_n)
            for k in range(half):
                outs[d][k] = keep_z[k, i] + got_z[k, i]
                outs[d][half + k] = keep_x[k, i] + got_x[k, i]

    summands = list(local(by_y, [(steps, part, group)] * y_n, [SMEM] + [VMEM] * 4, y_i.reshape(1).astype(jnp.int32), *pairs))
    for d in range(1, y_n):
        summands[d] = shift(summands[d], "y", d)

    per = rows_n // x_n

    def over_x(x_ref, *refs):
        parts, outs, held = refs[:y_n], refs[y_n:-1], refs[-1]
        total = sum((p[...] for p in parts[1:]), parts[0][...]).reshape(steps * part, group)
        held[...] = total.T.reshape(rows_n, share, steps * part)
        for d in range(x_n):
            for i in range(per):
                outs[d][i] = held[i * x_n + lax.rem(x_ref[0] + d, x_n)]

    def over_z(x_ref, *refs):
        for d in range(x_n):
            for i in range(per):
                refs[-1][lax.rem(x_ref[0] + x_n - d, x_n) * per + i] = refs[d][i]

    x_at = x_i.reshape(1).astype(jnp.int32)
    y_rows = list(local(over_x, [(per, share, steps * part)] * x_n, [SMEM] + [VMEM] * y_n, x_at, *summands,
                        scratch=[(rows_n, share, steps * part)]))
    for d in range(1, x_n):
        y_rows[d] = shift(y_rows[d], "x", d)
    y_rows = local(over_z, (z_n, share, steps * part), [SMEM] + [VMEM] * x_n, x_at, *y_rows)
    y_rows = lax.all_to_all(y_rows, "z", 0, 0, tiled=True)

    count = steps + links_n
    t_rows, t_cols = part // z_n, width // x_n

    def gram(y_ref, n_ref, tiles, turned):
        turned[...] = y_ref[...].reshape(rows_n * share, steps * part).T

        def put(which, value):
            for i in range(z_n):
                for j in range(x_n):
                    tiles[i * x_n + j, which] = value[i * t_rows:(i + 1) * t_rows, j * t_cols:(j + 1) * t_cols]

        for k in range(steps):
            low = max(k - 1, 0)
            value = matmul(turned[low * part:(k + 1) * part, :], n_ref[:, k * width:(k + 1) * width])
            put(k, value[(k - low) * part:])
            if k:
                put(steps + k - 1, value[:part])

    tiles = local(gram, (cols_n, count, t_rows, t_cols), [VMEM] * 2, y_rows, group_n,
                  scratch=[(steps * part, rows_n * share)])
    summed = lax.all_to_all(tiles, COL, 0, 0, tiled=True)

    home = y_rows.reshape(y_n, 2, share, steps * part)
    home = jnp.stack([pick(home, core, 1), shift(pick(home, 1 - core, 1), "core", 1)], axis=1)
    home = [pick(home, (y_i + d) % y_n, 0) for d in range(y_n)]
    home = [home[0]] + [shift(home[d], "y", d) for d in range(1, y_n)]

    def finish_cols(place_ref, depth_ref, *refs):
        dst, held = refs[y_n:]
        for d in range(y_n):
            y_from = lax.rem(place_ref[0] + y_n - d, y_n)
            held[y_from * 2 + place_ref[1]] = refs[d][0]
            held[y_from * 2 + 1 - place_ref[1]] = refs[d][1]
        for i in range(rows_n):
            for k in range(steps):
                sign = jnp.where(depth_ref[0] > k, -1.0, 0.0).astype(F32)
                dst[k, :, i * part:(i + 1) * part] = sign * held[i, :, k * part:(k + 1) * part]

    cols = local(finish_cols, (steps, share, width), [SMEM, SMEM] + [VMEM] * y_n,
                 jnp.stack([y_i, core]).astype(jnp.int32), depth, *home, scratch=[(rows_n, share, steps * part)])

    def total_kernel(src, dst):
        total = src[0]
        for i in range(1, cols_n):
            total = total + src[i]
        for i in range(cols_n):
            dst[i] = total

    every = lax.all_to_all(local(total_kernel, tiles.shape, [VMEM], summed), COL, 0, 0, tiled=True)

    def finish(src, *refs):
        diag_refs, link_refs, (links, diags) = refs[:steps], refs[steps:count], refs[count:]
        for i in range(z_n):
            for j in range(x_n):
                place = (slice(i * t_rows, (i + 1) * t_rows), slice(j * t_cols, (j + 1) * t_cols))
                for k in range(steps):
                    diags[(k,) + place] = diag_refs[k][place] + src[i * x_n + j, k]
                for k in range(links_n):
                    last = link_refs[k].shape[0] - part
                    links[(k,) + place] = src[i * x_n + j, steps + k] - link_refs[k][last + i * t_rows:last + (i + 1) * t_rows, place[1]]

    links, diags = local(finish, [(links_n, part, width), (steps, part, width)], [VMEM] * (count + 1),
                         every, *diag_own, *link_own)
    return cols, links, diags


def solution(mesh):
    axes = Mesh(mesh.devices.reshape(4, 2, 8, 4), ("y", "core", "z", "x"))
    return jax.shard_map(
        shards,
        mesh=axes,
        in_specs=(P(ROW, COL), P(None, ALL, None), P(), P(), P()),
        out_specs=(P(None, ALL, None), P(None, ROW, None), P(None, ROW, None)),
        check_vma=False,
    )
```

```python
import jax
import jax.numpy as jnp
from jax import lax
from jax.experimental import pallas as pl
from jax.experimental.pallas import tpu as pltpu
from jax.sharding import Mesh, PartitionSpec as P

BLOCK = 128
ROW = ("y", "core")
COL = ("z", "x")
ALL = ROW + COL
F32 = jnp.float32
HIGHEST = lax.Precision.HIGHEST
VMEM = pl.BlockSpec(memory_space=pltpu.VMEM)
SMEM = pl.BlockSpec(memory_space=pltpu.SMEM)
ANY = pl.BlockSpec(memory_space=pl.ANY)
MIB = 2**20


def matmul(a, b, dims=((1,), (0,)), precision=HIGHEST):
    return lax.dot_general(a, b, (dims, ((), ())), precision=precision, preferred_element_type=F32)


def local(kernel, out_shapes, specs, *args, after=(), scratch=(), vmem=4):
    many = isinstance(out_shapes, list)
    shapes = [jax.ShapeDtypeStruct(s, F32) for s in (out_shapes if many else [out_shapes])]
    out = pl.pallas_call(
        lambda *refs: kernel(*refs[:len(args)], *refs[len(args) + len(after):]),
        out_shape=shapes,
        in_specs=list(specs) + [ANY] * len(after),
        out_specs=[VMEM] * len(shapes),
        grid=(1,) if any(spec.block_shape for spec in specs) else (),
        scratch_shapes=[pltpu.VMEM(shape, F32) for shape in scratch],
        compiler_params=pltpu.CompilerParams(vmem_limit_bytes=vmem * MIB),
    )(*args, *after)
    return out if many else out[0]


def pack(pieces, after=()):
    def kernel(*refs):
        at = 0
        for ref in refs[:-1]:
            refs[-1][at:at + ref.shape[0]] = ref[...]
            at += ref.shape[0]

    rows = sum(piece.shape[0] for piece in pieces)
    return local(kernel, (rows,) + pieces[0].shape[1:], [VMEM] * len(pieces), *pieces, after=after)


def shift(value, axis, distance):
    n = lax.axis_size(axis)
    return lax.ppermute(value, axis, [(i, (i + distance) % n) for i in range(n)])


def ring(value, axis):
    half = value.shape[0] // 2
    out, up, down = [value], value, value
    for _ in range(lax.axis_size(axis) // 2 - 1):
        up, down = shift(up, axis, 1), shift(down, axis, -1)
        out += [up, down]
    return out + [shift(up[:half], axis, 1), shift(down[half:], axis, -1)]


def ring_sources(axis):
    n, me = lax.axis_size(axis), lax.axis_index(axis)
    offsets = [0]
    for s in range(1, n // 2):
        offsets += [n - s, s]
    return [(me + o) % n for o in offsets + [n // 2]]


def block(k, shape):
    return pl.BlockSpec((None,) + shape[1:], lambda i: (k,) + (0,) * (len(shape) - 1))


def pick(value, index, dim):
    return lax.dynamic_index_in_dim(value, index, dim, False)


def shards(sigma_top, panel, parent_panel, diag_inverse, block_depth):
    rows_n, cols_n = lax.axis_size(ROW), lax.axis_size(COL)
    y_n, z_n, x_n = (lax.axis_size(axis) for axis in ("y", "z", "x"))
    r, c = lax.axis_index(ROW), lax.axis_index(COL)
    y_i, core, x_i = lax.axis_index("y"), lax.axis_index("core"), lax.axis_index("x")
    steps, share, width = panel.shape
    group = sigma_top.shape[1]
    part = width // rows_n
    half = steps // 2
    links_n = steps - 1
    own_block = ((r * cols_n + c) * share // BLOCK).reshape(1).astype(jnp.int32)

    group_panel = lax.all_gather(panel, ROW, axis=0)
    group_depth = pick(block_depth.reshape(rows_n, -1), c * share // BLOCK, 1)

    def masked(block_ref, depth_ref, panel_ref, k):
        return jnp.where(depth_ref[block_ref[0]] > k, 1.0, 0.0).astype(F32) * panel_ref[k]

    def head_first(block_ref, depth_ref, panel_ref, *refs):
        parents, out = refs[:-1], refs[-1]
        value = masked(block_ref, depth_ref, panel_ref, 0)
        out[:, :width] = value
        for k in range(1, half):
            value = masked(block_ref, depth_ref, panel_ref, k) - matmul(value, parents[k - 1][...])
            out[:, k * width:(k + 1) * width] = value

    def head_second(block_ref, depth_ref, panel_ref, first_ref, *refs):
        parents, out = refs[:-1], refs[-1]
        value = first_ref[:, (half - 1) * width:]
        for k in range(half, steps):
            value = masked(block_ref, depth_ref, panel_ref, k) - matmul(value, parents[k - half][...])
            out[:, (k - half) * width:(k - half + 1) * width] = value

    parent_at = [block(k, parent_panel.shape) for k in range(links_n)]
    inverse_at = [block(k, diag_inverse.shape) for k in range(steps)]
    n_z = local(head_first, (share, half * width), [SMEM, SMEM, VMEM] + parent_at[:half - 1],
                own_block, block_depth, panel, *[parent_panel] * (half - 1))
    n_x = local(head_second, (share, half * width), [SMEM, SMEM, VMEM, VMEM] + parent_at[half - 1:],
                own_block, block_depth, panel, n_z, *[parent_panel] * (links_n - half + 1))

    by_z = ring(n_z, "z")
    by_x = ring(n_x, "x")

    starts = jnp.stack([(zz * x_n + xx) * share for zz in ring_sources("z") for xx in ring_sources("x")])

    def turn(starts_ref, top, z_major, x_major):
        for i in range(z_n):
            for j in range(x_n):
                rows = top[pl.ds(pl.multiple_of(starts_ref[i * x_n + j], share), share), :]
                z_major[i, j * share:(j + 1) * share, :] = rows
                x_major[j, i * share:(i + 1) * share, :] = rows

    z_major, x_major = local(turn, [(z_n, x_n * share, group), (x_n, z_n * share, group)], [SMEM, VMEM],
                             starts.astype(jnp.int32), sigma_top, after=(by_z[1],))

    def product(total, blocks, tops):
        block = blocks[0] if len(blocks) == 1 else jnp.concatenate(blocks, axis=0)
        term = matmul(block, tops.reshape(-1, group), ((0,), (0,)), lax.Precision.HIGH)
        return term if total is None else total + term

    z_sum = x_sum = None
    arrived = ring(pack(by_z), "x")
    for j in range(x_n):
        z_sum = product(z_sum, arrived[j:] if j == x_n - 1 else arrived[j:j + 1], x_major[j:j + 1])
    arrived = ring(pack(by_x, after=(by_z[-1],)), "z")
    x_sum = product(x_sum, arrived[:1], z_major[:1])
    for j in range(1, z_n - 1, 2):
        x_sum = product(x_sum, arrived[j:j + 2], z_major[j:j + 2])
    x_sum = product(x_sum, arrived[z_n - 1:], z_major[z_n - 1:])

    def group_head(depth_ref, panel_ref, parent_ref, out):
        for k in range(steps):
            at = slice(k * width, (k + 1) * width)
            for i in range(rows_n):
                mask = jnp.where(depth_ref[i] > k, 1.0, 0.0).astype(F32)
                out[i * share:(i + 1) * share, at] = mask * panel_ref[i, k]
            if k:
                out[:, at] -= matmul(out[:, (k - 1) * width:k * width], parent_ref[k - 1])

    group_n = local(group_head, (rows_n * share, steps * width), [SMEM, VMEM, VMEM], group_depth, group_panel, parent_panel, vmem=12)

    def unit_rows(first_ref):
        at = lax.broadcasted_iota(jnp.int32, (part, width), 0) + first_ref[0]
        return (lax.broadcasted_iota(jnp.int32, (part, width), 1) == at).astype(F32)

    def down_first(first_ref, inverse_ref, parent_ref, left, rows):
        unit = unit_rows(first_ref)
        left[...] = matmul(unit, inverse_ref[...], ((1,), (1,)))
        rows[:part] = matmul(unit, parent_ref[...], ((1,), (1,)))
        rows[part:] = unit

    def down(first_ref, inverse_ref, parent_ref, above, left, rows):
        left[...] = matmul(above[...], inverse_ref[...], ((1,), (1,)))
        rows[:-part] = matmul(above[...], parent_ref[...], ((1,), (1,)))
        rows[-part:] = unit_rows(first_ref)

    def bottom(inverse_ref, parent_ref, above, own, carried):
        value = matmul(matmul(above[...], inverse_ref[...], ((1,), (1,))), inverse_ref[...])
        own[...] = value[-part:]
        carried[...] = matmul(value, parent_ref[...])

    def up(inverse_ref, parent_ref, left, below, own, carried):
        value = matmul(left[...], inverse_ref[...]) + below[:-part]
        own[...] = value[-part:]
        carried[...] = matmul(value, parent_ref[...])

    def up_last(inverse_ref, left, below, own):
        own[...] = matmul(left[...], inverse_ref[...]) + below[:-part]

    first = (r * part).reshape(1).astype(jnp.int32)
    lefts, rows = [None] * steps, None
    for k in range(steps - 1, 0, -1):
        above = [] if rows is None else [rows]
        tall = (steps - k) * part
        lefts[k], rows = local(down if above else down_first, [(tall, width), (tall + part, width)],
                               [SMEM, inverse_at[k], parent_at[k - 1]] + [VMEM] * len(above),
                               first, diag_inverse, parent_panel, *above)
    diag_own, link_own = [None] * steps, [None] * links_n
    diag_own[0], carried = local(bottom, [(part, width), (steps * part, width)], [inverse_at[0], parent_at[0], VMEM],
                                 diag_inverse, parent_panel, rows)
    for k in range(1, steps):
        link_own[k - 1] = carried
        if k < steps - 1:
            diag_own[k], carried = local(up, [(part, width), ((steps - k) * part, width)],
                                         [inverse_at[k], parent_at[k], VMEM, VMEM],
                                         diag_inverse, parent_panel, lefts[k], carried)
        else:
            diag_own[k] = local(up_last, (part, width), [inverse_at[k], VMEM, VMEM], diag_inverse, lefts[k], carried)

    def split(core_ref, total, keep, give):
        for k in range(half):
            for i in range(y_n):
                keep[k, i] = total[k, i, core_ref[0]]
                give[k, i] = total[k, i, 1 - core_ref[0]]

    core_at = core.reshape(1).astype(jnp.int32)
    pairs = []
    for total in (z_sum, x_sum):
        keep, give = local(split, [(half, y_n, part, group)] * 2, [SMEM, VMEM], core_at,
                           total.reshape(half, y_n, 2, part, group))
        pairs += [keep, shift(give, "core", 1)]

    def by_y(y_ref, keep_z, got_z, keep_x, got_x, *outs):
        for d in range(y_n):
            i = lax.rem(y_ref[0] + d, y_n)
            for k in range(half):
                outs[d][k] = keep_z[k, i] + got_z[k, i]
                outs[d][half + k] = keep_x[k, i] + got_x[k, i]

    summands = list(local(by_y, [(steps, part, group)] * y_n, [SMEM] + [VMEM] * 4, y_i.reshape(1).astype(jnp.int32), *pairs, vmem=6))
    for d in range(1, y_n):
        summands[d] = shift(summands[d], "y", d)

    per = rows_n // x_n

    def over_x(x_ref, *refs):
        parts, outs, held = refs[:y_n], refs[y_n:-1], refs[-1]
        total = sum((p[...] for p in parts[1:]), parts[0][...]).reshape(steps * part, group)
        held[...] = total.T.reshape(rows_n, share, steps * part)
        for d in range(x_n):
            for i in range(per):
                outs[d][i] = held[i * x_n + lax.rem(x_ref[0] + d, x_n)]

    def over_z(x_ref, *refs):
        for d in range(x_n):
            for i in range(per):
                refs[-1][lax.rem(x_ref[0] + x_n - d, x_n) * per + i] = refs[d][i]

    x_at = x_i.reshape(1).astype(jnp.int32)
    y_rows = list(local(over_x, [(per, share, steps * part)] * x_n, [SMEM] + [VMEM] * y_n, x_at, *summands,
                        scratch=[(rows_n, share, steps * part)]))
    for d in range(1, x_n):
        y_rows[d] = shift(y_rows[d], "x", d)
    y_rows = local(over_z, (z_n, share, steps * part), [SMEM] + [VMEM] * x_n, x_at, *y_rows)
    y_rows = lax.all_to_all(y_rows, "z", 0, 0, tiled=True)

    count = steps + links_n
    t_rows, t_cols = part // z_n, width // x_n

    def gram(y_ref, n_ref, tiles, turned):
        turned[...] = y_ref[...].reshape(rows_n * share, steps * part).T

        def put(which, value):
            for i in range(z_n):
                for j in range(x_n):
                    tiles[i * x_n + j, which] = value[i * t_rows:(i + 1) * t_rows, j * t_cols:(j + 1) * t_cols]

        for k in range(steps):
            low = max(k - 1, 0)
            value = matmul(turned[low * part:(k + 1) * part, :], n_ref[:, k * width:(k + 1) * width])
            put(k, value[(k - low) * part:])
            if k:
                put(steps + k - 1, value[:part])

    tiles = local(gram, (cols_n, count, t_rows, t_cols), [VMEM] * 2, y_rows, group_n, after=(diag_own[-1],), vmem=8,
                  scratch=[(steps * part, rows_n * share)])
    summed = lax.all_to_all(tiles, COL, 0, 0, tiled=True)

    home = y_rows.reshape(y_n, 2, share, steps * part)
    home = jnp.stack([pick(home, core, 1), shift(pick(home, 1 - core, 1), "core", 1)], axis=1)
    home = [pick(home, (y_i + d) % y_n, 0) for d in range(y_n)]
    home = [home[0]] + [shift(home[d], "y", d) for d in range(1, y_n)]

    def finish_cols(place_ref, block_ref, depth_ref, *refs):
        dst, held = refs[y_n:]
        for d in range(y_n):
            y_from = lax.rem(place_ref[0] + y_n - d, y_n)
            held[y_from * 2 + place_ref[1]] = refs[d][0]
            held[y_from * 2 + 1 - place_ref[1]] = refs[d][1]
        for i in range(rows_n):
            for k in range(steps):
                sign = jnp.where(depth_ref[block_ref[0]] > k, -1.0, 0.0).astype(F32)
                dst[k, :, i * part:(i + 1) * part] = sign * held[i, :, k * part:(k + 1) * part]

    cols = local(finish_cols, (steps, share, width), [SMEM] * 3 + [VMEM] * y_n,
                 jnp.stack([y_i, core]).astype(jnp.int32), own_block, block_depth, *home, scratch=[(rows_n, share, steps * part)])

    def total_kernel(src, dst):
        total = src[0]
        for i in range(1, cols_n):
            total = total + src[i]
        for i in range(cols_n):
            dst[i] = total

    every = lax.all_to_all(local(total_kernel, tiles.shape, [VMEM], summed), COL, 0, 0, tiled=True)

    def finish(src, *refs):
        diag_refs, link_refs, (links, diags) = refs[:steps], refs[steps:count], refs[count:]
        for i in range(z_n):
            for j in range(x_n):
                place = (slice(i * t_rows, (i + 1) * t_rows), slice(j * t_cols, (j + 1) * t_cols))
                for k in range(steps):
                    diags[(k,) + place] = diag_refs[k][place] + src[i * x_n + j, k]
                for k in range(links_n):
                    last = link_refs[k].shape[0] - part
                    links[(k,) + place] = src[i * x_n + j, steps + k] - link_refs[k][last + i * t_rows:last + (i + 1) * t_rows, place[1]]

    links, diags = local(finish, [(links_n, part, width), (steps, part, width)], [VMEM] * (count + 1),
                         every, *diag_own, *link_own)
    return cols, links, diags


def solution(mesh):
    axes = Mesh(mesh.devices.reshape(4, 2, 8, 4), ("y", "core", "z", "x"))
    return jax.shard_map(
        shards,
        mesh=axes,
        in_specs=(P(ROW, COL), P(None, ALL, None), P(), P(), P()),
        out_specs=(P(None, ALL, None), P(None, ROW, None), P(None, ROW, None)),
        check_vma=False,
    )
```

```python
import jax
import jax.numpy as jnp
from jax import lax
from jax.experimental import pallas as pl
from jax.experimental.pallas import tpu as pltpu
from jax.sharding import Mesh, PartitionSpec as P

BLOCK = 128
ROW = ("y", "core")
COL = ("z", "x")
ALL = ROW + COL
F32 = jnp.float32
HIGHEST = lax.Precision.HIGHEST
VMEM = pl.BlockSpec(memory_space=pltpu.VMEM)
SMEM = pl.BlockSpec(memory_space=pltpu.SMEM)
ANY = pl.BlockSpec(memory_space=pl.ANY)
HBM = pl.BlockSpec(memory_space=pltpu.HBM)
MIB = 2**20


def matmul(a, b, dims=((1,), (0,)), precision=HIGHEST):
    return lax.dot_general(a, b, (dims, ((), ())), precision=precision, preferred_element_type=F32)


def local(kernel, out_shapes, specs, *args, after=(), scratch=(), semaphores=0, vmem=4):
    many = isinstance(out_shapes, list)
    shapes = [jax.ShapeDtypeStruct(s, F32) for s in (out_shapes if many else [out_shapes])]
    out = pl.pallas_call(
        lambda *refs: kernel(*refs[:len(args)], *refs[len(args) + len(after):]),
        out_shape=shapes,
        in_specs=list(specs) + [ANY] * len(after),
        out_specs=[VMEM] * len(shapes),
        grid=(1,) if any(spec.block_shape for spec in specs) else (),
        scratch_shapes=[pltpu.VMEM(shape, F32) for shape in scratch]
        + ([pltpu.SemaphoreType.DMA((semaphores,))] if semaphores else []),
        compiler_params=pltpu.CompilerParams(vmem_limit_bytes=vmem * MIB),
    )(*args, *after)
    return out if many else out[0]


def pack(pieces, after=()):
    def kernel(*refs):
        at = 0
        for ref in refs[:-1]:
            refs[-1][at:at + ref.shape[0]] = ref[...]
            at += ref.shape[0]

    rows = sum(piece.shape[0] for piece in pieces)
    return local(kernel, (rows,) + pieces[0].shape[1:], [VMEM] * len(pieces), *pieces, after=after)


def shift(value, axis, distance):
    n = lax.axis_size(axis)
    return lax.ppermute(value, axis, [(i, (i + distance) % n) for i in range(n)])


def ring(value, axis):
    half = value.shape[0] // 2
    out, up, down = [value], value, value
    for _ in range(lax.axis_size(axis) // 2 - 1):
        up, down = shift(up, axis, 1), shift(down, axis, -1)
        out += [up, down]
    return out + [shift(up[:half], axis, 1), shift(down[half:], axis, -1)]


def ring_sources(axis):
    n, me = lax.axis_size(axis), lax.axis_index(axis)
    offsets = [0]
    for s in range(1, n // 2):
        offsets += [n - s, s]
    return [(me + o) % n for o in offsets + [n // 2]]


def block(k, shape):
    return pl.BlockSpec((None,) + shape[1:], lambda i: (k,) + (0,) * (len(shape) - 1))


def pick(value, index, dim):
    return lax.dynamic_index_in_dim(value, index, dim, False)


def shards(sigma_top, panel, parent_panel, diag_inverse, block_depth):
    rows_n, cols_n = lax.axis_size(ROW), lax.axis_size(COL)
    y_n, z_n, x_n = (lax.axis_size(axis) for axis in ("y", "z", "x"))
    r, c = lax.axis_index(ROW), lax.axis_index(COL)
    y_i, core, x_i = lax.axis_index("y"), lax.axis_index("core"), lax.axis_index("x")
    steps, share, width = panel.shape
    group = sigma_top.shape[1]
    part = width // rows_n
    half = steps // 2
    links_n = steps - 1
    own_block = ((r * cols_n + c) * share // BLOCK).reshape(1).astype(jnp.int32)

    group_panel = lax.all_gather(panel, ROW, axis=0)
    group_depth = pick(block_depth.reshape(rows_n, -1), c * share // BLOCK, 1)

    def masked(block_ref, depth_ref, panel_ref, k):
        return jnp.where(depth_ref[block_ref[0]] > k, 1.0, 0.0).astype(F32) * panel_ref[k]

    def head_first(block_ref, depth_ref, panel_hbm, parent_hbm, out, panel_ref, parent_ref, arrived):
        copies = [pltpu.make_async_copy(panel_hbm.at[:half], panel_ref, arrived.at[0]),
                  pltpu.make_async_copy(parent_hbm.at[:half - 1], parent_ref, arrived.at[1])]
        for copy in copies:
            copy.start()
        copies[0].wait()
        value = masked(block_ref, depth_ref, panel_ref, 0)
        out[:, :width] = value
        copies[1].wait()
        for k in range(1, half):
            value = masked(block_ref, depth_ref, panel_ref, k) - matmul(value, parent_ref[k - 1])
            out[:, k * width:(k + 1) * width] = value

    def head_second(block_ref, depth_ref, panel_ref, first_ref, *refs):
        parents, out = refs[:-1], refs[-1]
        value = first_ref[:, (half - 1) * width:]
        for k in range(half, steps):
            value = masked(block_ref, depth_ref, panel_ref, k) - matmul(value, parents[k - half][...])
            out[:, (k - half) * width:(k - half + 1) * width] = value

    parent_at = [block(k, parent_panel.shape) for k in range(links_n)]
    inverse_at = [block(k, diag_inverse.shape) for k in range(steps)]
    n_z = local(head_first, (share, half * width), [SMEM, SMEM, HBM, HBM], own_block, block_depth, panel, parent_panel,
                scratch=[(half, share, width), (half - 1, width, width)], semaphores=2)
    n_x = local(head_second, (share, half * width), [SMEM, SMEM, VMEM, VMEM] + parent_at[half - 1:],
                own_block, block_depth, panel, n_z, *[parent_panel] * (links_n - half + 1))

    by_z = ring(n_z, "z")
    by_x = ring(n_x, "x")

    starts = jnp.stack([(zz * x_n + xx) * share for zz in ring_sources("z") for xx in ring_sources("x")])

    def turn(starts_ref, top, z_major, x_major):
        for i in range(z_n):
            for j in range(x_n):
                rows = top[pl.ds(pl.multiple_of(starts_ref[i * x_n + j], share), share), :]
                z_major[i, j * share:(j + 1) * share, :] = rows
                x_major[j, i * share:(i + 1) * share, :] = rows

    z_major, x_major = local(turn, [(z_n, x_n * share, group), (x_n, z_n * share, group)], [SMEM, VMEM],
                             starts.astype(jnp.int32), sigma_top, after=(by_z[1],))

    def product(total, blocks, tops):
        block = blocks[0] if len(blocks) == 1 else jnp.concatenate(blocks, axis=0)
        term = matmul(block, tops.reshape(-1, group), ((0,), (0,)), lax.Precision.HIGH)
        return term if total is None else total + term

    z_sum = x_sum = None
    arrived = ring(pack(by_z), "x")
    for j in range(x_n):
        z_sum = product(z_sum, arrived[j:] if j == x_n - 1 else arrived[j:j + 1], x_major[j:j + 1])
    arrived = ring(pack(by_x, after=(by_z[-1],)), "z")
    x_sum = product(x_sum, arrived[:1], z_major[:1])
    for j in range(1, z_n - 1, 2):
        x_sum = product(x_sum, arrived[j:j + 2], z_major[j:j + 2])
    x_sum = product(x_sum, arrived[z_n - 1:], z_major[z_n - 1:])

    def group_head(depth_ref, panel_ref, parent_ref, out):
        for k in range(steps):
            at = slice(k * width, (k + 1) * width)
            for i in range(rows_n):
                mask = jnp.where(depth_ref[i] > k, 1.0, 0.0).astype(F32)
                out[i * share:(i + 1) * share, at] = mask * panel_ref[i, k]
            if k:
                out[:, at] -= matmul(out[:, (k - 1) * width:k * width], parent_ref[k - 1])

    group_n = local(group_head, (rows_n * share, steps * width), [SMEM, VMEM, VMEM], group_depth, group_panel, parent_panel, vmem=12)

    def split(core_ref, total, keep, give):
        for k in range(half):
            for i in range(y_n):
                keep[k, i] = total[k, i, core_ref[0]]
                give[k, i] = total[k, i, 1 - core_ref[0]]

    core_at = core.reshape(1).astype(jnp.int32)
    pairs = []
    for total in (z_sum, x_sum):
        keep, give = local(split, [(half, y_n, part, group)] * 2, [SMEM, VMEM], core_at,
                           total.reshape(half, y_n, 2, part, group))
        pairs += [keep, shift(give, "core", 1)]

    def by_y(y_ref, keep_z, got_z, keep_x, got_x, *outs):
        for d in range(y_n):
            i = lax.rem(y_ref[0] + d, y_n)
            for k in range(half):
                outs[d][k] = keep_z[k, i] + got_z[k, i]
                outs[d][half + k] = keep_x[k, i] + got_x[k, i]

    summands = list(local(by_y, [(steps, part, group)] * y_n, [SMEM] + [VMEM] * 4, y_i.reshape(1).astype(jnp.int32), *pairs, vmem=6))
    for d in range(1, y_n):
        summands[d] = shift(summands[d], "y", d)

    per = rows_n // x_n

    def over_x(x_ref, *refs):
        parts, outs, held = refs[:y_n], refs[y_n:-1], refs[-1]
        total = sum((p[...] for p in parts[1:]), parts[0][...]).reshape(steps * part, group)
        held[...] = total.T.reshape(rows_n, share, steps * part)
        for d in range(x_n):
            for i in range(per):
                outs[d][i] = held[i * x_n + lax.rem(x_ref[0] + d, x_n)]

    def over_z(x_ref, *refs):
        for d in range(x_n):
            for i in range(per):
                refs[-1][lax.rem(x_ref[0] + x_n - d, x_n) * per + i] = refs[d][i]

    x_at = x_i.reshape(1).astype(jnp.int32)
    y_rows = list(local(over_x, [(per, share, steps * part)] * x_n, [SMEM] + [VMEM] * y_n, x_at, *summands,
                        after=(group_n,), scratch=[(rows_n, share, steps * part)]))
    for d in range(1, x_n):
        y_rows[d] = shift(y_rows[d], "x", d)
    y_rows = local(over_z, (z_n, share, steps * part), [SMEM] + [VMEM] * x_n, x_at, *y_rows)
    y_rows = lax.all_to_all(y_rows, "z", 0, 0, tiled=True)

    count = steps + links_n
    t_rows, t_cols = part // z_n, width // x_n

    def gram(y_ref, n_ref, tiles, turned):
        turned[...] = y_ref[...].reshape(rows_n * share, steps * part).T

        def put(which, value):
            for i in range(z_n):
                for j in range(x_n):
                    tiles[i * x_n + j, which] = value[i * t_rows:(i + 1) * t_rows, j * t_cols:(j + 1) * t_cols]

        for k in range(steps):
            low = max(k - 1, 0)
            value = matmul(turned[low * part:(k + 1) * part, :], n_ref[:, k * width:(k + 1) * width])
            put(k, value[(k - low) * part:])
            if k:
                put(steps + k - 1, value[:part])

    tiles = local(gram, (cols_n, count, t_rows, t_cols), [VMEM] * 2, y_rows, group_n, vmem=8,
                  scratch=[(steps * part, rows_n * share)])
    summed = lax.all_to_all(tiles, COL, 0, 0, tiled=True)

    home = y_rows.reshape(y_n, 2, share, steps * part)
    home = jnp.stack([pick(home, core, 1), shift(pick(home, 1 - core, 1), "core", 1)], axis=1)
    home = [pick(home, (y_i + d) % y_n, 0) for d in range(y_n)]
    home = [home[0]] + [shift(home[d], "y", d) for d in range(1, y_n)]

    def finish_cols(place_ref, block_ref, depth_ref, *refs):
        dst, held = refs[y_n:]
        for d in range(y_n):
            y_from = lax.rem(place_ref[0] + y_n - d, y_n)
            held[y_from * 2 + place_ref[1]] = refs[d][0]
            held[y_from * 2 + 1 - place_ref[1]] = refs[d][1]
        for i in range(rows_n):
            for k in range(steps):
                sign = jnp.where(depth_ref[block_ref[0]] > k, -1.0, 0.0).astype(F32)
                dst[k, :, i * part:(i + 1) * part] = sign * held[i, :, k * part:(k + 1) * part]

    cols = local(finish_cols, (steps, share, width), [SMEM] * 3 + [VMEM] * y_n,
                 jnp.stack([y_i, core]).astype(jnp.int32), own_block, block_depth, *home, scratch=[(rows_n, share, steps * part)])

    def unit_rows(first_ref):
        at = lax.broadcasted_iota(jnp.int32, (part, width), 0) + first_ref[0]
        return (lax.broadcasted_iota(jnp.int32, (part, width), 1) == at).astype(F32)

    def down_first(first_ref, inverse_ref, parent_ref, left, rows):
        unit = unit_rows(first_ref)
        left[...] = matmul(unit, inverse_ref[...], ((1,), (1,)))
        rows[:part] = matmul(unit, parent_ref[...], ((1,), (1,)))
        rows[part:] = unit

    def down(first_ref, inverse_ref, parent_ref, above, left, rows):
        left[...] = matmul(above[...], inverse_ref[...], ((1,), (1,)))
        rows[:-part] = matmul(above[...], parent_ref[...], ((1,), (1,)))
        rows[-part:] = unit_rows(first_ref)

    def bottom(inverse_ref, parent_ref, above, own, carried):
        value = matmul(matmul(above[...], inverse_ref[...], ((1,), (1,))), inverse_ref[...])
        own[...] = value[-part:]
        carried[...] = matmul(value, parent_ref[...])

    def up(inverse_ref, parent_ref, left, below, own, carried):
        value = matmul(left[...], inverse_ref[...]) + below[:-part]
        own[...] = value[-part:]
        carried[...] = matmul(value, parent_ref[...])

    def up_last(inverse_ref, left, below, own):
        own[...] = matmul(left[...], inverse_ref[...]) + below[:-part]

    first = (r * part).reshape(1).astype(jnp.int32)
    lefts, rows = [None] * steps, None
    for k in range(steps - 1, 0, -1):
        above = [] if rows is None else [rows]
        tall = (steps - k) * part
        lefts[k], rows = local(down if above else down_first, [(tall, width), (tall + part, width)],
                               [SMEM, inverse_at[k], parent_at[k - 1]] + [VMEM] * len(above),
                               first, diag_inverse, parent_panel, *above, after=() if above else (tiles,))
    diag_own, link_own = [None] * steps, [None] * links_n
    diag_own[0], carried = local(bottom, [(part, width), (steps * part, width)], [inverse_at[0], parent_at[0], VMEM],
                                 diag_inverse, parent_panel, rows)
    for k in range(1, steps):
        link_own[k - 1] = carried
        if k < steps - 1:
            diag_own[k], carried = local(up, [(part, width), ((steps - k) * part, width)],
                                         [inverse_at[k], parent_at[k], VMEM, VMEM],
                                         diag_inverse, parent_panel, lefts[k], carried)
        else:
            diag_own[k] = local(up_last, (part, width), [inverse_at[k], VMEM, VMEM], diag_inverse, lefts[k], carried)

    def total_kernel(src, dst):
        total = src[0]
        for i in range(1, cols_n):
            total = total + src[i]
        for i in range(cols_n):
            dst[i] = total

    every = lax.all_to_all(local(total_kernel, tiles.shape, [VMEM], summed, after=(diag_own[-1],)), COL, 0, 0, tiled=True)

    def finish(src, *refs):
        diag_refs, link_refs, (links, diags) = refs[:steps], refs[steps:count], refs[count:]
        for i in range(z_n):
            for j in range(x_n):
                place = (slice(i * t_rows, (i + 1) * t_rows), slice(j * t_cols, (j + 1) * t_cols))
                for k in range(steps):
                    diags[(k,) + place] = diag_refs[k][place] + src[i * x_n + j, k]
                for k in range(links_n):
                    last = link_refs[k].shape[0] - part
                    links[(k,) + place] = src[i * x_n + j, steps + k] - link_refs[k][last + i * t_rows:last + (i + 1) * t_rows, place[1]]

    links, diags = local(finish, [(links_n, part, width), (steps, part, width)], [VMEM] * (count + 1),
                         every, *diag_own, *link_own)
    return cols, links, diags


def solution(mesh):
    axes = Mesh(mesh.devices.reshape(4, 2, 8, 4), ("y", "core", "z", "x"))
    return jax.shard_map(
        shards,
        mesh=axes,
        in_specs=(P(ROW, COL), P(None, ALL, None), P(), P(), P()),
        out_specs=(P(None, ALL, None), P(None, ROW, None), P(None, ROW, None)),
        check_vma=False,
    )
```

```python
import jax
import jax.numpy as jnp
from jax import lax
from jax.experimental import pallas as pl
from jax.experimental.pallas import tpu as pltpu
from jax.sharding import Mesh, PartitionSpec as P

BLOCK = 128
ROW = ("y", "core")
COL = ("z", "x")
ALL = ROW + COL
F32 = jnp.float32
HIGHEST = lax.Precision.HIGHEST
VMEM = pl.BlockSpec(memory_space=pltpu.VMEM)
SMEM = pl.BlockSpec(memory_space=pltpu.SMEM)
ANY = pl.BlockSpec(memory_space=pl.ANY)
HBM = pl.BlockSpec(memory_space=pltpu.HBM)
MIB = 2**20


def matmul(a, b, dims=((1,), (0,)), precision=HIGHEST):
    return lax.dot_general(a, b, (dims, ((), ())), precision=precision, preferred_element_type=F32)


def local(kernel, out_shapes, specs, *args, after=(), scratch=(), semaphores=0, vmem=4):
    many = isinstance(out_shapes, list)
    shapes = [jax.ShapeDtypeStruct(s, F32) for s in (out_shapes if many else [out_shapes])]
    out = pl.pallas_call(
        lambda *refs: kernel(*refs[:len(args)], *refs[len(args) + len(after):]),
        out_shape=shapes,
        in_specs=list(specs) + [ANY] * len(after),
        out_specs=[VMEM] * len(shapes),
        grid=(1,) if any(spec.block_shape for spec in specs) else (),
        scratch_shapes=[pltpu.VMEM(shape, F32) if isinstance(shape, tuple) else shape for shape in scratch]
        + ([pltpu.SemaphoreType.DMA((semaphores,))] if semaphores else []),
        compiler_params=pltpu.CompilerParams(vmem_limit_bytes=vmem * MIB),
    )(*args, *after)
    return out if many else out[0]


def pack(pieces, after=()):
    def kernel(*refs):
        at = 0
        for ref in refs[:-1]:
            refs[-1][at:at + ref.shape[0]] = ref[...]
            at += ref.shape[0]

    rows = sum(piece.shape[0] for piece in pieces)
    return local(kernel, (rows,) + pieces[0].shape[1:], [VMEM] * len(pieces), *pieces, after=after)


def shift(value, axis, distance):
    n = lax.axis_size(axis)
    return lax.ppermute(value, axis, [(i, (i + distance) % n) for i in range(n)])


def ring(value, axis):
    half = value.shape[0] // 2
    out, up, down = [value], value, value
    for _ in range(lax.axis_size(axis) // 2 - 1):
        up, down = shift(up, axis, 1), shift(down, axis, -1)
        out += [up, down]
    return out + [shift(up[:half], axis, 1), shift(down[half:], axis, -1)]


def ring_sources(axis):
    n, me = lax.axis_size(axis), lax.axis_index(axis)
    offsets = [0]
    for s in range(1, n // 2):
        offsets += [n - s, s]
    return [(me + o) % n for o in offsets + [n // 2]]


def block(k, shape):
    return pl.BlockSpec((None,) + shape[1:], lambda i: (k,) + (0,) * (len(shape) - 1))


def pick(value, index, dim):
    return lax.dynamic_index_in_dim(value, index, dim, False)


def shards(sigma_top, panel, parent_panel, diag_inverse, block_depth):
    rows_n, cols_n = lax.axis_size(ROW), lax.axis_size(COL)
    y_n, z_n, x_n = (lax.axis_size(axis) for axis in ("y", "z", "x"))
    r, c = lax.axis_index(ROW), lax.axis_index(COL)
    y_i, core, x_i = lax.axis_index("y"), lax.axis_index("core"), lax.axis_index("x")
    steps, share, width = panel.shape
    group = sigma_top.shape[1]
    part = width // rows_n
    units = steps * y_n
    z_units = (units * 9 + 8) // 16
    cut = z_units * 2 * part
    mid, off = cut // width, cut % width
    links_n = steps - 1
    own_block = ((r * cols_n + c) * share // BLOCK).reshape(1).astype(jnp.int32)

    group_panel = lax.all_gather(panel, ROW, axis=0)
    group_depth = pick(block_depth.reshape(rows_n, -1), c * share // BLOCK, 1)

    def fetch(copies, arrived):
        copies = [pltpu.make_async_copy(src, dst, arrived.at[i]) for i, (src, dst) in enumerate(copies)]
        for copy in copies:
            copy.start()
        for copy in copies:
            copy.wait()

    def masked(block_ref, depth_ref, value, k):
        return jnp.where(depth_ref[block_ref[0]] > k, 1.0, 0.0).astype(F32) * value

    def head_first(block_ref, depth_hbm, panel_hbm, parent_hbm, out, middle, panel_ref, parent_ref, depth_ref, arrived):
        fetch([(depth_hbm, depth_ref), (panel_hbm.at[:mid + 1], panel_ref), (parent_hbm.at[:mid], parent_ref)], arrived)
        value = None
        for k in range(mid + 1):
            own = masked(block_ref, depth_ref, panel_ref[k], k)
            value = own - matmul(value, parent_ref[k - 1]) if k else own
            columns = min(width, cut - k * width)
            if columns:
                out[:, k * width:k * width + columns] = value[:, :columns]
        middle[...] = value

    def head_second(block_ref, depth_hbm, panel_hbm, parent_hbm, middle, out, panel_ref, parent_ref, depth_ref, arrived):
        fetch([(depth_hbm, depth_ref), (panel_hbm.at[mid + 1:], panel_ref), (parent_hbm.at[mid:], parent_ref)], arrived)
        value = middle[...]
        out[:, :width - off] = value[:, off:]
        for k in range(mid + 1, steps):
            own = masked(block_ref, depth_ref, panel_ref[k - mid - 1], k)
            value = own - matmul(value, parent_ref[k - mid - 1])
            out[:, k * width - cut:(k + 1) * width - cut] = value

    depth_at = pltpu.SMEM(block_depth.shape, jnp.int32)
    heads = [SMEM, HBM, HBM, HBM]
    n_z, middle = local(head_first, [(share, cut), (share, width)], heads, own_block, block_depth, panel, parent_panel,
                        scratch=[(mid + 1, share, width), (mid, width, width), depth_at], semaphores=3)
    n_x = local(head_second, (share, steps * width - cut), heads + [VMEM], own_block, block_depth, panel, parent_panel,
                middle, scratch=[(links_n - mid, share, width), (links_n - mid, width, width), depth_at], semaphores=3)

    by_z = ring(n_z, "z")
    by_x = ring(n_x, "x")

    starts = jnp.stack([(zz * x_n + xx) * share for zz in ring_sources("z") for xx in ring_sources("x")])

    def turn(starts_ref, top, z_major, x_major):
        for i in range(z_n):
            for j in range(x_n):
                rows = top[pl.ds(pl.multiple_of(starts_ref[i * x_n + j], share), share), :]
                z_major[i, j * share:(j + 1) * share, :] = rows
                x_major[j, i * share:(i + 1) * share, :] = rows

    z_major, x_major = local(turn, [(z_n, x_n * share, group), (x_n, z_n * share, group)], [SMEM, VMEM],
                             starts.astype(jnp.int32), sigma_top, after=(by_z[1],))

    def product(total, blocks, tops):
        block = blocks[0] if len(blocks) == 1 else jnp.concatenate(blocks, axis=0)
        term = matmul(block, tops.reshape(-1, group), ((0,), (0,)), lax.Precision.HIGH)
        return term if total is None else total + term

    z_sum = x_sum = None
    arrived = ring(pack(by_z), "x")
    for j in range(x_n):
        z_sum = product(z_sum, arrived[j:] if j == x_n - 1 else arrived[j:j + 1], x_major[j:j + 1])
    arrived = ring(pack(by_x, after=(by_z[-1],)), "z")
    x_sum = product(x_sum, arrived[:1], z_major[:1])
    for j in range(1, z_n - 1, 2):
        x_sum = product(x_sum, arrived[j:j + 2], z_major[j:j + 2])
    x_sum = product(x_sum, arrived[z_n - 1:], z_major[z_n - 1:])

    def group_head(depth_ref, panel_ref, parent_ref, out):
        for k in range(steps):
            at = slice(k * width, (k + 1) * width)
            for i in range(rows_n):
                mask = jnp.where(depth_ref[i] > k, 1.0, 0.0).astype(F32)
                out[i * share:(i + 1) * share, at] = mask * panel_ref[i, k]
            if k:
                out[:, at] -= matmul(out[:, (k - 1) * width:k * width], parent_ref[k - 1])

    group_n = local(group_head, (rows_n * share, steps * width), [SMEM, VMEM, VMEM], group_depth, group_panel, parent_panel, vmem=12)

    def split(core_ref, z_ref, x_ref, keep, give):
        for unit in range(units):
            ref, at = (z_ref, unit) if unit < z_units else (x_ref, unit - z_units)
            keep[unit // y_n, unit % y_n] = ref[at, core_ref[0]]
            give[unit // y_n, unit % y_n] = ref[at, 1 - core_ref[0]]

    keep, give = local(split, [(steps, y_n, part, group)] * 2, [SMEM, VMEM, VMEM], core.reshape(1).astype(jnp.int32),
                       z_sum.reshape(z_units, 2, part, group), x_sum.reshape(units - z_units, 2, part, group), vmem=6)
    got = shift(give, "core", 1)

    def by_y(y_ref, keep_ref, got_ref, *outs):
        for d in range(y_n):
            i = lax.rem(y_ref[0] + d, y_n)
            for k in range(steps):
                outs[d][k] = keep_ref[k, i] + got_ref[k, i]

    summands = list(local(by_y, [(steps, part, group)] * y_n, [SMEM, VMEM, VMEM], y_i.reshape(1).astype(jnp.int32),
                          keep, got, vmem=6))
    for d in range(1, y_n):
        summands[d] = shift(summands[d], "y", d)

    per = rows_n // x_n

    def over_x(x_ref, *refs):
        parts, outs, held = refs[:y_n], refs[y_n:-1], refs[-1]
        total = sum((p[...] for p in parts[1:]), parts[0][...]).reshape(steps * part, group)
        held[...] = total.T.reshape(rows_n, share, steps * part)
        for d in range(x_n):
            for i in range(per):
                outs[d][i] = held[i * x_n + lax.rem(x_ref[0] + d, x_n)]

    def over_z(x_ref, *refs):
        for d in range(x_n):
            for i in range(per):
                refs[-1][lax.rem(x_ref[0] + x_n - d, x_n) * per + i] = refs[d][i]

    x_at = x_i.reshape(1).astype(jnp.int32)
    y_rows = list(local(over_x, [(per, share, steps * part)] * x_n, [SMEM] + [VMEM] * y_n, x_at, *summands,
                        after=(group_n,), scratch=[(rows_n, share, steps * part)]))
    for d in range(1, x_n):
        y_rows[d] = shift(y_rows[d], "x", d)
    y_rows = local(over_z, (z_n, share, steps * part), [SMEM] + [VMEM] * x_n, x_at, *y_rows)
    y_rows = lax.all_to_all(y_rows, "z", 0, 0, tiled=True)

    count = steps + links_n
    t_rows, t_cols = part // z_n, width // x_n

    def gram(y_ref, n_ref, tiles, turned):
        turned[...] = y_ref[...].reshape(rows_n * share, steps * part).T

        def put(which, value):
            for i in range(z_n):
                for j in range(x_n):
                    tiles[i * x_n + j, which] = value[i * t_rows:(i + 1) * t_rows, j * t_cols:(j + 1) * t_cols]

        for k in range(steps):
            low = max(k - 1, 0)
            value = matmul(turned[low * part:(k + 1) * part, :], n_ref[:, k * width:(k + 1) * width])
            put(k, value[(k - low) * part:])
            if k:
                put(steps + k - 1, value[:part])

    tiles = local(gram, (cols_n, count, t_rows, t_cols), [VMEM] * 2, y_rows, group_n, vmem=8,
                  scratch=[(steps * part, rows_n * share)])
    summed = lax.all_to_all(tiles, COL, 0, 0, tiled=True)

    home = y_rows.reshape(y_n, 2, share, steps * part)
    home = jnp.stack([pick(home, core, 1), shift(pick(home, 1 - core, 1), "core", 1)], axis=1)
    home = [pick(home, (y_i + d) % y_n, 0) for d in range(y_n)]
    home = [home[0]] + [shift(home[d], "y", d) for d in range(1, y_n)]

    def finish_cols(place_ref, block_ref, depth_ref, *refs):
        dst, held = refs[y_n:]
        for d in range(y_n):
            y_from = lax.rem(place_ref[0] + y_n - d, y_n)
            held[y_from * 2 + place_ref[1]] = refs[d][0]
            held[y_from * 2 + 1 - place_ref[1]] = refs[d][1]
        for i in range(rows_n):
            for k in range(steps):
                sign = jnp.where(depth_ref[block_ref[0]] > k, -1.0, 0.0).astype(F32)
                dst[k, :, i * part:(i + 1) * part] = sign * held[i, :, k * part:(k + 1) * part]

    cols = local(finish_cols, (steps, share, width), [SMEM] * 3 + [VMEM] * y_n,
                 jnp.stack([y_i, core]).astype(jnp.int32), own_block, block_depth, *home, scratch=[(rows_n, share, steps * part)])

    def unit_rows(first_ref):
        at = lax.broadcasted_iota(jnp.int32, (part, width), 0) + first_ref[0]
        return (lax.broadcasted_iota(jnp.int32, (part, width), 1) == at).astype(F32)

    def down_first(first_ref, inverse_ref, parent_ref, left, rows):
        unit = unit_rows(first_ref)
        left[...] = matmul(unit, inverse_ref[...], ((1,), (1,)))
        rows[:part] = matmul(unit, parent_ref[...], ((1,), (1,)))
        rows[part:] = unit

    def down(first_ref, inverse_ref, parent_ref, above, left, rows):
        left[...] = matmul(above[...], inverse_ref[...], ((1,), (1,)))
        rows[:-part] = matmul(above[...], parent_ref[...], ((1,), (1,)))
        rows[-part:] = unit_rows(first_ref)

    def bottom(inverse_ref, parent_ref, above, own, carried):
        value = matmul(matmul(above[...], inverse_ref[...], ((1,), (1,))), inverse_ref[...])
        own[...] = value[-part:]
        carried[...] = matmul(value, parent_ref[...])

    def up(inverse_ref, parent_ref, left, below, own, carried):
        value = matmul(left[...], inverse_ref[...]) + below[:-part]
        own[...] = value[-part:]
        carried[...] = matmul(value, parent_ref[...])

    def up_last(inverse_ref, left, below, own):
        own[...] = matmul(left[...], inverse_ref[...]) + below[:-part]

    parent_at = [block(k, parent_panel.shape) for k in range(links_n)]
    inverse_at = [block(k, diag_inverse.shape) for k in range(steps)]
    first = (r * part).reshape(1).astype(jnp.int32)
    lefts, rows = [None] * steps, None
    for k in range(steps - 1, 0, -1):
        above = [] if rows is None else [rows]
        tall = (steps - k) * part
        lefts[k], rows = local(down if above else down_first, [(tall, width), (tall + part, width)],
                               [SMEM, inverse_at[k], parent_at[k - 1]] + [VMEM] * len(above),
                               first, diag_inverse, parent_panel, *above, after=() if above else (tiles,))
    diag_own, link_own = [None] * steps, [None] * links_n
    diag_own[0], carried = local(bottom, [(part, width), (steps * part, width)], [inverse_at[0], parent_at[0], VMEM],
                                 diag_inverse, parent_panel, rows)
    for k in range(1, steps):
        link_own[k - 1] = carried
        if k < steps - 1:
            diag_own[k], carried = local(up, [(part, width), ((steps - k) * part, width)],
                                         [inverse_at[k], parent_at[k], VMEM, VMEM],
                                         diag_inverse, parent_panel, lefts[k], carried)
        else:
            diag_own[k] = local(up_last, (part, width), [inverse_at[k], VMEM, VMEM], diag_inverse, lefts[k], carried)

    def total_kernel(src, dst):
        total = src[0]
        for i in range(1, cols_n):
            total = total + src[i]
        for i in range(cols_n):
            dst[i] = total

    every = lax.all_to_all(local(total_kernel, tiles.shape, [VMEM], summed, after=(diag_own[-1],)), COL, 0, 0, tiled=True)

    def finish(src, *refs):
        diag_refs, link_refs, (links, diags) = refs[:steps], refs[steps:count], refs[count:]
        for i in range(z_n):
            for j in range(x_n):
                place = (slice(i * t_rows, (i + 1) * t_rows), slice(j * t_cols, (j + 1) * t_cols))
                for k in range(steps):
                    diags[(k,) + place] = diag_refs[k][place] + src[i * x_n + j, k]
                for k in range(links_n):
                    last = link_refs[k].shape[0] - part
                    links[(k,) + place] = src[i * x_n + j, steps + k] - link_refs[k][last + i * t_rows:last + (i + 1) * t_rows, place[1]]

    links, diags = local(finish, [(links_n, part, width), (steps, part, width)], [VMEM] * (count + 1),
                         every, *diag_own, *link_own)
    return cols, links, diags


def solution(mesh):
    axes = Mesh(mesh.devices.reshape(4, 2, 8, 4), ("y", "core", "z", "x"))
    return jax.shard_map(
        shards,
        mesh=axes,
        in_specs=(P(ROW, COL), P(None, ALL, None), P(), P(), P()),
        out_specs=(P(None, ALL, None), P(None, ROW, None), P(None, ROW, None)),
        check_vma=False,
    )
```

```python
import jax
import jax.numpy as jnp
from jax import lax
from jax.experimental import pallas as pl
from jax.experimental.pallas import tpu as pltpu
from jax.sharding import Mesh, PartitionSpec as P

BLOCK = 128
ROW = ("y", "core")
COL = ("z", "x")
ALL = ROW + COL
F32 = jnp.float32
HIGHEST = lax.Precision.HIGHEST
VMEM = pl.BlockSpec(memory_space=pltpu.VMEM)
SMEM = pl.BlockSpec(memory_space=pltpu.SMEM)
ANY = pl.BlockSpec(memory_space=pl.ANY)
HBM = pl.BlockSpec(memory_space=pltpu.HBM)
MIB = 2**20


def matmul(a, b, dims=((1,), (0,)), precision=HIGHEST):
    return lax.dot_general(a, b, (dims, ((), ())), precision=precision, preferred_element_type=F32)


def local(kernel, out_shapes, specs, *args, after=(), scratch=(), semaphores=0, vmem=4):
    many = isinstance(out_shapes, list)
    shapes = [jax.ShapeDtypeStruct(s, F32) for s in (out_shapes if many else [out_shapes])]
    out = pl.pallas_call(
        lambda *refs: kernel(*refs[:len(args)], *refs[len(args) + len(after):]),
        out_shape=shapes,
        in_specs=list(specs) + [ANY] * len(after),
        out_specs=[VMEM] * len(shapes),
        grid=(1,) if any(spec.block_shape for spec in specs) else (),
        scratch_shapes=[pltpu.VMEM(shape, F32) if isinstance(shape, tuple) else shape for shape in scratch]
        + ([pltpu.SemaphoreType.DMA((semaphores,))] if semaphores else []),
        compiler_params=pltpu.CompilerParams(vmem_limit_bytes=vmem * MIB),
    )(*args, *after)
    return out if many else out[0]


def pack(pieces, after=()):
    def kernel(*refs):
        at = 0
        for ref in refs[:-1]:
            refs[-1][at:at + ref.shape[0]] = ref[...]
            at += ref.shape[0]

    rows = sum(piece.shape[0] for piece in pieces)
    return local(kernel, (rows,) + pieces[0].shape[1:], [VMEM] * len(pieces), *pieces, after=after)


def shift(value, axis, distance):
    n = lax.axis_size(axis)
    return lax.ppermute(value, axis, [(i, (i + distance) % n) for i in range(n)])


def ring(value, axis):
    half = value.shape[0] // 2
    out, up, down = [value], value, value
    for _ in range(lax.axis_size(axis) // 2 - 1):
        up, down = shift(up, axis, 1), shift(down, axis, -1)
        out += [up, down]
    return out + [shift(up[:half], axis, 1), shift(down[half:], axis, -1)]


def ring_sources(axis):
    n, me = lax.axis_size(axis), lax.axis_index(axis)
    offsets = [0]
    for s in range(1, n // 2):
        offsets += [n - s, s]
    return [(me + o) % n for o in offsets + [n // 2]]


def block(k, shape):
    return pl.BlockSpec((None,) + shape[1:], lambda i: (k,) + (0,) * (len(shape) - 1))


def pick(value, index, dim):
    return lax.dynamic_index_in_dim(value, index, dim, False)


def shards(sigma_top, panel, parent_panel, diag_inverse, block_depth):
    rows_n, cols_n = lax.axis_size(ROW), lax.axis_size(COL)
    y_n, z_n, x_n = (lax.axis_size(axis) for axis in ("y", "z", "x"))
    r, c = lax.axis_index(ROW), lax.axis_index(COL)
    y_i, core, x_i = lax.axis_index("y"), lax.axis_index("core"), lax.axis_index("x")
    steps, share, width = panel.shape
    group = sigma_top.shape[1]
    part = width // rows_n
    units = steps * y_n
    z_units = (units * 9 + 8) // 16
    cut = z_units * 2 * part
    mid, off = cut // width, cut % width
    links_n = steps - 1
    own_block = ((r * cols_n + c) * share // BLOCK).reshape(1).astype(jnp.int32)

    group_panel = lax.all_gather(panel, ROW, axis=0)
    group_depth = pick(block_depth.reshape(rows_n, -1), c * share // BLOCK, 1)

    def fetch(copies, arrived):
        copies = [pltpu.make_async_copy(src, dst, arrived.at[i]) for i, (src, dst) in enumerate(copies)]
        for copy in copies:
            copy.start()
        for copy in copies:
            copy.wait()

    def masked(block_ref, depth_ref, value, k):
        return jnp.where(depth_ref[block_ref[0]] > k, 1.0, 0.0).astype(F32) * value

    def head_first(block_ref, depth_hbm, panel_hbm, parent_hbm, out, middle, panel_ref, parent_ref, depth_ref, arrived):
        fetch([(depth_hbm, depth_ref), (panel_hbm.at[:mid + 1], panel_ref), (parent_hbm.at[:mid], parent_ref)], arrived)
        value = None
        for k in range(mid + 1):
            own = masked(block_ref, depth_ref, panel_ref[k], k)
            value = own - matmul(value, parent_ref[k - 1]) if k else own
            columns = min(width, cut - k * width)
            if columns:
                out[:, k * width:k * width + columns] = value[:, :columns]
        middle[...] = value

    def head_second(block_ref, depth_hbm, panel_hbm, parent_hbm, middle, out, panel_ref, parent_ref, depth_ref, arrived):
        fetch([(depth_hbm, depth_ref), (panel_hbm.at[mid + 1:], panel_ref), (parent_hbm.at[mid:], parent_ref)], arrived)
        value = middle[...]
        out[:, :width - off] = value[:, off:]
        for k in range(mid + 1, steps):
            own = masked(block_ref, depth_ref, panel_ref[k - mid - 1], k)
            value = own - matmul(value, parent_ref[k - mid - 1])
            out[:, k * width - cut:(k + 1) * width - cut] = value

    depth_at = pltpu.SMEM(block_depth.shape, jnp.int32)
    heads = [SMEM, HBM, HBM, HBM]
    n_z, middle = local(head_first, [(share, cut), (share, width)], heads, own_block, block_depth, panel, parent_panel,
                        scratch=[(mid + 1, share, width), (mid, width, width), depth_at], semaphores=3)
    n_x = local(head_second, (share, steps * width - cut), heads + [VMEM], own_block, block_depth, panel, parent_panel,
                middle, scratch=[(links_n - mid, share, width), (links_n - mid, width, width), depth_at], semaphores=3)

    by_z = ring(n_z, "z")
    by_x = [n_x, shift(n_x, "x", 1), shift(n_x, "x", -1), shift(n_x, "x", 2)]

    starts = jnp.stack([(zz * x_n + xx) * share for zz in ring_sources("z") for xx in ring_sources("x")])

    def turn(starts_ref, top, z_major, x_major):
        for i in range(z_n):
            for j in range(x_n):
                rows = top[pl.ds(pl.multiple_of(starts_ref[i * x_n + j], share), share), :]
                z_major[i, j * share:(j + 1) * share, :] = rows
                x_major[j, i * share:(i + 1) * share, :] = rows

    z_major, x_major = local(turn, [(z_n, x_n * share, group), (x_n, z_n * share, group)], [SMEM, VMEM],
                             starts.astype(jnp.int32), sigma_top, after=(by_z[1],))

    def product(total, blocks, tops):
        block = blocks[0] if len(blocks) == 1 else jnp.concatenate(blocks, axis=0)
        term = matmul(block, tops.reshape(-1, group), ((0,), (0,)), lax.Precision.HIGH)
        return term if total is None else total + term

    z_sum = x_sum = None
    arrived = ring(pack(by_z), "x")
    for j in range(x_n):
        z_sum = product(z_sum, arrived[j:] if j == x_n - 1 else arrived[j:j + 1], x_major[j:j + 1])
    arrived = ring(pack(by_x, after=(by_z[-1],)), "z")
    x_sum = product(x_sum, arrived[:1], z_major[:1])
    for j in range(1, z_n - 1, 2):
        x_sum = product(x_sum, arrived[j:j + 2], z_major[j:j + 2])
    x_sum = product(x_sum, arrived[z_n - 1:], z_major[z_n - 1:])

    def group_head(depth_ref, panel_ref, parent_ref, out):
        for k in range(steps):
            at = slice(k * width, (k + 1) * width)
            for i in range(rows_n):
                mask = jnp.where(depth_ref[i] > k, 1.0, 0.0).astype(F32)
                out[i * share:(i + 1) * share, at] = mask * panel_ref[i, k]
            if k:
                out[:, at] -= matmul(out[:, (k - 1) * width:k * width], parent_ref[k - 1])

    group_n = local(group_head, (rows_n * share, steps * width), [SMEM, VMEM, VMEM], group_depth, group_panel, parent_panel, vmem=12)

    def split(core_ref, z_ref, x_ref, keep, give):
        for unit in range(units):
            ref, at = (z_ref, unit) if unit < z_units else (x_ref, unit - z_units)
            keep[unit // y_n, unit % y_n] = ref[at, core_ref[0]]
            give[unit // y_n, unit % y_n] = ref[at, 1 - core_ref[0]]

    keep, give = local(split, [(steps, y_n, part, group)] * 2, [SMEM, VMEM, VMEM], core.reshape(1).astype(jnp.int32),
                       z_sum.reshape(z_units, 2, part, group), x_sum.reshape(units - z_units, 2, part, group), vmem=6)
    got = shift(give, "core", 1)

    def by_y(y_ref, keep_ref, got_ref, *outs):
        for d in range(y_n):
            i = lax.rem(y_ref[0] + d, y_n)
            for k in range(steps):
                outs[d][k] = keep_ref[k, i] + got_ref[k, i]

    summands = list(local(by_y, [(steps, part, group)] * y_n, [SMEM, VMEM, VMEM], y_i.reshape(1).astype(jnp.int32),
                          keep, got, vmem=6))
    for d in range(1, y_n):
        summands[d] = shift(summands[d], "y", d)

    per = rows_n // x_n

    def over_x(x_ref, *refs):
        parts, outs, held = refs[:y_n], refs[y_n:-1], refs[-1]
        total = sum((p[...] for p in parts[1:]), parts[0][...]).reshape(steps * part, group)
        held[...] = total.T.reshape(rows_n, share, steps * part)
        for d in range(x_n):
            for i in range(per):
                outs[d][i] = held[i * x_n + lax.rem(x_ref[0] + d, x_n)]

    def over_z(x_ref, *refs):
        for d in range(x_n):
            for i in range(per):
                refs[-1][lax.rem(x_ref[0] + x_n - d, x_n) * per + i] = refs[d][i]

    x_at = x_i.reshape(1).astype(jnp.int32)
    y_rows = list(local(over_x, [(per, share, steps * part)] * x_n, [SMEM] + [VMEM] * y_n, x_at, *summands,
                        after=(group_n,), scratch=[(rows_n, share, steps * part)]))
    for d in range(1, x_n):
        y_rows[d] = shift(y_rows[d], "x", d)
    y_rows = local(over_z, (z_n, share, steps * part), [SMEM] + [VMEM] * x_n, x_at, *y_rows)
    y_rows = lax.all_to_all(y_rows, "z", 0, 0, tiled=True)

    count = steps + links_n
    t_rows, t_cols = part // z_n, width // x_n

    def gram(x_ref, y_ref, n_ref, *refs):
        outs, (turned, held) = refs[:x_n], refs[x_n:]
        turned[...] = y_ref[...].reshape(rows_n * share, steps * part).T

        def put(which, value):
            for j in range(x_n):
                held[j, which] = value[:, j * t_cols:(j + 1) * t_cols]

        for k in range(steps):
            low = max(k - 1, 0)
            value = matmul(turned[low * part:(k + 1) * part, :], n_ref[:, k * width:(k + 1) * width])
            put(k, value[(k - low) * part:])
            if k:
                put(steps + k - 1, value[:part])
        for d in range(x_n):
            outs[d][...] = held[lax.rem(x_ref[0] + d, x_n)]

    grams = list(local(gram, [(count, part, t_cols)] * x_n, [SMEM] + [VMEM] * 2, x_at, y_rows, group_n, vmem=10,
                       scratch=[(steps * part, rows_n * share), (x_n, count, part, t_cols)]))
    tiles = grams[0]
    for d in range(1, x_n):
        grams[d] = shift(grams[d], "x", d)

    def sum_x(*refs):
        total = sum((ref[...] for ref in refs[1:-1]), refs[0][...])
        for i in range(z_n):
            refs[-1][i] = total[:, i * t_rows:(i + 1) * t_rows]

    summed = local(sum_x, (z_n, count, t_rows, t_cols), [VMEM] * x_n, *grams)
    summed = lax.all_to_all(summed, "z", 0, 0, tiled=True)

    home = y_rows.reshape(y_n, 2, share, steps * part)
    home = jnp.stack([pick(home, core, 1), shift(pick(home, 1 - core, 1), "core", 1)], axis=1)
    home = [pick(home, (y_i + d) % y_n, 0) for d in range(y_n)]
    home = [home[0]] + [shift(home[d], "y", d) for d in range(1, y_n)]

    def finish_cols(place_ref, block_ref, depth_ref, *refs):
        dst, held = refs[y_n:]
        for d in range(y_n):
            y_from = lax.rem(place_ref[0] + y_n - d, y_n)
            held[y_from * 2 + place_ref[1]] = refs[d][0]
            held[y_from * 2 + 1 - place_ref[1]] = refs[d][1]
        for i in range(rows_n):
            for k in range(steps):
                sign = jnp.where(depth_ref[block_ref[0]] > k, -1.0, 0.0).astype(F32)
                dst[k, :, i * part:(i + 1) * part] = sign * held[i, :, k * part:(k + 1) * part]

    cols = local(finish_cols, (steps, share, width), [SMEM] * 3 + [VMEM] * y_n,
                 jnp.stack([y_i, core]).astype(jnp.int32), own_block, block_depth, *home, scratch=[(rows_n, share, steps * part)])

    def unit_rows(first_ref):
        at = lax.broadcasted_iota(jnp.int32, (part, width), 0) + first_ref[0]
        return (lax.broadcasted_iota(jnp.int32, (part, width), 1) == at).astype(F32)

    def down_first(first_ref, inverse_ref, parent_ref, left, rows):
        unit = unit_rows(first_ref)
        left[...] = matmul(unit, inverse_ref[...], ((1,), (1,)))
        rows[:part] = matmul(unit, parent_ref[...], ((1,), (1,)))
        rows[part:] = unit

    def down(first_ref, inverse_ref, parent_ref, above, left, rows):
        left[...] = matmul(above[...], inverse_ref[...], ((1,), (1,)))
        rows[:-part] = matmul(above[...], parent_ref[...], ((1,), (1,)))
        rows[-part:] = unit_rows(first_ref)

    def bottom(inverse_ref, parent_ref, above, own, carried):
        value = matmul(matmul(above[...], inverse_ref[...], ((1,), (1,))), inverse_ref[...])
        own[...] = value[-part:]
        carried[...] = matmul(value, parent_ref[...])

    def up(inverse_ref, parent_ref, left, below, own, carried):
        value = matmul(left[...], inverse_ref[...]) + below[:-part]
        own[...] = value[-part:]
        carried[...] = matmul(value, parent_ref[...])

    def up_last(inverse_ref, left, below, own):
        own[...] = matmul(left[...], inverse_ref[...]) + below[:-part]

    parent_at = [block(k, parent_panel.shape) for k in range(links_n)]
    inverse_at = [block(k, diag_inverse.shape) for k in range(steps)]
    first = (r * part).reshape(1).astype(jnp.int32)
    lefts, rows = [None] * steps, None
    for k in range(steps - 1, 0, -1):
        above = [] if rows is None else [rows]
        tall = (steps - k) * part
        lefts[k], rows = local(down if above else down_first, [(tall, width), (tall + part, width)],
                               [SMEM, inverse_at[k], parent_at[k - 1]] + [VMEM] * len(above),
                               first, diag_inverse, parent_panel, *above, after=() if above else (tiles,))
    diag_own, link_own = [None] * steps, [None] * links_n
    diag_own[0], carried = local(bottom, [(part, width), (steps * part, width)], [inverse_at[0], parent_at[0], VMEM],
                                 diag_inverse, parent_panel, rows)
    for k in range(1, steps):
        link_own[k - 1] = carried
        if k < steps - 1:
            diag_own[k], carried = local(up, [(part, width), ((steps - k) * part, width)],
                                         [inverse_at[k], parent_at[k], VMEM, VMEM],
                                         diag_inverse, parent_panel, lefts[k], carried)
        else:
            diag_own[k] = local(up_last, (part, width), [inverse_at[k], VMEM, VMEM], diag_inverse, lefts[k], carried)

    def sum_z(src, dst):
        total = sum((src[i] for i in range(1, z_n)), src[0])
        for i in range(z_n):
            dst[i] = total

    every = lax.all_to_all(local(sum_z, summed.shape, [VMEM], summed, after=(diag_own[-1],)), "z", 0, 0, tiled=True)
    every = [every] + [shift(every, "x", d) for d in range(1, x_n)]

    def finish(x_ref, *refs):
        srcs, refs = refs[:x_n], refs[x_n:]
        diag_refs, link_refs, (links, diags, held) = refs[:steps], refs[steps:count], refs[count:]
        for d in range(x_n):
            held[lax.rem(x_ref[0] + x_n - d, x_n)] = srcs[d][...]
        for i in range(z_n):
            for j in range(x_n):
                place = (slice(i * t_rows, (i + 1) * t_rows), slice(j * t_cols, (j + 1) * t_cols))
                for k in range(steps):
                    diags[(k,) + place] = diag_refs[k][place] + held[j, i, k]
                for k in range(links_n):
                    last = link_refs[k].shape[0] - part
                    links[(k,) + place] = held[j, i, steps + k] - link_refs[k][last + i * t_rows:last + (i + 1) * t_rows, place[1]]

    links, diags = local(finish, [(links_n, part, width), (steps, part, width)], [SMEM] + [VMEM] * (x_n + count),
                         x_at, *every, *diag_own, *link_own, vmem=10, scratch=[(x_n, z_n, count, t_rows, t_cols)])
    return cols, links, diags


def solution(mesh):
    axes = Mesh(mesh.devices.reshape(4, 2, 8, 4), ("y", "core", "z", "x"))
    return jax.shard_map(
        shards,
        mesh=axes,
        in_specs=(P(ROW, COL), P(None, ALL, None), P(), P(), P()),
        out_specs=(P(None, ALL, None), P(None, ROW, None), P(None, ROW, None)),
        check_vma=False,
    )
```

```python
import jax
import jax.numpy as jnp
from jax import lax
from jax.experimental import pallas as pl
from jax.experimental.pallas import tpu as pltpu
from jax.sharding import Mesh, PartitionSpec as P

BLOCK = 128
ROW = ("y", "core")
COL = ("z", "x")
ALL = ROW + COL
F32 = jnp.float32
HIGHEST = lax.Precision.HIGHEST
VMEM = pl.BlockSpec(memory_space=pltpu.VMEM)
SMEM = pl.BlockSpec(memory_space=pltpu.SMEM)
ANY = pl.BlockSpec(memory_space=pl.ANY)
HBM = pl.BlockSpec(memory_space=pltpu.HBM)
MIB = 2**20


def matmul(a, b, dims=((1,), (0,)), precision=HIGHEST):
    return lax.dot_general(a, b, (dims, ((), ())), precision=precision, preferred_element_type=F32)


def local(kernel, out_shapes, specs, *args, after=(), scratch=(), semaphores=0, vmem=4):
    many = isinstance(out_shapes, list)
    shapes = [jax.ShapeDtypeStruct(s, F32) for s in (out_shapes if many else [out_shapes])]
    out = pl.pallas_call(
        lambda *refs: kernel(*refs[:len(args)], *refs[len(args) + len(after):]),
        out_shape=shapes,
        in_specs=list(specs) + [ANY] * len(after),
        out_specs=[VMEM] * len(shapes),
        grid=(1,) if any(spec.block_shape for spec in specs) else (),
        scratch_shapes=[pltpu.VMEM(shape, F32) if isinstance(shape, tuple) else shape for shape in scratch]
        + ([pltpu.SemaphoreType.DMA((semaphores,))] if semaphores else []),
        compiler_params=pltpu.CompilerParams(vmem_limit_bytes=vmem * MIB),
    )(*args, *after)
    return out if many else out[0]


def pack(pieces, after=()):
    def kernel(*refs):
        at = 0
        for ref in refs[:-1]:
            refs[-1][at:at + ref.shape[0]] = ref[...]
            at += ref.shape[0]

    rows = sum(piece.shape[0] for piece in pieces)
    return local(kernel, (rows,) + pieces[0].shape[1:], [VMEM] * len(pieces), *pieces, after=after)


def shift(value, axis, distance):
    n = lax.axis_size(axis)
    return lax.ppermute(value, axis, [(i, (i + distance) % n) for i in range(n)])


def ring(value, axis):
    half = value.shape[0] // 2
    out, up, down = [value], value, value
    for _ in range(lax.axis_size(axis) // 2 - 1):
        up, down = shift(up, axis, 1), shift(down, axis, -1)
        out += [up, down]
    return out + [shift(up[:half], axis, 1), shift(down[half:], axis, -1)]


def ring_sources(axis):
    n, me = lax.axis_size(axis), lax.axis_index(axis)
    offsets = [0]
    for s in range(1, n // 2):
        offsets += [n - s, s]
    return [(me + o) % n for o in offsets + [n // 2]]


def block(k, shape):
    return pl.BlockSpec((None,) + shape[1:], lambda i: (k,) + (0,) * (len(shape) - 1))


def pick(value, index, dim):
    return lax.dynamic_index_in_dim(value, index, dim, False)


def shards(sigma_top, panel, parent_panel, diag_inverse, block_depth):
    rows_n, cols_n = lax.axis_size(ROW), lax.axis_size(COL)
    y_n, z_n, x_n = (lax.axis_size(axis) for axis in ("y", "z", "x"))
    r, c = lax.axis_index(ROW), lax.axis_index(COL)
    y_i, core, x_i = lax.axis_index("y"), lax.axis_index("core"), lax.axis_index("x")
    steps, share, width = panel.shape
    group = sigma_top.shape[1]
    part = width // rows_n
    units = steps * y_n
    z_units = (units * 9 + 8) // 16
    cut = z_units * 2 * part
    mid, off = cut // width, cut % width
    links_n = steps - 1
    own_block = ((r * cols_n + c) * share // BLOCK).reshape(1).astype(jnp.int32)

    group_panel = lax.all_gather(panel, ROW, axis=0)
    group_depth = pick(block_depth.reshape(rows_n, -1), c * share // BLOCK, 1)

    def fetch(copies, arrived):
        copies = [pltpu.make_async_copy(src, dst, arrived.at[i]) for i, (src, dst) in enumerate(copies)]
        for copy in copies:
            copy.start()
        for copy in copies:
            copy.wait()

    def masked(block_ref, depth_ref, value, k):
        return jnp.where(depth_ref[block_ref[0]] > k, 1.0, 0.0).astype(F32) * value

    def head_first(block_ref, depth_hbm, panel_hbm, parent_hbm, out, middle, panel_ref, parent_ref, depth_ref, arrived):
        fetch([(depth_hbm, depth_ref), (panel_hbm.at[:mid + 1], panel_ref), (parent_hbm.at[:mid], parent_ref)], arrived)
        value = None
        for k in range(mid + 1):
            own = masked(block_ref, depth_ref, panel_ref[k], k)
            value = own - matmul(value, parent_ref[k - 1]) if k else own
            columns = min(width, cut - k * width)
            if columns:
                out[:, k * width:k * width + columns] = value[:, :columns]
        middle[...] = value

    def head_second(block_ref, depth_hbm, panel_hbm, parent_hbm, middle, out, panel_ref, parent_ref, depth_ref, arrived):
        fetch([(depth_hbm, depth_ref), (panel_hbm.at[mid + 1:], panel_ref), (parent_hbm.at[mid:], parent_ref)], arrived)
        value = middle[...]
        out[:, :width - off] = value[:, off:]
        for k in range(mid + 1, steps):
            own = masked(block_ref, depth_ref, panel_ref[k - mid - 1], k)
            value = own - matmul(value, parent_ref[k - mid - 1])
            out[:, k * width - cut:(k + 1) * width - cut] = value

    depth_at = pltpu.SMEM(block_depth.shape, jnp.int32)
    heads = [SMEM, HBM, HBM, HBM]
    n_z, middle = local(head_first, [(share, cut), (share, width)], heads, own_block, block_depth, panel, parent_panel,
                        scratch=[(mid + 1, share, width), (mid, width, width), depth_at], semaphores=3)
    n_x = local(head_second, (share, steps * width - cut), heads + [VMEM], own_block, block_depth, panel, parent_panel,
                middle, scratch=[(links_n - mid, share, width), (links_n - mid, width, width), depth_at], semaphores=3)

    by_z = ring(n_z, "z")
    by_x = [n_x, shift(n_x, "x", 1), shift(n_x, "x", -1), shift(n_x, "x", 2)]

    starts = jnp.stack([(zz * x_n + xx) * share for zz in ring_sources("z") for xx in ring_sources("x")])

    def turn(starts_ref, top, z_major, x_major):
        for i in range(z_n):
            for j in range(x_n):
                rows = top[pl.ds(pl.multiple_of(starts_ref[i * x_n + j], share), share), :]
                z_major[i, j * share:(j + 1) * share, :] = rows
                x_major[j, i * share:(i + 1) * share, :] = rows

    z_major, x_major = local(turn, [(z_n, x_n * share, group), (x_n, z_n * share, group)], [SMEM, VMEM],
                             starts.astype(jnp.int32), sigma_top, after=(by_z[1], group_panel))

    def product(total, blocks, tops):
        block = blocks[0] if len(blocks) == 1 else jnp.concatenate(blocks, axis=0)
        term = matmul(block, tops.reshape(-1, group), ((0,), (0,)), lax.Precision.HIGH)
        return term if total is None else total + term

    z_sum = x_sum = None
    arrived = ring(pack(by_z), "x")
    for j in range(x_n):
        z_sum = product(z_sum, arrived[j:] if j == x_n - 1 else arrived[j:j + 1], x_major[j:j + 1])
    arrived = ring(pack(by_x, after=(by_z[-1],)), "z")
    x_sum = product(x_sum, arrived[:1], z_major[:1])
    for j in range(1, z_n - 1, 2):
        x_sum = product(x_sum, arrived[j:j + 2], z_major[j:j + 2])
    x_sum = product(x_sum, arrived[z_n - 1:], z_major[z_n - 1:])

    def group_head(depth_ref, panel_ref, parent_ref, out):
        for k in range(steps):
            at = slice(k * width, (k + 1) * width)
            for i in range(rows_n):
                mask = jnp.where(depth_ref[i] > k, 1.0, 0.0).astype(F32)
                out[i * share:(i + 1) * share, at] = mask * panel_ref[i, k]
            if k:
                out[:, at] -= matmul(out[:, (k - 1) * width:k * width], parent_ref[k - 1])

    group_n = local(group_head, (rows_n * share, steps * width), [SMEM, VMEM, VMEM], group_depth, group_panel, parent_panel, vmem=12)

    def split(core_ref, z_ref, x_ref, keep, give):
        for unit in range(units):
            ref, at = (z_ref, unit) if unit < z_units else (x_ref, unit - z_units)
            keep[unit // y_n, unit % y_n] = ref[at, core_ref[0]]
            give[unit // y_n, unit % y_n] = ref[at, 1 - core_ref[0]]

    keep, give = local(split, [(steps, y_n, part, group)] * 2, [SMEM, VMEM, VMEM], core.reshape(1).astype(jnp.int32),
                       z_sum.reshape(z_units, 2, part, group), x_sum.reshape(units - z_units, 2, part, group), vmem=6)
    got = shift(give, "core", 1)

    def by_y(y_ref, keep_ref, got_ref, *outs):
        for d in range(y_n):
            i = lax.rem(y_ref[0] + d, y_n)
            for k in range(steps):
                outs[d][k] = keep_ref[k, i] + got_ref[k, i]

    summands = list(local(by_y, [(steps, part, group)] * y_n, [SMEM, VMEM, VMEM], y_i.reshape(1).astype(jnp.int32),
                          keep, got, vmem=6))
    for d in range(1, y_n):
        summands[d] = shift(summands[d], "y", d)

    per = rows_n // x_n

    def over_x(x_ref, *refs):
        parts, outs, held = refs[:y_n], refs[y_n:-1], refs[-1]
        total = sum((p[...] for p in parts[1:]), parts[0][...]).reshape(steps * part, group)
        held[...] = total.T.reshape(rows_n, share, steps * part)
        for d in range(x_n):
            for i in range(per):
                outs[d][i] = held[i * x_n + lax.rem(x_ref[0] + d, x_n)]

    def over_z(x_ref, *refs):
        for d in range(x_n):
            for i in range(per):
                refs[-1][lax.rem(x_ref[0] + x_n - d, x_n) * per + i] = refs[d][i]

    x_at = x_i.reshape(1).astype(jnp.int32)
    y_rows = list(local(over_x, [(per, share, steps * part)] * x_n, [SMEM] + [VMEM] * y_n, x_at, *summands,
                        after=(group_n,), scratch=[(rows_n, share, steps * part)]))
    for d in range(1, x_n):
        y_rows[d] = shift(y_rows[d], "x", d)
    sent = local(over_z, (z_n, share, steps * part), [SMEM] + [VMEM] * x_n, x_at, *y_rows)
    y_rows = lax.all_to_all(sent, "z", 0, 0, tiled=True)

    def unit_rows(first_ref):
        at = lax.broadcasted_iota(jnp.int32, (part, width), 0) + first_ref[0]
        return (lax.broadcasted_iota(jnp.int32, (part, width), 1) == at).astype(F32)

    def down_first(first_ref, inverse_ref, parent_ref, left, rows):
        unit = unit_rows(first_ref)
        left[...] = matmul(unit, inverse_ref[...], ((1,), (1,)))
        rows[:part] = matmul(unit, parent_ref[...], ((1,), (1,)))
        rows[part:] = unit

    def down(first_ref, inverse_ref, parent_ref, above, left, rows):
        left[...] = matmul(above[...], inverse_ref[...], ((1,), (1,)))
        rows[:-part] = matmul(above[...], parent_ref[...], ((1,), (1,)))
        rows[-part:] = unit_rows(first_ref)

    def bottom(inverse_ref, parent_ref, above, own, carried):
        value = matmul(matmul(above[...], inverse_ref[...], ((1,), (1,))), inverse_ref[...])
        own[...] = value[-part:]
        carried[...] = matmul(value, parent_ref[...])

    def up(inverse_ref, parent_ref, left, below, own, carried):
        value = matmul(left[...], inverse_ref[...]) + below[:-part]
        own[...] = value[-part:]
        carried[...] = matmul(value, parent_ref[...])

    def up_last(inverse_ref, left, below, own):
        own[...] = matmul(left[...], inverse_ref[...]) + below[:-part]

    parent_at = [block(k, parent_panel.shape) for k in range(links_n)]
    inverse_at = [block(k, diag_inverse.shape) for k in range(steps)]
    first = (r * part).reshape(1).astype(jnp.int32)
    lefts, rows = [None] * steps, None
    for k in range(steps - 1, 0, -1):
        above = [] if rows is None else [rows]
        tall = (steps - k) * part
        lefts[k], rows = local(down if above else down_first, [(tall, width), (tall + part, width)],
                               [SMEM, inverse_at[k], parent_at[k - 1]] + [VMEM] * len(above),
                               first, diag_inverse, parent_panel, *above, after=() if above else (sent,))
    count = steps + links_n
    t_rows, t_cols = part // z_n, width // x_n

    def gram(x_ref, y_ref, n_ref, *refs):
        outs, (turned, held) = refs[:x_n], refs[x_n:]
        turned[...] = y_ref[...].reshape(rows_n * share, steps * part).T

        def put(which, value):
            for j in range(x_n):
                held[j, which] = value[:, j * t_cols:(j + 1) * t_cols]

        for k in range(steps):
            low = max(k - 1, 0)
            value = matmul(turned[low * part:(k + 1) * part, :], n_ref[:, k * width:(k + 1) * width])
            put(k, value[(k - low) * part:])
            if k:
                put(steps + k - 1, value[:part])
        for d in range(x_n):
            outs[d][...] = held[lax.rem(x_ref[0] + d, x_n)]

    grams = list(local(gram, [(count, part, t_cols)] * x_n, [SMEM] + [VMEM] * 2, x_at, y_rows, group_n, after=(rows,), vmem=10,
                       scratch=[(steps * part, rows_n * share), (x_n, count, part, t_cols)]))
    for d in range(1, x_n):
        grams[d] = shift(grams[d], "x", d)

    diag_own, link_own = [None] * steps, [None] * links_n
    diag_own[0], carried = local(bottom, [(part, width), (steps * part, width)], [inverse_at[0], parent_at[0], VMEM],
                                 diag_inverse, parent_panel, rows, after=(grams[0],))
    for k in range(1, steps):
        link_own[k - 1] = carried
        if k < steps - 1:
            diag_own[k], carried = local(up, [(part, width), ((steps - k) * part, width)],
                                         [inverse_at[k], parent_at[k], VMEM, VMEM],
                                         diag_inverse, parent_panel, lefts[k], carried)
        else:
            diag_own[k] = local(up_last, (part, width), [inverse_at[k], VMEM, VMEM], diag_inverse, lefts[k], carried)

    def sum_x(*refs):
        total = sum((ref[...] for ref in refs[1:-1]), refs[0][...])
        for i in range(z_n):
            refs[-1][i] = total[:, i * t_rows:(i + 1) * t_rows]

    summed = local(sum_x, (z_n, count, t_rows, t_cols), [VMEM] * x_n, *grams, after=(diag_own[-1],))
    summed = lax.all_to_all(summed, "z", 0, 0, tiled=True)

    home = y_rows.reshape(y_n, 2, share, steps * part)
    home = jnp.stack([pick(home, core, 1), shift(pick(home, 1 - core, 1), "core", 1)], axis=1)
    home = [pick(home, (y_i + d) % y_n, 0) for d in range(y_n)]
    home = [home[0]] + [shift(home[d], "y", d) for d in range(1, y_n)]

    def finish_cols(place_ref, block_ref, depth_ref, *refs):
        dst, held = refs[y_n:]
        for d in range(y_n):
            y_from = lax.rem(place_ref[0] + y_n - d, y_n)
            held[y_from * 2 + place_ref[1]] = refs[d][0]
            held[y_from * 2 + 1 - place_ref[1]] = refs[d][1]
        for i in range(rows_n):
            for k in range(steps):
                sign = jnp.where(depth_ref[block_ref[0]] > k, -1.0, 0.0).astype(F32)
                dst[k, :, i * part:(i + 1) * part] = sign * held[i, :, k * part:(k + 1) * part]

    cols = local(finish_cols, (steps, share, width), [SMEM] * 3 + [VMEM] * y_n,
                 jnp.stack([y_i, core]).astype(jnp.int32), own_block, block_depth, *home, scratch=[(rows_n, share, steps * part)])

    def sum_z(src, dst):
        total = sum((src[i] for i in range(1, z_n)), src[0])
        for i in range(z_n):
            dst[i] = total

    every = lax.all_to_all(local(sum_z, summed.shape, [VMEM], summed, after=tuple(home)), "z", 0, 0, tiled=True)
    every = [every] + [shift(every, "x", d) for d in range(1, x_n)]

    def finish(x_ref, *refs):
        srcs, refs = refs[:x_n], refs[x_n:]
        diag_refs, link_refs, (links, diags, held) = refs[:steps], refs[steps:count], refs[count:]
        for d in range(x_n):
            held[lax.rem(x_ref[0] + x_n - d, x_n)] = srcs[d][...]
        for i in range(z_n):
            for j in range(x_n):
                place = (slice(i * t_rows, (i + 1) * t_rows), slice(j * t_cols, (j + 1) * t_cols))
                for k in range(steps):
                    diags[(k,) + place] = diag_refs[k][place] + held[j, i, k]
                for k in range(links_n):
                    last = link_refs[k].shape[0] - part
                    links[(k,) + place] = held[j, i, steps + k] - link_refs[k][last + i * t_rows:last + (i + 1) * t_rows, place[1]]

    links, diags = local(finish, [(links_n, part, width), (steps, part, width)], [SMEM] + [VMEM] * (x_n + count),
                         x_at, *every, *diag_own, *link_own, vmem=10, scratch=[(x_n, z_n, count, t_rows, t_cols)])
    return cols, links, diags


def solution(mesh):
    axes = Mesh(mesh.devices.reshape(4, 2, 8, 4), ("y", "core", "z", "x"))
    return jax.shard_map(
        shards,
        mesh=axes,
        in_specs=(P(ROW, COL), P(None, ALL, None), P(), P(), P()),
        out_specs=(P(None, ALL, None), P(None, ROW, None), P(None, ROW, None)),
        check_vma=False,
    )
```

```python
import jax
import jax.numpy as jnp
from jax import lax
from jax.experimental import pallas as pl
from jax.experimental.pallas import tpu as pltpu
from jax.sharding import Mesh, PartitionSpec as P

BLOCK = 128
ROW = ("y", "core")
COL = ("z", "x")
ALL = ROW + COL
F32 = jnp.float32
HIGHEST = lax.Precision.HIGHEST
VMEM = pl.BlockSpec(memory_space=pltpu.VMEM)
SMEM = pl.BlockSpec(memory_space=pltpu.SMEM)
ANY = pl.BlockSpec(memory_space=pl.ANY)
HBM = pl.BlockSpec(memory_space=pltpu.HBM)
MIB = 2**20


def matmul(a, b, dims=((1,), (0,)), precision=HIGHEST):
    return lax.dot_general(a, b, (dims, ((), ())), precision=precision, preferred_element_type=F32)


def local(kernel, out_shapes, specs, *args, after=(), scratch=(), semaphores=0, vmem=4):
    many = isinstance(out_shapes, list)
    shapes = [jax.ShapeDtypeStruct(s, F32) for s in (out_shapes if many else [out_shapes])]
    out = pl.pallas_call(
        lambda *refs: kernel(*refs[:len(args)], *refs[len(args) + len(after):]),
        out_shape=shapes,
        in_specs=list(specs) + [ANY] * len(after),
        out_specs=[VMEM] * len(shapes),
        grid=(1,) if any(spec.block_shape for spec in specs) else (),
        scratch_shapes=[pltpu.VMEM(shape, F32) if isinstance(shape, tuple) else shape for shape in scratch]
        + ([pltpu.SemaphoreType.DMA((semaphores,))] if semaphores else []),
        compiler_params=pltpu.CompilerParams(vmem_limit_bytes=vmem * MIB),
    )(*args, *after)
    return out if many else out[0]


def pack(pieces, after=()):
    def kernel(*refs):
        at = 0
        for ref in refs[:-1]:
            refs[-1][at:at + ref.shape[0]] = ref[...]
            at += ref.shape[0]

    rows = sum(piece.shape[0] for piece in pieces)
    return local(kernel, (rows,) + pieces[0].shape[1:], [VMEM] * len(pieces), *pieces, after=after)


def shift(value, axis, distance):
    n = lax.axis_size(axis)
    return lax.ppermute(value, axis, [(i, (i + distance) % n) for i in range(n)])


def ring(value, axis):
    half = value.shape[0] // 2
    out, up, down = [value], value, value
    for _ in range(lax.axis_size(axis) // 2 - 1):
        up, down = shift(up, axis, 1), shift(down, axis, -1)
        out += [up, down]
    return out + [shift(up[:half], axis, 1), shift(down[half:], axis, -1)]


def ring_sources(axis):
    n, me = lax.axis_size(axis), lax.axis_index(axis)
    offsets = [0]
    for s in range(1, n // 2):
        offsets += [n - s, s]
    return [(me + o) % n for o in offsets + [n // 2]]


def block(k, shape):
    return pl.BlockSpec((None,) + shape[1:], lambda i: (k,) + (0,) * (len(shape) - 1))


def pick(value, index, dim):
    return lax.dynamic_index_in_dim(value, index, dim, False)


def shards(sigma_top, panel, parent_panel, diag_inverse, block_depth):
    rows_n, cols_n = lax.axis_size(ROW), lax.axis_size(COL)
    y_n, z_n, x_n = (lax.axis_size(axis) for axis in ("y", "z", "x"))
    r, c = lax.axis_index(ROW), lax.axis_index(COL)
    y_i, core, x_i = lax.axis_index("y"), lax.axis_index("core"), lax.axis_index("x")
    steps, share, width = panel.shape
    group = sigma_top.shape[1]
    part = width // rows_n
    units = steps * y_n
    z_units = (units * 9 + 8) // 16
    cut = z_units * 2 * part
    mid, off = cut // width, cut % width
    links_n = steps - 1
    own_block = ((r * cols_n + c) * share // BLOCK).reshape(1).astype(jnp.int32)

    group_panel = lax.all_gather(panel, ROW, axis=0)
    group_depth = pick(block_depth.reshape(rows_n, -1), c * share // BLOCK, 1)

    def fetch(copies, arrived):
        copies = [pltpu.make_async_copy(src, dst, arrived.at[i]) for i, (src, dst) in enumerate(copies)]
        for copy in copies:
            copy.start()
        for copy in copies:
            copy.wait()

    def masked(block_ref, depth_ref, value, k):
        return jnp.where(depth_ref[block_ref[0]] > k, 1.0, 0.0).astype(F32) * value

    def head_first(block_ref, depth_hbm, panel_hbm, parent_hbm, out, middle, panel_ref, parent_ref, depth_ref, arrived):
        fetch([(depth_hbm, depth_ref), (panel_hbm.at[:mid + 1], panel_ref), (parent_hbm.at[:mid], parent_ref)], arrived)
        value = None
        for k in range(mid + 1):
            own = masked(block_ref, depth_ref, panel_ref[k], k)
            value = own - matmul(value, parent_ref[k - 1]) if k else own
            columns = min(width, cut - k * width)
            if columns:
                out[:, k * width:k * width + columns] = value[:, :columns]
        middle[...] = value

    def head_second(block_ref, depth_hbm, panel_hbm, parent_hbm, middle, out, panel_ref, parent_ref, depth_ref, arrived):
        fetch([(depth_hbm, depth_ref), (panel_hbm.at[mid + 1:], panel_ref), (parent_hbm.at[mid:], parent_ref)], arrived)
        value = middle[...]
        out[:, :width - off] = value[:, off:]
        for k in range(mid + 1, steps):
            own = masked(block_ref, depth_ref, panel_ref[k - mid - 1], k)
            value = own - matmul(value, parent_ref[k - mid - 1])
            out[:, k * width - cut:(k + 1) * width - cut] = value

    depth_at = pltpu.SMEM(block_depth.shape, jnp.int32)
    heads = [SMEM, HBM, HBM, HBM]
    far = [pltpu.with_memory_space_constraint(a, pltpu.HBM) for a in (block_depth, panel, parent_panel)]
    n_z, middle = local(head_first, [(share, cut), (share, width)], heads, own_block, *far,
                        scratch=[(mid + 1, share, width), (mid, width, width), depth_at], semaphores=3)
    n_x = local(head_second, (share, steps * width - cut), heads + [VMEM], own_block, *far,
                middle, scratch=[(links_n - mid, share, width), (links_n - mid, width, width), depth_at], semaphores=3)

    by_z = ring(n_z, "z")
    by_x = ring(n_x, "x")

    starts = jnp.stack([(zz * x_n + xx) * share for zz in ring_sources("z") for xx in ring_sources("x")])

    def turn(starts_ref, top, z_major, x_major):
        for i in range(z_n):
            for j in range(x_n):
                rows = top[pl.ds(pl.multiple_of(starts_ref[i * x_n + j], share), share), :]
                z_major[i, j * share:(j + 1) * share, :] = rows
                x_major[j, i * share:(i + 1) * share, :] = rows

    z_major, x_major = local(turn, [(z_n, x_n * share, group), (x_n, z_n * share, group)], [SMEM, VMEM],
                             starts.astype(jnp.int32), sigma_top, after=(by_z[1],))

    def product(total, blocks, tops):
        block = blocks[0] if len(blocks) == 1 else jnp.concatenate(blocks, axis=0)
        term = matmul(block, tops.reshape(-1, group), ((0,), (0,)), lax.Precision.HIGH)
        return term if total is None else total + term

    z_sum = x_sum = None
    arrived = ring(pack(by_z), "x")
    for j in range(x_n):
        z_sum = product(z_sum, arrived[j:] if j == x_n - 1 else arrived[j:j + 1], x_major[j:j + 1])
    arrived = ring(pack(by_x, after=(by_z[-1],)), "z")
    x_sum = product(x_sum, arrived[:1], z_major[:1])
    for j in range(1, z_n - 1, 2):
        x_sum = product(x_sum, arrived[j:j + 2], z_major[j:j + 2])
    x_sum = product(x_sum, arrived[z_n - 1:], z_major[z_n - 1:])

    def group_head(depth_ref, panel_ref, parent_ref, out):
        for k in range(steps):
            at = slice(k * width, (k + 1) * width)
            for i in range(rows_n):
                mask = jnp.where(depth_ref[i] > k, 1.0, 0.0).astype(F32)
                out[i * share:(i + 1) * share, at] = mask * panel_ref[i, k]
            if k:
                out[:, at] -= matmul(out[:, (k - 1) * width:k * width], parent_ref[k - 1])

    group_n = local(group_head, (rows_n * share, steps * width), [SMEM, VMEM, VMEM], group_depth, group_panel, parent_panel, vmem=12)

    def split(core_ref, z_ref, x_ref, keep, give):
        for unit in range(units):
            ref, at = (z_ref, unit) if unit < z_units else (x_ref, unit - z_units)
            keep[unit // y_n, unit % y_n] = ref[at, core_ref[0]]
            give[unit // y_n, unit % y_n] = ref[at, 1 - core_ref[0]]

    keep, give = local(split, [(steps, y_n, part, group)] * 2, [SMEM, VMEM, VMEM], core.reshape(1).astype(jnp.int32),
                       z_sum.reshape(z_units, 2, part, group), x_sum.reshape(units - z_units, 2, part, group), vmem=6)
    got = shift(give, "core", 1)

    def by_y(y_ref, keep_ref, got_ref, *outs):
        for d in range(y_n):
            i = lax.rem(y_ref[0] + d, y_n)
            for k in range(steps):
                outs[d][k] = keep_ref[k, i] + got_ref[k, i]

    summands = list(local(by_y, [(steps, part, group)] * y_n, [SMEM, VMEM, VMEM], y_i.reshape(1).astype(jnp.int32),
                          keep, got, vmem=6))
    for d in range(1, y_n):
        summands[d] = shift(summands[d], "y", d)

    per = rows_n // x_n

    def over_x(x_ref, *refs):
        parts, outs, held = refs[:y_n], refs[y_n:-1], refs[-1]
        total = sum((p[...] for p in parts[1:]), parts[0][...]).reshape(steps * part, group)
        held[...] = total.T.reshape(rows_n, share, steps * part)
        for d in range(x_n):
            for i in range(per):
                outs[d][i] = held[i * x_n + lax.rem(x_ref[0] + d, x_n)]

    def over_z(x_ref, *refs):
        for d in range(x_n):
            for i in range(per):
                refs[-1][lax.rem(x_ref[0] + x_n - d, x_n) * per + i] = refs[d][i]

    x_at = x_i.reshape(1).astype(jnp.int32)
    y_rows = list(local(over_x, [(per, share, steps * part)] * x_n, [SMEM] + [VMEM] * y_n, x_at, *summands,
                        after=(group_n,), scratch=[(rows_n, share, steps * part)]))
    for d in range(1, x_n):
        y_rows[d] = shift(y_rows[d], "x", d)
    y_rows = local(over_z, (z_n, share, steps * part), [SMEM] + [VMEM] * x_n, x_at, *y_rows)
    y_rows = lax.all_to_all(y_rows, "z", 0, 0, tiled=True)

    count = steps + links_n
    t_rows, t_cols = part // z_n, width // x_n

    def gram(y_ref, n_ref, tiles, turned):
        turned[...] = y_ref[...].reshape(rows_n * share, steps * part).T

        def put(which, value):
            for i in range(z_n):
                for j in range(x_n):
                    tiles[i * x_n + j, which] = value[i * t_rows:(i + 1) * t_rows, j * t_cols:(j + 1) * t_cols]

        for k in range(steps):
            low = max(k - 1, 0)
            value = matmul(turned[low * part:(k + 1) * part, :], n_ref[:, k * width:(k + 1) * width])
            put(k, value[(k - low) * part:])
            if k:
                put(steps + k - 1, value[:part])

    tiles = local(gram, (cols_n, count, t_rows, t_cols), [VMEM] * 2, y_rows, group_n, vmem=8,
                  scratch=[(steps * part, rows_n * share)])
    summed = lax.all_to_all(tiles, COL, 0, 0, tiled=True)

    home = y_rows.reshape(y_n, 2, share, steps * part)
    home = jnp.stack([pick(home, core, 1), shift(pick(home, 1 - core, 1), "core", 1)], axis=1)
    home = [pick(home, (y_i + d) % y_n, 0) for d in range(y_n)]
    home = [home[0]] + [shift(home[d], "y", d) for d in range(1, y_n)]

    def finish_cols(place_ref, block_ref, depth_ref, *refs):
        dst, held = refs[y_n:]
        for d in range(y_n):
            y_from = lax.rem(place_ref[0] + y_n - d, y_n)
            held[y_from * 2 + place_ref[1]] = refs[d][0]
            held[y_from * 2 + 1 - place_ref[1]] = refs[d][1]
        for i in range(rows_n):
            for k in range(steps):
                sign = jnp.where(depth_ref[block_ref[0]] > k, -1.0, 0.0).astype(F32)
                dst[k, :, i * part:(i + 1) * part] = sign * held[i, :, k * part:(k + 1) * part]

    cols = local(finish_cols, (steps, share, width), [SMEM] * 3 + [VMEM] * y_n,
                 jnp.stack([y_i, core]).astype(jnp.int32), own_block, block_depth, *home, scratch=[(rows_n, share, steps * part)])

    def unit_rows(first_ref):
        at = lax.broadcasted_iota(jnp.int32, (part, width), 0) + first_ref[0]
        return (lax.broadcasted_iota(jnp.int32, (part, width), 1) == at).astype(F32)

    def down_first(first_ref, inverse_ref, parent_ref, left, rows):
        unit = unit_rows(first_ref)
        left[...] = matmul(unit, inverse_ref[...], ((1,), (1,)))
        rows[:part] = matmul(unit, parent_ref[...], ((1,), (1,)))
        rows[part:] = unit

    def down(first_ref, inverse_ref, parent_ref, above, left, rows):
        left[...] = matmul(above[...], inverse_ref[...], ((1,), (1,)))
        rows[:-part] = matmul(above[...], parent_ref[...], ((1,), (1,)))
        rows[-part:] = unit_rows(first_ref)

    def bottom(inverse_ref, parent_ref, above, own, carried):
        value = matmul(matmul(above[...], inverse_ref[...], ((1,), (1,))), inverse_ref[...])
        own[...] = value[-part:]
        carried[...] = matmul(value, parent_ref[...])

    def up(inverse_ref, parent_ref, left, below, own, carried):
        value = matmul(left[...], inverse_ref[...]) + below[:-part]
        own[...] = value[-part:]
        carried[...] = matmul(value, parent_ref[...])

    def up_last(inverse_ref, left, below, own):
        own[...] = matmul(left[...], inverse_ref[...]) + below[:-part]

    parent_at = [block(k, parent_panel.shape) for k in range(links_n)]
    inverse_at = [block(k, diag_inverse.shape) for k in range(steps)]
    first = (r * part).reshape(1).astype(jnp.int32)
    lefts, rows = [None] * steps, None
    for k in range(steps - 1, 0, -1):
        above = [] if rows is None else [rows]
        tall = (steps - k) * part
        lefts[k], rows = local(down if above else down_first, [(tall, width), (tall + part, width)],
                               [SMEM, inverse_at[k], parent_at[k - 1]] + [VMEM] * len(above),
                               first, diag_inverse, parent_panel, *above, after=() if above else (tiles,))
    diag_own, link_own = [None] * steps, [None] * links_n
    diag_own[0], carried = local(bottom, [(part, width), (steps * part, width)], [inverse_at[0], parent_at[0], VMEM],
                                 diag_inverse, parent_panel, rows)
    for k in range(1, steps):
        link_own[k - 1] = carried
        if k < steps - 1:
            diag_own[k], carried = local(up, [(part, width), ((steps - k) * part, width)],
                                         [inverse_at[k], parent_at[k], VMEM, VMEM],
                                         diag_inverse, parent_panel, lefts[k], carried)
        else:
            diag_own[k] = local(up_last, (part, width), [inverse_at[k], VMEM, VMEM], diag_inverse, lefts[k], carried)

    def total_kernel(src, dst):
        total = src[0]
        for i in range(1, cols_n):
            total = total + src[i]
        for i in range(cols_n):
            dst[i] = total

    every = lax.all_to_all(local(total_kernel, tiles.shape, [VMEM], summed, after=(diag_own[-1],)), COL, 0, 0, tiled=True)

    def finish(src, *refs):
        diag_refs, link_refs, (links, diags) = refs[:steps], refs[steps:count], refs[count:]
        for i in range(z_n):
            for j in range(x_n):
                place = (slice(i * t_rows, (i + 1) * t_rows), slice(j * t_cols, (j + 1) * t_cols))
                for k in range(steps):
                    diags[(k,) + place] = diag_refs[k][place] + src[i * x_n + j, k]
                for k in range(links_n):
                    last = link_refs[k].shape[0] - part
                    links[(k,) + place] = src[i * x_n + j, steps + k] - link_refs[k][last + i * t_rows:last + (i + 1) * t_rows, place[1]]

    links, diags = local(finish, [(links_n, part, width), (steps, part, width)], [VMEM] * (count + 1),
                         every, *diag_own, *link_own)
    return cols, links, diags


def solution(mesh):
    axes = Mesh(mesh.devices.reshape(4, 2, 8, 4), ("y", "core", "z", "x"))
    return jax.shard_map(
        shards,
        mesh=axes,
        in_specs=(P(ROW, COL), P(None, ALL, None), P(), P(), P()),
        out_specs=(P(None, ALL, None), P(None, ROW, None), P(None, ROW, None)),
        check_vma=False,
    )
```

```python
import jax
import jax.numpy as jnp
from jax import lax
from jax.experimental import pallas as pl
from jax.experimental.pallas import tpu as pltpu
from jax.sharding import Mesh, PartitionSpec as P

BLOCK = 128
ROW = ("y", "core")
COL = ("z", "x")
ALL = ROW + COL
F32 = jnp.float32
HIGHEST = lax.Precision.HIGHEST
VMEM = pl.BlockSpec(memory_space=pltpu.VMEM)
SMEM = pl.BlockSpec(memory_space=pltpu.SMEM)
ANY = pl.BlockSpec(memory_space=pl.ANY)
HBM = pl.BlockSpec(memory_space=pltpu.HBM)
MIB = 2**20


def matmul(a, b, dims=((1,), (0,)), precision=HIGHEST):
    return lax.dot_general(a, b, (dims, ((), ())), precision=precision, preferred_element_type=F32)


def local(kernel, out_shapes, specs, *args, after=(), scratch=(), semaphores=0, vmem=4):
    many = isinstance(out_shapes, list)
    shapes = [jax.ShapeDtypeStruct(s, F32) for s in (out_shapes if many else [out_shapes])]
    out = pl.pallas_call(
        lambda *refs: kernel(*refs[:len(args)], *refs[len(args) + len(after):]),
        out_shape=shapes,
        in_specs=list(specs) + [ANY] * len(after),
        out_specs=[VMEM] * len(shapes),
        grid=(1,) if any(spec.block_shape for spec in specs) else (),
        scratch_shapes=[pltpu.VMEM(shape, F32) if isinstance(shape, tuple) else shape for shape in scratch]
        + ([pltpu.SemaphoreType.DMA((semaphores,))] if semaphores else []),
        compiler_params=pltpu.CompilerParams(vmem_limit_bytes=vmem * MIB),
    )(*args, *after)
    return out if many else out[0]


def pack(pieces, after=()):
    def kernel(*refs):
        at = 0
        for ref in refs[:-1]:
            refs[-1][at:at + ref.shape[0]] = ref[...]
            at += ref.shape[0]

    rows = sum(piece.shape[0] for piece in pieces)
    return local(kernel, (rows,) + pieces[0].shape[1:], [VMEM] * len(pieces), *pieces, after=after)


def shift(value, axis, distance):
    n = lax.axis_size(axis)
    return lax.ppermute(value, axis, [(i, (i + distance) % n) for i in range(n)])


def ring(value, axis):
    half = value.shape[0] // 2
    out, up, down = [value], value, value
    for _ in range(lax.axis_size(axis) // 2 - 1):
        up, down = shift(up, axis, 1), shift(down, axis, -1)
        out += [up, down]
    return out + [shift(up[:half], axis, 1), shift(down[half:], axis, -1)]


def ring_sources(axis):
    n, me = lax.axis_size(axis), lax.axis_index(axis)
    offsets = [0]
    for s in range(1, n // 2):
        offsets += [n - s, s]
    return [(me + o) % n for o in offsets + [n // 2]]


def block(k, shape):
    return pl.BlockSpec((None,) + shape[1:], lambda i: (k,) + (0,) * (len(shape) - 1))


def pick(value, index, dim):
    return lax.dynamic_index_in_dim(value, index, dim, False)


def shards(sigma_top, panel, parent_panel, diag_inverse, block_depth):
    rows_n, cols_n = lax.axis_size(ROW), lax.axis_size(COL)
    y_n, z_n, x_n = (lax.axis_size(axis) for axis in ("y", "z", "x"))
    r, c = lax.axis_index(ROW), lax.axis_index(COL)
    y_i, core, x_i = lax.axis_index("y"), lax.axis_index("core"), lax.axis_index("x")
    steps, share, width = panel.shape
    group = sigma_top.shape[1]
    part = width // rows_n
    units = steps * y_n
    z_units = (units * 9 + 8) // 16
    cut = z_units * 2 * part
    links_n = steps - 1
    own_block = ((r * cols_n + c) * share // BLOCK).reshape(1).astype(jnp.int32)

    group_panel = lax.all_gather(panel, ROW, axis=0)
    group_depth = pick(block_depth.reshape(rows_n, -1), c * share // BLOCK, 1)

    def head(block_ref, depth_hbm, panel_hbm, parent_hbm, out_z, out_x, panel_ref, parent_ref, depth_ref, arrived):
        copies = [pltpu.make_async_copy(depth_hbm, depth_ref, arrived.at[0]),
                  pltpu.make_async_copy(panel_hbm, panel_ref, arrived.at[1])]
        copies += [pltpu.make_async_copy(parent_hbm.at[k], parent_ref.at[k], arrived.at[2 + k]) for k in range(links_n)]
        for copy in copies:
            copy.start()
        for copy in copies[:2]:
            copy.wait()
        value = None
        for k in range(steps):
            own = jnp.where(depth_ref[block_ref[0]] > k, 1.0, 0.0).astype(F32) * panel_ref[k]
            if k:
                copies[1 + k].wait()
                own = own - matmul(value, parent_ref[k - 1])
            value = own
            columns = min(max(cut - k * width, 0), width)
            if columns:
                out_z[:, k * width:k * width + columns] = value[:, :columns]
            if columns < width:
                at = k * width + columns - cut
                out_x[:, at:at + width - columns] = value[:, columns:]

    far = [pltpu.with_memory_space_constraint(a, pltpu.HBM) for a in (block_depth, panel, parent_panel)]
    n_z, n_x = local(head, [(share, cut), (share, steps * width - cut)], [SMEM, HBM, HBM, HBM], own_block, *far, vmem=6,
                     scratch=[panel.shape, parent_panel.shape, pltpu.SMEM(block_depth.shape, jnp.int32)],
                     semaphores=2 + links_n)

    by_z = ring(n_z, "z")
    by_x = [n_x, shift(n_x, "x", 1), shift(n_x, "x", -1), shift(n_x, "x", 2)]

    starts = jnp.stack([(zz * x_n + xx) * share for zz in ring_sources("z") for xx in ring_sources("x")])

    def turn(starts_ref, top, z_major, x_major):
        for i in range(z_n):
            for j in range(x_n):
                rows = top[pl.ds(pl.multiple_of(starts_ref[i * x_n + j], share), share), :]
                z_major[i, j * share:(j + 1) * share, :] = rows
                x_major[j, i * share:(i + 1) * share, :] = rows

    z_major, x_major = local(turn, [(z_n, x_n * share, group), (x_n, z_n * share, group)], [SMEM, VMEM],
                             starts.astype(jnp.int32), sigma_top, after=(by_z[1],))

    def product(total, blocks, tops):
        block = blocks[0] if len(blocks) == 1 else jnp.concatenate(blocks, axis=0)
        term = matmul(block, tops.reshape(-1, group), ((0,), (0,)), lax.Precision.HIGH)
        return term if total is None else total + term

    z_sum = x_sum = None
    arrived = ring(pack(by_z), "x")
    for j in range(x_n):
        z_sum = product(z_sum, arrived[j:] if j == x_n - 1 else arrived[j:j + 1], x_major[j:j + 1])
    arrived = ring(pack(by_x, after=(by_z[-1],)), "z")
    x_sum = product(x_sum, arrived[:1], z_major[:1])
    for j in range(1, z_n - 1, 2):
        x_sum = product(x_sum, arrived[j:j + 2], z_major[j:j + 2])
    x_sum = product(x_sum, arrived[z_n - 1:], z_major[z_n - 1:])

    def group_head(depth_ref, panel_ref, parent_ref, out):
        for k in range(steps):
            at = slice(k * width, (k + 1) * width)
            for i in range(rows_n):
                mask = jnp.where(depth_ref[i] > k, 1.0, 0.0).astype(F32)
                out[i * share:(i + 1) * share, at] = mask * panel_ref[i, k]
            if k:
                out[:, at] -= matmul(out[:, (k - 1) * width:k * width], parent_ref[k - 1])

    group_n = local(group_head, (rows_n * share, steps * width), [SMEM, VMEM, VMEM], group_depth, group_panel, parent_panel, vmem=12)

    def split(core_ref, z_ref, x_ref, keep, give):
        for unit in range(units):
            ref, at = (z_ref, unit) if unit < z_units else (x_ref, unit - z_units)
            keep[unit // y_n, unit % y_n] = ref[at, core_ref[0]]
            give[unit // y_n, unit % y_n] = ref[at, 1 - core_ref[0]]

    keep, give = local(split, [(steps, y_n, part, group)] * 2, [SMEM, VMEM, VMEM], core.reshape(1).astype(jnp.int32),
                       z_sum.reshape(z_units, 2, part, group), x_sum.reshape(units - z_units, 2, part, group), vmem=6)
    got = shift(give, "core", 1)

    def by_y(y_ref, keep_ref, got_ref, *outs):
        for d in range(y_n):
            i = lax.rem(y_ref[0] + d, y_n)
            for k in range(steps):
                outs[d][k] = keep_ref[k, i] + got_ref[k, i]

    summands = list(local(by_y, [(steps, part, group)] * y_n, [SMEM, VMEM, VMEM], y_i.reshape(1).astype(jnp.int32),
                          keep, got, vmem=6))
    for d in range(1, y_n):
        summands[d] = shift(summands[d], "y", d)

    per = rows_n // x_n

    def over_x(x_ref, *refs):
        parts, outs, held = refs[:y_n], refs[y_n:-1], refs[-1]
        total = sum((p[...] for p in parts[1:]), parts[0][...]).reshape(steps * part, group)
        held[...] = total.T.reshape(rows_n, share, steps * part)
        for d in range(x_n):
            for i in range(per):
                outs[d][i] = held[i * x_n + lax.rem(x_ref[0] + d, x_n)]

    def over_z(x_ref, *refs):
        for d in range(x_n):
            for i in range(per):
                refs[-1][lax.rem(x_ref[0] + x_n - d, x_n) * per + i] = refs[d][i]

    x_at = x_i.reshape(1).astype(jnp.int32)
    y_rows = list(local(over_x, [(per, share, steps * part)] * x_n, [SMEM] + [VMEM] * y_n, x_at, *summands,
                        after=(group_n,), scratch=[(rows_n, share, steps * part)]))
    for d in range(1, x_n):
        y_rows[d] = shift(y_rows[d], "x", d)
    y_rows = local(over_z, (z_n, share, steps * part), [SMEM] + [VMEM] * x_n, x_at, *y_rows)
    y_rows = lax.all_to_all(y_rows, "z", 0, 0, tiled=True)

    count = steps + links_n
    t_rows, t_cols = part // z_n, width // x_n

    def gram(y_ref, n_ref, tiles, turned):
        turned[...] = y_ref[...].reshape(rows_n * share, steps * part).T

        def put(which, value):
            for i in range(z_n):
                for j in range(x_n):
                    tiles[i * x_n + j, which] = value[i * t_rows:(i + 1) * t_rows, j * t_cols:(j + 1) * t_cols]

        for k in range(steps):
            low = max(k - 1, 0)
            value = matmul(turned[low * part:(k + 1) * part, :], n_ref[:, k * width:(k + 1) * width])
            put(k, value[(k - low) * part:])
            if k:
                put(steps + k - 1, value[:part])

    tiles = local(gram, (cols_n, count, t_rows, t_cols), [VMEM] * 2, y_rows, group_n, vmem=8,
                  scratch=[(steps * part, rows_n * share)])
    summed = lax.all_to_all(tiles, COL, 0, 0, tiled=True)

    home = y_rows.reshape(y_n, 2, share, steps * part)
    home = jnp.stack([pick(home, core, 1), shift(pick(home, 1 - core, 1), "core", 1)], axis=1)
    home = [pick(home, (y_i + d) % y_n, 0) for d in range(y_n)]
    home = [home[0]] + [shift(home[d], "y", d) for d in range(1, y_n)]

    def finish_cols(place_ref, block_ref, depth_ref, *refs):
        dst, held = refs[y_n:]
        for d in range(y_n):
            y_from = lax.rem(place_ref[0] + y_n - d, y_n)
            held[y_from * 2 + place_ref[1]] = refs[d][0]
            held[y_from * 2 + 1 - place_ref[1]] = refs[d][1]
        for i in range(rows_n):
            for k in range(steps):
                sign = jnp.where(depth_ref[block_ref[0]] > k, -1.0, 0.0).astype(F32)
                dst[k, :, i * part:(i + 1) * part] = sign * held[i, :, k * part:(k + 1) * part]

    cols = local(finish_cols, (steps, share, width), [SMEM] * 3 + [VMEM] * y_n,
                 jnp.stack([y_i, core]).astype(jnp.int32), own_block, block_depth, *home, scratch=[(rows_n, share, steps * part)])

    def unit_rows(first_ref):
        at = lax.broadcasted_iota(jnp.int32, (part, width), 0) + first_ref[0]
        return (lax.broadcasted_iota(jnp.int32, (part, width), 1) == at).astype(F32)

    def down_first(first_ref, inverse_ref, parent_ref, left, rows):
        unit = unit_rows(first_ref)
        left[...] = matmul(unit, inverse_ref[...], ((1,), (1,)))
        rows[:part] = matmul(unit, parent_ref[...], ((1,), (1,)))
        rows[part:] = unit

    def down(first_ref, inverse_ref, parent_ref, above, left, rows):
        left[...] = matmul(above[...], inverse_ref[...], ((1,), (1,)))
        rows[:-part] = matmul(above[...], parent_ref[...], ((1,), (1,)))
        rows[-part:] = unit_rows(first_ref)

    def bottom(inverse_ref, parent_ref, above, own, carried):
        value = matmul(matmul(above[...], inverse_ref[...], ((1,), (1,))), inverse_ref[...])
        own[...] = value[-part:]
        carried[...] = matmul(value, parent_ref[...])

    def up(inverse_ref, parent_ref, left, below, own, carried):
        value = matmul(left[...], inverse_ref[...]) + below[:-part]
        own[...] = value[-part:]
        carried[...] = matmul(value, parent_ref[...])

    def up_last(inverse_ref, left, below, own):
        own[...] = matmul(left[...], inverse_ref[...]) + below[:-part]

    parent_at = [block(k, parent_panel.shape) for k in range(links_n)]
    inverse_at = [block(k, diag_inverse.shape) for k in range(steps)]
    first = (r * part).reshape(1).astype(jnp.int32)
    lefts, rows = [None] * steps, None
    for k in range(steps - 1, 0, -1):
        above = [] if rows is None else [rows]
        tall = (steps - k) * part
        lefts[k], rows = local(down if above else down_first, [(tall, width), (tall + part, width)],
                               [SMEM, inverse_at[k], parent_at[k - 1]] + [VMEM] * len(above),
                               first, diag_inverse, parent_panel, *above, after=() if above else (tiles,))
    diag_own, link_own = [None] * steps, [None] * links_n
    diag_own[0], carried = local(bottom, [(part, width), (steps * part, width)], [inverse_at[0], parent_at[0], VMEM],
                                 diag_inverse, parent_panel, rows)
    for k in range(1, steps):
        link_own[k - 1] = carried
        if k < steps - 1:
            diag_own[k], carried = local(up, [(part, width), ((steps - k) * part, width)],
                                         [inverse_at[k], parent_at[k], VMEM, VMEM],
                                         diag_inverse, parent_panel, lefts[k], carried)
        else:
            diag_own[k] = local(up_last, (part, width), [inverse_at[k], VMEM, VMEM], diag_inverse, lefts[k], carried)

    def total_kernel(src, dst):
        total = src[0]
        for i in range(1, cols_n):
            total = total + src[i]
        for i in range(cols_n):
            dst[i] = total

    every = lax.all_to_all(local(total_kernel, tiles.shape, [VMEM], summed, after=(diag_own[-1],)), COL, 0, 0, tiled=True)

    def finish(src, *refs):
        diag_refs, link_refs, (links, diags) = refs[:steps], refs[steps:count], refs[count:]
        for i in range(z_n):
            for j in range(x_n):
                place = (slice(i * t_rows, (i + 1) * t_rows), slice(j * t_cols, (j + 1) * t_cols))
                for k in range(steps):
                    diags[(k,) + place] = diag_refs[k][place] + src[i * x_n + j, k]
                for k in range(links_n):
                    last = link_refs[k].shape[0] - part
                    links[(k,) + place] = src[i * x_n + j, steps + k] - link_refs[k][last + i * t_rows:last + (i + 1) * t_rows, place[1]]

    links, diags = local(finish, [(links_n, part, width), (steps, part, width)], [VMEM] * (count + 1),
                         every, *diag_own, *link_own)
    return cols, links, diags


def solution(mesh):
    axes = Mesh(mesh.devices.reshape(4, 2, 8, 4), ("y", "core", "z", "x"))
    return jax.shard_map(
        shards,
        mesh=axes,
        in_specs=(P(ROW, COL), P(None, ALL, None), P(), P(), P()),
        out_specs=(P(None, ALL, None), P(None, ROW, None), P(None, ROW, None)),
        check_vma=False,
    )
```

```python
import jax
import jax.numpy as jnp
from jax import lax
from jax.experimental import pallas as pl
from jax.experimental.pallas import tpu as pltpu
from jax.sharding import Mesh, PartitionSpec as P

BLOCK = 128
ROW = ("y", "core")
COL = ("z", "x")
ALL = ROW + COL
F32 = jnp.float32
HIGHEST = lax.Precision.HIGHEST
VMEM = pl.BlockSpec(memory_space=pltpu.VMEM)
SMEM = pl.BlockSpec(memory_space=pltpu.SMEM)
ANY = pl.BlockSpec(memory_space=pl.ANY)
HBM = pl.BlockSpec(memory_space=pltpu.HBM)
MIB = 2**20


def matmul(a, b, dims=((1,), (0,)), precision=HIGHEST):
    return lax.dot_general(a, b, (dims, ((), ())), precision=precision, preferred_element_type=F32)


def local(kernel, out_shapes, specs, *args, after=(), scratch=(), semaphores=0, vmem=4):
    many = isinstance(out_shapes, list)
    shapes = [jax.ShapeDtypeStruct(s, F32) for s in (out_shapes if many else [out_shapes])]
    out = pl.pallas_call(
        lambda *refs: kernel(*refs[:len(args)], *refs[len(args) + len(after):]),
        out_shape=shapes,
        in_specs=list(specs) + [ANY] * len(after),
        out_specs=[VMEM] * len(shapes),
        grid=(1,) if any(spec.block_shape for spec in specs) else (),
        scratch_shapes=[pltpu.VMEM(shape, F32) if isinstance(shape, tuple) else shape for shape in scratch]
        + ([pltpu.SemaphoreType.DMA((semaphores,))] if semaphores else []),
        compiler_params=pltpu.CompilerParams(vmem_limit_bytes=vmem * MIB),
    )(*args, *after)
    return out if many else out[0]


def pack(pieces, after=()):
    def kernel(*refs):
        at = 0
        for ref in refs[:-1]:
            refs[-1][at:at + ref.shape[0]] = ref[...]
            at += ref.shape[0]

    rows = sum(piece.shape[0] for piece in pieces)
    return local(kernel, (rows,) + pieces[0].shape[1:], [VMEM] * len(pieces), *pieces, after=after)


def shift(value, axis, distance):
    n = lax.axis_size(axis)
    return lax.ppermute(value, axis, [(i, (i + distance) % n) for i in range(n)])


def ring(value, axis):
    half = value.shape[0] // 2
    out, up, down = [value], value, value
    for _ in range(lax.axis_size(axis) // 2 - 1):
        up, down = shift(up, axis, 1), shift(down, axis, -1)
        out += [up, down]
    return out + [shift(up[:half], axis, 1), shift(down[half:], axis, -1)]


def ring_sources(axis):
    n, me = lax.axis_size(axis), lax.axis_index(axis)
    offsets = [0]
    for s in range(1, n // 2):
        offsets += [n - s, s]
    return [(me + o) % n for o in offsets + [n // 2]]


def block(k, shape):
    return pl.BlockSpec((None,) + shape[1:], lambda i: (k,) + (0,) * (len(shape) - 1))


def pick(value, index, dim):
    return lax.dynamic_index_in_dim(value, index, dim, False)


def shards(sigma_top, panel, parent_panel, diag_inverse, block_depth):
    rows_n, cols_n = lax.axis_size(ROW), lax.axis_size(COL)
    y_n, z_n, x_n = (lax.axis_size(axis) for axis in ("y", "z", "x"))
    r, c = lax.axis_index(ROW), lax.axis_index(COL)
    y_i, core, x_i = lax.axis_index("y"), lax.axis_index("core"), lax.axis_index("x")
    steps, share, width = panel.shape
    group = sigma_top.shape[1]
    part = width // rows_n
    units = steps * y_n
    z_units = (units * 10 + 8) // 16
    cut = z_units * 2 * part
    links_n = steps - 1
    own_block = ((r * cols_n + c) * share // BLOCK).reshape(1).astype(jnp.int32)

    group_panel = lax.all_gather(panel, ROW, axis=0)
    group_depth = pick(block_depth.reshape(rows_n, -1), c * share // BLOCK, 1)

    def head(block_ref, depth_hbm, panel_hbm, parent_hbm, out_z, out_x, panel_ref, parent_ref, depth_ref, arrived):
        copies = [pltpu.make_async_copy(depth_hbm, depth_ref, arrived.at[0]),
                  pltpu.make_async_copy(panel_hbm, panel_ref, arrived.at[1])]
        copies += [pltpu.make_async_copy(parent_hbm.at[k], parent_ref.at[k], arrived.at[2 + k]) for k in range(links_n)]
        for copy in copies:
            copy.start()
        for copy in copies[:2]:
            copy.wait()
        value = None
        for k in range(steps):
            own = jnp.where(depth_ref[block_ref[0]] > k, 1.0, 0.0).astype(F32) * panel_ref[k]
            if k:
                copies[1 + k].wait()
                own = own - matmul(value, parent_ref[k - 1])
            value = own
            columns = min(max(cut - k * width, 0), width)
            if columns:
                out_z[:, k * width:k * width + columns] = value[:, :columns]
            if columns < width:
                at = k * width + columns - cut
                out_x[:, at:at + width - columns] = value[:, columns:]

    far = [pltpu.with_memory_space_constraint(a, pltpu.HBM) for a in (block_depth, panel, parent_panel)]
    n_z, n_x = local(head, [(share, cut), (share, steps * width - cut)], [SMEM, HBM, HBM, HBM], own_block, *far, vmem=6,
                     scratch=[panel.shape, parent_panel.shape, pltpu.SMEM(block_depth.shape, jnp.int32)],
                     semaphores=2 + links_n)

    by_z = ring(n_z, "z")
    by_x = [n_x, shift(n_x, "x", 1), shift(n_x, "x", -1), shift(n_x, "x", 2)]

    starts = jnp.stack([(zz * x_n + xx) * share for zz in ring_sources("z") for xx in ring_sources("x")])

    def turn(starts_ref, top, z_major, x_major):
        for i in range(z_n):
            for j in range(x_n):
                rows = top[pl.ds(pl.multiple_of(starts_ref[i * x_n + j], share), share), :]
                z_major[i, j * share:(j + 1) * share, :] = rows
                x_major[j, i * share:(i + 1) * share, :] = rows

    z_major, x_major = local(turn, [(z_n, x_n * share, group), (x_n, z_n * share, group)], [SMEM, VMEM],
                             starts.astype(jnp.int32), sigma_top, after=(by_z[1],))

    def product(total, blocks, tops):
        block = blocks[0] if len(blocks) == 1 else jnp.concatenate(blocks, axis=0)
        term = matmul(block, tops.reshape(-1, group), ((0,), (0,)), lax.Precision.HIGH)
        return term if total is None else total + term

    z_sum = x_sum = None
    low = pack(by_z[:z_n // 2], after=tuple(by_x[1:]))
    high = pack(by_z[z_n // 2:])
    arrived = [[low, high]] + [[shift(low, "x", d), shift(high, "x", d)] for d in (1, -1)]
    arrived.append([shift(arrived[1][0], "x", 1), shift(arrived[2][1], "x", -1)])
    for j in range(x_n):
        z_sum = product(z_sum, arrived[j], x_major[j:j + 1])
    arrived = ring(pack(by_x, after=(by_z[-1],)), "z")
    x_sum = product(x_sum, arrived[:1], z_major[:1])
    for j in range(1, z_n - 1, 2):
        x_sum = product(x_sum, arrived[j:j + 2], z_major[j:j + 2])
    x_sum = product(x_sum, arrived[z_n - 1:], z_major[z_n - 1:])

    def group_head(depth_ref, panel_ref, parent_ref, out):
        for k in range(steps):
            at = slice(k * width, (k + 1) * width)
            for i in range(rows_n):
                mask = jnp.where(depth_ref[i] > k, 1.0, 0.0).astype(F32)
                out[i * share:(i + 1) * share, at] = mask * panel_ref[i, k]
            if k:
                out[:, at] -= matmul(out[:, (k - 1) * width:k * width], parent_ref[k - 1])

    group_n = local(group_head, (rows_n * share, steps * width), [SMEM, VMEM, VMEM], group_depth, group_panel, parent_panel, vmem=12)

    def split(core_ref, z_ref, x_ref, keep, give):
        for unit in range(units):
            ref, at = (z_ref, unit) if unit < z_units else (x_ref, unit - z_units)
            keep[unit // y_n, unit % y_n] = ref[at, core_ref[0]]
            give[unit // y_n, unit % y_n] = ref[at, 1 - core_ref[0]]

    keep, give = local(split, [(steps, y_n, part, group)] * 2, [SMEM, VMEM, VMEM], core.reshape(1).astype(jnp.int32),
                       z_sum.reshape(z_units, 2, part, group), x_sum.reshape(units - z_units, 2, part, group), vmem=6)
    got = shift(give, "core", 1)

    def by_y(y_ref, keep_ref, got_ref, *outs):
        for d in range(y_n):
            i = lax.rem(y_ref[0] + d, y_n)
            for k in range(steps):
                outs[d][k] = keep_ref[k, i] + got_ref[k, i]

    summands = list(local(by_y, [(steps, part, group)] * y_n, [SMEM, VMEM, VMEM], y_i.reshape(1).astype(jnp.int32),
                          keep, got, vmem=6))
    for d in range(1, y_n):
        summands[d] = shift(summands[d], "y", d)

    per = rows_n // x_n

    def over_x(x_ref, *refs):
        parts, outs, held = refs[:y_n], refs[y_n:-1], refs[-1]
        total = sum((p[...] for p in parts[1:]), parts[0][...]).reshape(steps * part, group)
        held[...] = total.T.reshape(rows_n, share, steps * part)
        for d in range(x_n):
            for i in range(per):
                outs[d][i] = held[i * x_n + lax.rem(x_ref[0] + d, x_n)]

    def over_z(x_ref, *refs):
        for d in range(x_n):
            for i in range(per):
                refs[-1][lax.rem(x_ref[0] + x_n - d, x_n) * per + i] = refs[d][i]

    x_at = x_i.reshape(1).astype(jnp.int32)
    y_rows = list(local(over_x, [(per, share, steps * part)] * x_n, [SMEM] + [VMEM] * y_n, x_at, *summands,
                        after=(group_n,), scratch=[(rows_n, share, steps * part)]))
    for d in range(1, x_n):
        y_rows[d] = shift(y_rows[d], "x", d)
    y_rows = local(over_z, (z_n, share, steps * part), [SMEM] + [VMEM] * x_n, x_at, *y_rows)
    y_rows = lax.all_to_all(y_rows, "z", 0, 0, tiled=True)

    count = steps + links_n
    t_rows, t_cols = part // z_n, width // x_n

    def gram(y_ref, n_ref, tiles, turned):
        turned[...] = y_ref[...].reshape(rows_n * share, steps * part).T

        def put(which, value):
            for i in range(z_n):
                for j in range(x_n):
                    tiles[i * x_n + j, which] = value[i * t_rows:(i + 1) * t_rows, j * t_cols:(j + 1) * t_cols]

        for k in range(steps):
            low = max(k - 1, 0)
            value = matmul(turned[low * part:(k + 1) * part, :], n_ref[:, k * width:(k + 1) * width])
            put(k, value[(k - low) * part:])
            if k:
                put(steps + k - 1, value[:part])

    tiles = local(gram, (cols_n, count, t_rows, t_cols), [VMEM] * 2, y_rows, group_n, vmem=8,
                  scratch=[(steps * part, rows_n * share)])
    summed = lax.all_to_all(tiles, COL, 0, 0, tiled=True)

    home = y_rows.reshape(y_n, 2, share, steps * part)
    home = jnp.stack([pick(home, core, 1), shift(pick(home, 1 - core, 1), "core", 1)], axis=1)
    home = [pick(home, (y_i + d) % y_n, 0) for d in range(y_n)]
    home = [home[0]] + [shift(home[d], "y", d) for d in range(1, y_n)]

    def finish_cols(place_ref, block_ref, depth_ref, *refs):
        dst, held = refs[y_n:]
        for d in range(y_n):
            y_from = lax.rem(place_ref[0] + y_n - d, y_n)
            held[y_from * 2 + place_ref[1]] = refs[d][0]
            held[y_from * 2 + 1 - place_ref[1]] = refs[d][1]
        for i in range(rows_n):
            for k in range(steps):
                sign = jnp.where(depth_ref[block_ref[0]] > k, -1.0, 0.0).astype(F32)
                dst[k, :, i * part:(i + 1) * part] = sign * held[i, :, k * part:(k + 1) * part]

    cols = local(finish_cols, (steps, share, width), [SMEM] * 3 + [VMEM] * y_n,
                 jnp.stack([y_i, core]).astype(jnp.int32), own_block, block_depth, *home, scratch=[(rows_n, share, steps * part)])

    def unit_rows(first_ref):
        at = lax.broadcasted_iota(jnp.int32, (part, width), 0) + first_ref[0]
        return (lax.broadcasted_iota(jnp.int32, (part, width), 1) == at).astype(F32)

    def down_first(first_ref, inverse_ref, parent_ref, left, rows):
        unit = unit_rows(first_ref)
        left[...] = matmul(unit, inverse_ref[...], ((1,), (1,)))
        rows[:part] = matmul(unit, parent_ref[...], ((1,), (1,)))
        rows[part:] = unit

    def down(first_ref, inverse_ref, parent_ref, above, left, rows):
        left[...] = matmul(above[...], inverse_ref[...], ((1,), (1,)))
        rows[:-part] = matmul(above[...], parent_ref[...], ((1,), (1,)))
        rows[-part:] = unit_rows(first_ref)

    def bottom(inverse_ref, parent_ref, above, own, carried):
        value = matmul(matmul(above[...], inverse_ref[...], ((1,), (1,))), inverse_ref[...])
        own[...] = value[-part:]
        carried[...] = matmul(value, parent_ref[...])

    def up(inverse_ref, parent_ref, left, below, own, carried):
        value = matmul(left[...], inverse_ref[...]) + below[:-part]
        own[...] = value[-part:]
        carried[...] = matmul(value, parent_ref[...])

    def up_last(inverse_ref, left, below, own):
        own[...] = matmul(left[...], inverse_ref[...]) + below[:-part]

    parent_at = [block(k, parent_panel.shape) for k in range(links_n)]
    inverse_at = [block(k, diag_inverse.shape) for k in range(steps)]
    first = (r * part).reshape(1).astype(jnp.int32)
    lefts, rows = [None] * steps, None
    for k in range(steps - 1, 0, -1):
        above = [] if rows is None else [rows]
        tall = (steps - k) * part
        lefts[k], rows = local(down if above else down_first, [(tall, width), (tall + part, width)],
                               [SMEM, inverse_at[k], parent_at[k - 1]] + [VMEM] * len(above),
                               first, diag_inverse, parent_panel, *above, after=() if above else (tiles,))
    diag_own, link_own = [None] * steps, [None] * links_n
    diag_own[0], carried = local(bottom, [(part, width), (steps * part, width)], [inverse_at[0], parent_at[0], VMEM],
                                 diag_inverse, parent_panel, rows)
    for k in range(1, steps):
        link_own[k - 1] = carried
        if k < steps - 1:
            diag_own[k], carried = local(up, [(part, width), ((steps - k) * part, width)],
                                         [inverse_at[k], parent_at[k], VMEM, VMEM],
                                         diag_inverse, parent_panel, lefts[k], carried)
        else:
            diag_own[k] = local(up_last, (part, width), [inverse_at[k], VMEM, VMEM], diag_inverse, lefts[k], carried)

    def total_kernel(src, dst):
        total = src[0]
        for i in range(1, cols_n):
            total = total + src[i]
        for i in range(cols_n):
            dst[i] = total

    every = lax.all_to_all(local(total_kernel, tiles.shape, [VMEM], summed, after=(diag_own[-1],)), COL, 0, 0, tiled=True)

    def finish(src, *refs):
        diag_refs, link_refs, (links, diags) = refs[:steps], refs[steps:count], refs[count:]
        for i in range(z_n):
            for j in range(x_n):
                place = (slice(i * t_rows, (i + 1) * t_rows), slice(j * t_cols, (j + 1) * t_cols))
                for k in range(steps):
                    diags[(k,) + place] = diag_refs[k][place] + src[i * x_n + j, k]
                for k in range(links_n):
                    last = link_refs[k].shape[0] - part
                    links[(k,) + place] = src[i * x_n + j, steps + k] - link_refs[k][last + i * t_rows:last + (i + 1) * t_rows, place[1]]

    links, diags = local(finish, [(links_n, part, width), (steps, part, width)], [VMEM] * (count + 1),
                         every, *diag_own, *link_own)
    return cols, links, diags


def solution(mesh):
    axes = Mesh(mesh.devices.reshape(4, 2, 8, 4), ("y", "core", "z", "x"))
    return jax.shard_map(
        shards,
        mesh=axes,
        in_specs=(P(ROW, COL), P(None, ALL, None), P(), P(), P()),
        out_specs=(P(None, ALL, None), P(None, ROW, None), P(None, ROW, None)),
        check_vma=False,
    )
```

```python
import jax
import jax.numpy as jnp
from jax import lax
from jax.experimental import pallas as pl
from jax.experimental.pallas import tpu as pltpu
from jax.sharding import Mesh, PartitionSpec as P

BLOCK = 128
ROW = ("y", "core")
COL = ("z", "x")
ALL = ROW + COL
F32 = jnp.float32
HIGHEST = lax.Precision.HIGHEST
VMEM = pl.BlockSpec(memory_space=pltpu.VMEM)
SMEM = pl.BlockSpec(memory_space=pltpu.SMEM)
ANY = pl.BlockSpec(memory_space=pl.ANY)
HBM = pl.BlockSpec(memory_space=pltpu.HBM)
MIB = 2**20


def matmul(a, b, dims=((1,), (0,)), precision=HIGHEST):
    return lax.dot_general(a, b, (dims, ((), ())), precision=precision, preferred_element_type=F32)


def local(kernel, out_shapes, specs, *args, after=(), scratch=(), semaphores=0, vmem=4):
    many = isinstance(out_shapes, list)
    shapes = [jax.ShapeDtypeStruct(s, F32) for s in (out_shapes if many else [out_shapes])]
    out = pl.pallas_call(
        lambda *refs: kernel(*refs[:len(args)], *refs[len(args) + len(after):]),
        out_shape=shapes,
        in_specs=list(specs) + [ANY] * len(after),
        out_specs=[VMEM] * len(shapes),
        grid=(1,) if any(spec.block_shape for spec in specs) else (),
        scratch_shapes=[pltpu.VMEM(shape, F32) if isinstance(shape, tuple) else shape for shape in scratch]
        + ([pltpu.SemaphoreType.DMA((semaphores,))] if semaphores else []),
        compiler_params=pltpu.CompilerParams(vmem_limit_bytes=vmem * MIB),
    )(*args, *after)
    return out if many else out[0]


def pack(pieces, after=()):
    def kernel(*refs):
        at = 0
        for ref in refs[:-1]:
            refs[-1][at:at + ref.shape[0]] = ref[...]
            at += ref.shape[0]

    rows = sum(piece.shape[0] for piece in pieces)
    return local(kernel, (rows,) + pieces[0].shape[1:], [VMEM] * len(pieces), *pieces, after=after)


def shift(value, axis, distance):
    n = lax.axis_size(axis)
    return lax.ppermute(value, axis, [(i, (i + distance) % n) for i in range(n)])


def ring(value, axis):
    half = value.shape[0] // 2
    out, up, down = [value], value, value
    for _ in range(lax.axis_size(axis) // 2 - 1):
        up, down = shift(up, axis, 1), shift(down, axis, -1)
        out += [up, down]
    return out + [shift(up[:half], axis, 1), shift(down[half:], axis, -1)]


def ring_sources(axis):
    n, me = lax.axis_size(axis), lax.axis_index(axis)
    offsets = [0]
    for s in range(1, n // 2):
        offsets += [n - s, s]
    return [(me + o) % n for o in offsets + [n // 2]]


def block(k, shape):
    return pl.BlockSpec((None,) + shape[1:], lambda i: (k,) + (0,) * (len(shape) - 1))


def pick(value, index, dim):
    return lax.dynamic_index_in_dim(value, index, dim, False)


def shards(sigma_top, panel, parent_panel, diag_inverse, block_depth):
    rows_n, cols_n = lax.axis_size(ROW), lax.axis_size(COL)
    y_n, z_n, x_n = (lax.axis_size(axis) for axis in ("y", "z", "x"))
    r, c = lax.axis_index(ROW), lax.axis_index(COL)
    y_i, core, x_i = lax.axis_index("y"), lax.axis_index("core"), lax.axis_index("x")
    steps, share, width = panel.shape
    group = sigma_top.shape[1]
    part = width // rows_n
    units = steps * y_n
    z_units = (units * 9 + 8) // 16
    cut = z_units * 2 * part
    links_n = steps - 1
    own_block = ((r * cols_n + c) * share // BLOCK).reshape(1).astype(jnp.int32)

    group_panel = lax.all_gather(panel, ROW, axis=0)
    group_depth = pick(block_depth.reshape(rows_n, -1), c * share // BLOCK, 1)

    def head(block_ref, depth_hbm, panel_hbm, parent_hbm, out_z, out_x, panel_ref, parent_ref, depth_ref, arrived):
        copies = [pltpu.make_async_copy(depth_hbm, depth_ref, arrived.at[0]),
                  pltpu.make_async_copy(panel_hbm, panel_ref, arrived.at[1])]
        copies += [pltpu.make_async_copy(parent_hbm.at[k], parent_ref.at[k], arrived.at[2 + k]) for k in range(links_n)]
        for copy in copies:
            copy.start()
        for copy in copies[:2]:
            copy.wait()
        value = None
        for k in range(steps):
            own = jnp.where(depth_ref[block_ref[0]] > k, 1.0, 0.0).astype(F32) * panel_ref[k]
            if k:
                copies[1 + k].wait()
                own = own - matmul(value, parent_ref[k - 1])
            value = own
            columns = min(max(cut - k * width, 0), width)
            if columns:
                out_z[:, k * width:k * width + columns] = value[:, :columns]
            if columns < width:
                at = k * width + columns - cut
                out_x[:, at:at + width - columns] = value[:, columns:]

    far = [pltpu.with_memory_space_constraint(a, pltpu.HBM) for a in (block_depth, panel, parent_panel)]
    n_z, n_x = local(head, [(share, cut), (share, steps * width - cut)], [SMEM, HBM, HBM, HBM], own_block, *far, vmem=6,
                     scratch=[panel.shape, parent_panel.shape, pltpu.SMEM(block_depth.shape, jnp.int32)],
                     semaphores=2 + links_n)

    by_z = ring(n_z, "z")
    by_x = [n_x, shift(n_x, "x", 1), shift(n_x, "x", -1), shift(n_x, "x", 2)]

    starts = jnp.stack([(zz * x_n + xx) * share for zz in ring_sources("z") for xx in ring_sources("x")])

    def turn(starts_ref, top, z_major, x_major):
        for i in range(z_n):
            for j in range(x_n):
                rows = top[pl.ds(pl.multiple_of(starts_ref[i * x_n + j], share), share), :]
                z_major[i, j * share:(j + 1) * share, :] = rows
                x_major[j, i * share:(i + 1) * share, :] = rows

    z_major, x_major = local(turn, [(z_n, x_n * share, group), (x_n, z_n * share, group)], [SMEM, VMEM],
                             starts.astype(jnp.int32), sigma_top, after=(by_z[1],))

    def product(total, blocks, tops):
        block = blocks[0] if len(blocks) == 1 else jnp.concatenate(blocks, axis=0)
        term = matmul(block, tops.reshape(-1, group), ((0,), (0,)), lax.Precision.HIGH)
        return term if total is None else total + term

    z_sum = x_sum = None
    arrived = ring(pack(by_z), "x")
    for j in range(x_n):
        z_sum = product(z_sum, arrived[j:] if j == x_n - 1 else arrived[j:j + 1], x_major[j:j + 1])
    arrived = ring(pack(by_x, after=(by_z[-2], by_z[-1])), "z")
    x_sum = product(x_sum, arrived[:1], z_major[:1])
    for j in range(1, z_n - 1, 2):
        x_sum = product(x_sum, arrived[j:j + 2], z_major[j:j + 2])
    x_sum = product(x_sum, arrived[z_n - 1:], z_major[z_n - 1:])

    def group_head(depth_ref, panel_ref, parent_ref, out):
        for k in range(steps):
            at = slice(k * width, (k + 1) * width)
            for i in range(rows_n):
                mask = jnp.where(depth_ref[i] > k, 1.0, 0.0).astype(F32)
                out[i * share:(i + 1) * share, at] = mask * panel_ref[i, k]
            if k:
                out[:, at] -= matmul(out[:, (k - 1) * width:k * width], parent_ref[k - 1])

    group_n = local(group_head, (rows_n * share, steps * width), [SMEM, VMEM, VMEM], group_depth, group_panel, parent_panel, vmem=12)

    def split(core_ref, z_ref, x_ref, keep, give):
        for unit in range(units):
            ref, at = (z_ref, unit) if unit < z_units else (x_ref, unit - z_units)
            keep[unit // y_n, unit % y_n] = ref[at, core_ref[0]]
            give[unit // y_n, unit % y_n] = ref[at, 1 - core_ref[0]]

    keep, give = local(split, [(steps, y_n, part, group)] * 2, [SMEM, VMEM, VMEM], core.reshape(1).astype(jnp.int32),
                       z_sum.reshape(z_units, 2, part, group), x_sum.reshape(units - z_units, 2, part, group), vmem=6)
    got = shift(give, "core", 1)

    def by_y(y_ref, keep_ref, got_ref, *outs):
        for d in range(y_n):
            i = lax.rem(y_ref[0] + d, y_n)
            for k in range(steps):
                outs[d][k] = keep_ref[k, i] + got_ref[k, i]

    summands = list(local(by_y, [(steps, part, group)] * y_n, [SMEM, VMEM, VMEM], y_i.reshape(1).astype(jnp.int32),
                          keep, got, vmem=6))
    for d in range(1, y_n):
        summands[d] = shift(summands[d], "y", d)

    per = rows_n // x_n

    def over_x(x_ref, *refs):
        parts, outs, held = refs[:y_n], refs[y_n:-1], refs[-1]
        total = sum((p[...] for p in parts[1:]), parts[0][...]).reshape(steps * part, group)
        held[...] = total.T.reshape(rows_n, share, steps * part)
        for d in range(x_n):
            for i in range(per):
                outs[d][i] = held[i * x_n + lax.rem(x_ref[0] + d, x_n)]

    def over_z(x_ref, *refs):
        for d in range(x_n):
            for i in range(per):
                refs[-1][lax.rem(x_ref[0] + x_n - d, x_n) * per + i] = refs[d][i]

    x_at = x_i.reshape(1).astype(jnp.int32)
    y_rows = list(local(over_x, [(per, share, steps * part)] * x_n, [SMEM] + [VMEM] * y_n, x_at, *summands,
                        after=(group_n,), scratch=[(rows_n, share, steps * part)]))
    for d in range(1, x_n):
        y_rows[d] = shift(y_rows[d], "x", d)
    y_rows = local(over_z, (z_n, share, steps * part), [SMEM] + [VMEM] * x_n, x_at, *y_rows)
    y_rows = lax.all_to_all(y_rows, "z", 0, 0, tiled=True)

    count = steps + links_n
    t_rows, t_cols = part // z_n, width // x_n

    def gram(y_ref, n_ref, tiles, turned):
        turned[...] = y_ref[...].reshape(rows_n * share, steps * part).T

        def put(which, value):
            for i in range(z_n):
                for j in range(x_n):
                    tiles[i * x_n + j, which] = value[i * t_rows:(i + 1) * t_rows, j * t_cols:(j + 1) * t_cols]

        for k in range(steps):
            low = max(k - 1, 0)
            value = matmul(turned[low * part:(k + 1) * part, :], n_ref[:, k * width:(k + 1) * width])
            put(k, value[(k - low) * part:])
            if k:
                put(steps + k - 1, value[:part])

    tiles = local(gram, (cols_n, count, t_rows, t_cols), [VMEM] * 2, y_rows, group_n, vmem=8,
                  scratch=[(steps * part, rows_n * share)])
    summed = lax.all_to_all(tiles, COL, 0, 0, tiled=True)

    home = y_rows.reshape(y_n, 2, share, steps * part)
    home = jnp.stack([pick(home, core, 1), shift(pick(home, 1 - core, 1), "core", 1)], axis=1)
    home = [pick(home, (y_i + d) % y_n, 0) for d in range(y_n)]
    home = [home[0]] + [shift(home[d], "y", d) for d in range(1, y_n)]

    def finish_cols(place_ref, block_ref, depth_ref, *refs):
        dst, held = refs[y_n:]
        for d in range(y_n):
            y_from = lax.rem(place_ref[0] + y_n - d, y_n)
            held[y_from * 2 + place_ref[1]] = refs[d][0]
            held[y_from * 2 + 1 - place_ref[1]] = refs[d][1]
        for i in range(rows_n):
            for k in range(steps):
                sign = jnp.where(depth_ref[block_ref[0]] > k, -1.0, 0.0).astype(F32)
                dst[k, :, i * part:(i + 1) * part] = sign * held[i, :, k * part:(k + 1) * part]

    cols = local(finish_cols, (steps, share, width), [SMEM] * 3 + [VMEM] * y_n,
                 jnp.stack([y_i, core]).astype(jnp.int32), own_block, block_depth, *home, scratch=[(rows_n, share, steps * part)])

    def unit_rows(first_ref):
        at = lax.broadcasted_iota(jnp.int32, (part, width), 0) + first_ref[0]
        return (lax.broadcasted_iota(jnp.int32, (part, width), 1) == at).astype(F32)

    def down_first(first_ref, inverse_ref, parent_ref, left, rows):
        unit = unit_rows(first_ref)
        left[...] = matmul(unit, inverse_ref[...], ((1,), (1,)))
        rows[:part] = matmul(unit, parent_ref[...], ((1,), (1,)))
        rows[part:] = unit

    def down(first_ref, inverse_ref, parent_ref, above, left, rows):
        left[...] = matmul(above[...], inverse_ref[...], ((1,), (1,)))
        rows[:-part] = matmul(above[...], parent_ref[...], ((1,), (1,)))
        rows[-part:] = unit_rows(first_ref)

    def bottom(inverse_ref, parent_ref, above, own, carried):
        value = matmul(matmul(above[...], inverse_ref[...], ((1,), (1,))), inverse_ref[...])
        own[...] = value[-part:]
        carried[...] = matmul(value, parent_ref[...])

    def up(inverse_ref, parent_ref, left, below, own, carried):
        value = matmul(left[...], inverse_ref[...]) + below[:-part]
        own[...] = value[-part:]
        carried[...] = matmul(value, parent_ref[...])

    def up_last(inverse_ref, left, below, own):
        own[...] = matmul(left[...], inverse_ref[...]) + below[:-part]

    parent_at = [block(k, parent_panel.shape) for k in range(links_n)]
    inverse_at = [block(k, diag_inverse.shape) for k in range(steps)]
    first = (r * part).reshape(1).astype(jnp.int32)
    lefts, rows = [None] * steps, None
    for k in range(steps - 1, 0, -1):
        above = [] if rows is None else [rows]
        tall = (steps - k) * part
        lefts[k], rows = local(down if above else down_first, [(tall, width), (tall + part, width)],
                               [SMEM, inverse_at[k], parent_at[k - 1]] + [VMEM] * len(above),
                               first, diag_inverse, parent_panel, *above, after=() if above else (tiles,))
    diag_own, link_own = [None] * steps, [None] * links_n
    diag_own[0], carried = local(bottom, [(part, width), (steps * part, width)], [inverse_at[0], parent_at[0], VMEM],
                                 diag_inverse, parent_panel, rows)
    for k in range(1, steps):
        link_own[k - 1] = carried
        if k < steps - 1:
            diag_own[k], carried = local(up, [(part, width), ((steps - k) * part, width)],
                                         [inverse_at[k], parent_at[k], VMEM, VMEM],
                                         diag_inverse, parent_panel, lefts[k], carried)
        else:
            diag_own[k] = local(up_last, (part, width), [inverse_at[k], VMEM, VMEM], diag_inverse, lefts[k], carried)

    def total_kernel(src, dst):
        total = src[0]
        for i in range(1, cols_n):
            total = total + src[i]
        for i in range(cols_n):
            dst[i] = total

    every = lax.all_to_all(local(total_kernel, tiles.shape, [VMEM], summed, after=(diag_own[-1],)), COL, 0, 0, tiled=True)

    def finish(src, *refs):
        diag_refs, link_refs, (links, diags) = refs[:steps], refs[steps:count], refs[count:]
        for i in range(z_n):
            for j in range(x_n):
                place = (slice(i * t_rows, (i + 1) * t_rows), slice(j * t_cols, (j + 1) * t_cols))
                for k in range(steps):
                    diags[(k,) + place] = diag_refs[k][place] + src[i * x_n + j, k]
                for k in range(links_n):
                    last = link_refs[k].shape[0] - part
                    links[(k,) + place] = src[i * x_n + j, steps + k] - link_refs[k][last + i * t_rows:last + (i + 1) * t_rows, place[1]]

    links, diags = local(finish, [(links_n, part, width), (steps, part, width)], [VMEM] * (count + 1),
                         every, *diag_own, *link_own)
    return cols, links, diags


def solution(mesh):
    axes = Mesh(mesh.devices.reshape(4, 2, 8, 4), ("y", "core", "z", "x"))
    return jax.shard_map(
        shards,
        mesh=axes,
        in_specs=(P(ROW, COL), P(None, ALL, None), P(), P(), P()),
        out_specs=(P(None, ALL, None), P(None, ROW, None), P(None, ROW, None)),
        check_vma=False,
    )
```
